128 devices in a mesh: dom: 32 (over y, x, core), lvl: 4 (over z).
Axes of the slice: x: 4, y: 4, z: 4, core: 2. Of those that a mesh axis runs over, the one named last changes fastest.
Arguments:
- positions: float32 [3, 2097152], P(None, ('dom', 'lvl')), may hold values from -0.8 to 0.8
- charges: float32 [2097152], P(('dom', 'lvl')), may hold values from -3 to 3
- block_leaf: int32 [16384], P(('dom', 'lvl')), may hold values from 0 to 8191, as said below
- leaf_slot: int32 [8192], replicated, may hold values from 0 to 8191, as said below
- m2m_ops: float32 [8, 81, 81], replicated, may hold values from -0.25 to 0.25
- l2l_ops: float32 [8, 81, 81], replicated, may hold values from -0.625 to 0.625
- m2l_ops: float32 [316, 81, 81], replicated, may hold values from -0.0024414062 to 0.0024414062
- item_target: int32 [32, 4, 4096], P('dom', 'lvl'), may hold values from 0 to 255
- item_source: int32 [32, 4, 4096], P('dom', 'lvl'), may hold values from 0 to 8191, as said below
- item_offset: int32 [32, 4, 4096], P('dom', 'lvl'), may hold values from 0 to 315
- coarse_target: int32 [32, 4, 2048], P('dom', 'lvl'), may hold values from 0 to 63
- coarse_source: int32 [32, 4, 2048], P('dom', 'lvl'), may hold values from 0 to 1023
- coarse_offset: int32 [32, 4, 2048], P('dom', 'lvl'), may hold values from 0 to 315
Outputs:
- forces: float32 [3, 2097152], P(None, ('dom', 'lvl'))
- potential: float32 [2097152], P(('dom', 'lvl'))
The draws below stay inside these ranges and needn't reach their ends.
Inputs may be any that keep to these rules, and one draw needn't show every extreme that they name: `block_leaf`: block b lies on device b // 128 of dom+lvl and names a leaf of that device's lvl group g, one of the leaves g * 2048 to (g + 1) * 2048 - 1. Of one device's blocks at most 8 name leaves owned by any one dom index, and in every lvl group one dom index receives exactly 8 blocks from every device of the group. `leaf_slot`: A permutation of the slots. The leaves of lvl group g take the slots of devices with lvl index g; device (d, g) owns the slots (d * 4 + g) * 64 to (d * 4 + g + 1) * 64 - 1. `item_source`: the items of one device name, among the slots owned by any one device, exactly 32 different slots.
All inputs are finite; a program needn't handle non-finite values.
Results may differ from the reference program's by a relative error of at most 0.0001.
Values sent between devices are 32-bit elements; how exact they have to be, the bound alone decides.
A program may use at most 192 MiB of HBM per device.

```python
import math
import jax
import jax.numpy as jnp
import numpy as np
from jax import lax

COEF = 81
NOFF = 316
BLK_DEV = 128
LEAF_DEV = 64
ITEM_DEV = 4096
PITEM_DEV = 2048
BLOCKS = 16384
ATOMS = 2097152
LEAVES_G = 2048
LEAVES = 8192
PARENTS = 1024
CAP = 8
SRC_CAP = 32
N_DOM = 32
N_LVL = 4
DEVICES = 128


def shared_layout(key):
    keys = jax.random.split(key, 5)
    perms = jax.vmap(lambda sub_key: jax.random.permutation(sub_key, LEAVES_G))(jax.random.split(keys[0], N_LVL)).astype(jnp.int32)
    groups = jnp.arange(N_LVL, dtype=jnp.int32)[:, None]
    table = (perms // LEAF_DEV * N_LVL + groups) * LEAF_DEV + perms % LEAF_DEV
    inverse = jnp.argsort(perms, axis=1).astype(jnp.int32)
    crowded = jax.random.randint(keys[1], (N_LVL,), 0, N_DOM).astype(jnp.int32)
    group_of = jnp.arange(DEVICES, dtype=jnp.int32) % N_LVL
    others = jax.vmap(lambda sub_key: jax.random.permutation(sub_key, (N_DOM - 1) * CAP))(jax.random.split(keys[2], DEVICES)).astype(jnp.int32)
    picked = others[:, :BLK_DEV - CAP] // CAP
    heavy = crowded[group_of][:, None]
    picked = picked + (picked >= heavy).astype(jnp.int32)
    owners = jnp.concatenate([jnp.broadcast_to(heavy, (DEVICES, CAP)), picked], axis=1)
    shuffle = jax.vmap(lambda sub_key: jax.random.permutation(sub_key, BLK_DEV))(jax.random.split(keys[3], DEVICES)).astype(jnp.int32)
    owners = jnp.take_along_axis(owners, shuffle, axis=1)
    within = jax.random.randint(keys[4], (DEVICES, BLK_DEV), 0, LEAF_DEV).astype(jnp.int32)
    leaves = jnp.take_along_axis(inverse[group_of], owners * LEAF_DEV + within, axis=1)
    block_leaf = leaves + group_of[:, None] * LEAVES_G
    return (table.reshape(-1).astype(jnp.int32), block_leaf.reshape(-1).astype(jnp.int32))


def draw_leaf_slot(key, part):
    layout = shared_layout(key)
    return layout[0]


def draw_block_leaf(key, part):
    layout = shared_layout(key)
    return layout[1]


def one_device_sources(key):
    keys = jax.random.split(key, 3)
    picks = jax.vmap(lambda sub_key: jax.random.permutation(sub_key, LEAF_DEV))(jax.random.split(keys[0], DEVICES)).astype(jnp.int32)
    owners = jnp.arange(DEVICES, dtype=jnp.int32)[:, None]
    pool = (owners * LEAF_DEV + picks[:, :SRC_CAP]).reshape(-1)
    extra = pool[jax.random.randint(keys[1], (ITEM_DEV - DEVICES * SRC_CAP,), 0, DEVICES * SRC_CAP)]
    listed = jnp.concatenate([pool, extra])
    return listed[jax.random.permutation(keys[2], ITEM_DEV)].astype(jnp.int32)


def draw_item_source(key, part):
    key = jax.random.fold_in(key, 13)
    drawn = jax.vmap(one_device_sources)(jax.random.split(key, DEVICES))
    return drawn.reshape(N_DOM, N_LVL, ITEM_DEV).astype(jnp.int32)


def with_ends(values, own_key, least, largest):
    longest = values.shape.index(max(values.shape))
    spots = []
    for shift in (0, 1):
        where = [jax.random.randint(jax.random.fold_in(own_key, axis), (), 0, length) for axis, length in enumerate(values.shape)]
        where[longest] = (where[longest] + shift) % values.shape[longest]
        spots.append(tuple(where))
    return values.at[spots[0]].set(least).at[spots[1]].set(largest)


def shard_levels(own_key, extent, cuts, low, top_value):
    factor_of = 1.0
    for dim, shards_of in cuts:
        heights = jax.random.uniform(jax.random.fold_in(jax.random.fold_in(own_key, 6), dim), (shards_of,), jnp.float32, low / len(cuts), top_value / len(cuts))
        factor_of = factor_of * jnp.repeat(jnp.exp(heights), extent[dim] // shards_of).reshape((-1,) + (1,) * (len(extent) - 1 - dim))
    return factor_of


def rank_table(number_of, lean):
    weights = [(1 << 20) // math.isqrt(standing ** lean) + 1 for standing in range(1, number_of + 1)]
    deviation = 1 + sum(weights) // (1 << 30)
    return np.cumsum(np.array([max(1, weight // deviation) for weight in weights]))


def ranked(rng, dims, amount, lean):
    listing = rank_table(amount, lean)
    ticket = jax.random.randint(jax.random.fold_in(rng, 1), dims, 0, int(listing[amount - 1]))
    standing = jnp.searchsorted(jnp.asarray(listing, jnp.int32), ticket, side="right")
    return jax.random.permutation(jax.random.fold_in(rng, 2), amount)[standing].astype(jnp.int32)


def gaussian(own_key, dims, scale, reach, pieces=(), kind=jnp.bfloat16):
    result = jax.random.normal(own_key, dims, jnp.float32) * scale
    if len(pieces) > 0:
        result = shard_levels(own_key, dims, pieces, -0.22, 0.18) * result
    return jnp.clip(result, min=-reach, max=reach).astype(kind)


def setup_inputs(seed: int = 0) -> dict:
    seeds = jax.random.split(jax.random.key(seed), 14)
    positions = jnp.clip(jax.random.uniform(seeds[0], (3, ATOMS), jnp.float32, -0.8, 0.8) * shard_levels(seeds[0], (3, ATOMS), ((1, 128),), -0.4, 0.0), -0.8, 0.8)
    charges = gaussian(seeds[1], (ATOMS,), 0.5, 3.0, ((0, 128),), jnp.float32)
    block_leaf = draw_block_leaf(jax.random.fold_in(seeds[13], 71), 0)
    leaf_slot = draw_leaf_slot(jax.random.fold_in(seeds[13], 71), 0)
    m2m_ops = gaussian(seeds[4], (8, COEF, COEF), (81 * 8) ** -0.5, 0.25, (), jnp.float32)
    l2l_ops = gaussian(seeds[5], (8, COEF, COEF), 81 ** -0.5, 0.625, (), jnp.float32)
    m2l_ops = gaussian(seeds[6], (NOFF, COEF, COEF), (81 * 65536) ** -0.5, 0.0024414062, (), jnp.float32)
    item_target = with_ends(ranked(seeds[7], (N_DOM, N_LVL, ITEM_DEV), N_LVL * LEAF_DEV, 2), jax.random.fold_in(seeds[7], 3), 0, (N_LVL * LEAF_DEV) - 1).astype(jnp.int32)
    item_source = draw_item_source(jax.random.fold_in(seeds[13], 71), 0)
    item_offset = with_ends(jax.random.randint(seeds[9], (N_DOM, N_LVL, ITEM_DEV), 0, NOFF), jax.random.fold_in(seeds[9], 1), 0, NOFF - 1).astype(jnp.int32)
    coarse_target = with_ends(jax.random.randint(seeds[10], (N_DOM, N_LVL, PITEM_DEV), 0, LEAF_DEV), jax.random.fold_in(seeds[10], 1), 0, LEAF_DEV - 1).astype(jnp.int32)
    coarse_source = with_ends(jax.random.randint(seeds[11], (N_DOM, N_LVL, PITEM_DEV), 0, PARENTS), jax.random.fold_in(seeds[11], 1), 0, PARENTS - 1).astype(jnp.int32)
    coarse_offset = with_ends(jax.random.randint(seeds[12], (N_DOM, N_LVL, PITEM_DEV), 0, NOFF), jax.random.fold_in(seeds[12], 1), 0, NOFF - 1).astype(jnp.int32)
    return {"positions": positions, "charges": charges, "block_leaf": block_leaf, "leaf_slot": leaf_slot, "m2m_ops": m2m_ops, "l2l_ops": l2l_ops, "m2l_ops": m2l_ops, "item_target": item_target, "item_source": item_source, "item_offset": item_offset, "coarse_target": coarse_target, "coarse_source": coarse_source, "coarse_offset": coarse_offset}


HIGH = lax.Precision.HIGHEST
softening = 0.04

def solid_basis(coords):
    along_x, along_y, along_z = (coords[0], coords[1], coords[2])
    squared = along_x * along_x + along_y * along_y + along_z * along_z
    nought = jnp.zeros_like(along_x)
    rows = [None] * 81
    diag_re = jnp.ones_like(along_x)
    diag_im = nought
    for azimuth in range(9):
        if azimuth > 0:
            factor = -1.0 / (2.0 * azimuth)
            diag_re, diag_im = (factor * (along_x * diag_re - along_y * diag_im), factor * (along_x * diag_im + along_y * diag_re))
        lower_re, lower_im = (nought, nought)
        upper_re, upper_im = (diag_re, diag_im)
        for degree in range(azimuth, 9):
            if degree > azimuth:
                factor = 1.0 / ((degree + azimuth) * (degree - azimuth))
                fresh_re = factor * ((2 * degree - 1) * along_z * upper_re - squared * lower_re)
                fresh_im = factor * ((2 * degree - 1) * along_z * upper_im - squared * lower_im)
                lower_re, lower_im, upper_re, upper_im = (upper_re, upper_im, fresh_re, fresh_im)
            weight = math.sqrt(math.factorial(degree + azimuth) * math.factorial(degree - azimuth))
            start = degree * degree
            if azimuth == 0:
                rows[start] = weight * upper_re
            else:
                rows[start + 2 * azimuth - 1] = weight * upper_re
                rows[start + 2 * azimuth] = weight * upper_im
    return jnp.stack(rows, axis=0)

def near_field(coords, charge):
    delta = coords[:, :, :, None] - coords[:, :, None, :]
    distance = lax.optimization_barrier(jnp.sum(delta * delta, axis=0)) + softening
    inverse = jnp.where(jnp.eye(128, dtype=bool)[None], 0.0, lax.rsqrt(distance))
    potential = lax.optimization_barrier(jnp.sum(inverse * charge[:, None, :], axis=2))
    strength = inverse * inverse * inverse * charge[:, None, :]
    force = charge[None] * lax.optimization_barrier(jnp.sum(delta * strength[None], axis=3))
    return (force, potential)

def far_field(values, pullback, charge, local_rows):
    cotangent = jnp.broadcast_to(jnp.transpose(local_rows)[:, :, None], values.shape)
    potential = lax.optimization_barrier(jnp.sum(values * cotangent, axis=0))
    slope, = pullback(cotangent)
    return (-charge[None] * slope, potential)

def by_octant(rows, tables, octant):
    total = jnp.zeros_like(rows)
    for index in range(8):
        moved = jnp.dot(rows, jnp.transpose(tables[index]), precision=HIGH, preferred_element_type=jnp.float32)
        total = total + jnp.where((octant == index)[:, None], moved, 0.0)
    return total

def translate_all(sources, source_ids, offsets, targets, rows, tables):
    count = source_ids.shape[0]
    width = 4096

    def step(total, batch):
        src, off, tgt = batch
        product = jnp.einsum('ikl,il->ik', tables[off], sources[src], precision=HIGH)
        return (total.at[tgt].add(product), None)
    shaped = (source_ids.reshape(count // width, width), offsets.reshape(count // width, width), targets.reshape(count // width, width))
    total, _ = lax.scan(step, jnp.zeros((rows, sources.shape[1]), jnp.float32), shaped)
    return total

def reference(positions, charges, block_leaf, leaf_slot, m2m_ops, l2l_ops, m2l_ops, item_target, item_source, item_offset, coarse_target, coarse_source, coarse_offset):
    coords = positions.reshape(3, DEVICES, BLK_DEV, 128).transpose(1, 0, 2, 3)
    charge = charges.reshape(DEVICES, BLK_DEV, 128)

    def moments_of(pair):
        block_coords, block_charge = pair
        values = solid_basis(block_coords)
        return jnp.einsum('kbn,bn->bk', values, block_charge, precision=HIGH)
    block_moments = lax.map(moments_of, (coords, charge)).reshape(BLOCKS, COEF)
    slot_of_block = leaf_slot[block_leaf]
    leaf_moments = jax.ops.segment_sum(block_moments, slot_of_block, num_segments=LEAVES)
    leaf_of_slot = jnp.zeros((LEAVES,), jnp.int32).at[leaf_slot].set(jnp.arange(LEAVES, dtype=jnp.int32))
    octant = leaf_of_slot % 8
    parent = leaf_of_slot // 8
    parent_moments = jax.ops.segment_sum(by_octant(leaf_moments, m2m_ops, octant), parent, num_segments=PARENTS)
    dom_index = jnp.arange(N_DOM, dtype=jnp.int32)[:, None, None]
    lvl_index = jnp.arange(N_LVL, dtype=jnp.int32)[None, :, None]
    leaf_targets = (dom_index * N_LVL + item_target // LEAF_DEV) * LEAF_DEV + item_target % LEAF_DEV
    coarse_targets = (dom_index * N_LVL + lvl_index) * LEAF_DEV + coarse_target
    leaf_locals = translate_all(leaf_moments, item_source.reshape(-1), item_offset.reshape(-1), leaf_targets.reshape(-1), LEAVES, m2l_ops)
    parent_locals = translate_all(parent_moments, coarse_source.reshape(-1), coarse_offset.reshape(-1), coarse_targets.reshape(-1), LEAVES, m2l_ops)
    slot_locals = leaf_locals + by_octant(parent_locals, l2l_ops, octant)
    block_locals = slot_locals[slot_of_block].reshape(DEVICES, BLK_DEV, COEF)

    def finish(triple):
        block_coords, block_charge, local_rows = triple
        values, pullback = jax.vjp(solid_basis, block_coords)
        far_force, far_phi = far_field(values, pullback, block_charge, local_rows)
        near_force, near_phi = near_field(block_coords, block_charge)
        return (near_force + far_force, near_phi + far_phi)
    forces, potential = lax.map(finish, (coords, charge, block_locals))
    forces = forces.transpose(1, 0, 2, 3).reshape(3, ATOMS)
    return (forces, potential.reshape(ATOMS))
```

```python
import functools
import math

import jax
import jax.numpy as jnp
import numpy as np
from jax import lax
from jax.experimental import pallas as pl
from jax.experimental.pallas import tpu as pltpu
from jax.sharding import PartitionSpec as P

COEF = 81
TOP = 8
LANES = 128
LEAF_DEV = 64
CAP = 8
GROUP = 4
SOFTENING = 0.04
HIGH = lax.Precision.HIGHEST
VMEM = pltpu.VMEM
MIB = 1 << 20


def dot(a, b, contract=((1,), (0,))):
    return lax.dot_general(
        a, b, (contract, ((), ())), precision=HIGH, preferred_element_type=jnp.float32
    )


def row_index(degree, azimuth, imaginary):
    start = degree * degree
    return start if azimuth == 0 else start + 2 * azimuth - 1 + int(imaginary)


def row_weight(degree, azimuth):
    return math.sqrt(math.factorial(degree + azimuth) * math.factorial(degree - azimuth))


def harmonics(x, y, z, emit):
    squared = x * x + y * y + z * z
    diag_re, diag_im = None, None
    for azimuth in range(TOP + 1):
        if azimuth == 1:
            diag_re, diag_im = -0.5 * x, -0.5 * y
        elif azimuth > 1:
            factor = -1.0 / (2.0 * azimuth)
            fx, fy = factor * x, factor * y
            diag_re, diag_im = fx * diag_re - fy * diag_im, fx * diag_im + fy * diag_re
        if azimuth == 0:
            parts = [jnp.ones_like(x)]
        else:
            parts = [diag_re, diag_im]
        for which, value in enumerate(parts):
            lower, upper = None, value
            for degree in range(azimuth, TOP + 1):
                if degree > azimuth:
                    factor = 1.0 / ((degree + azimuth) * (degree - azimuth))
                    if degree == 1 and azimuth == 0:
                        fresh = z
                    elif lower is None:
                        fresh = (factor * (2 * degree - 1)) * z * upper
                    else:
                        fresh = (factor * (2 * degree - 1)) * z * upper - (factor * squared) * lower
                    lower, upper = upper, fresh
                emit(row_index(degree, azimuth, which == 1), degree, upper)


def weight_column():
    out = np.zeros((LANES, 1), np.float32)
    for degree in range(TOP + 1):
        for azimuth in range(degree + 1):
            for imaginary in range(2 if azimuth else 1):
                out[row_index(degree, azimuth, imaginary), 0] = row_weight(degree, azimuth)
    return out


G_ROWS = 96 + 3 * 64


def gradient_matrix():
    out = np.zeros((G_ROWS, LANES), np.float64)

    def add(axis, row, degree, azimuth, value_re, value_im):
        if degree < 0 or azimuth > degree:
            return
        out[96 + 64 * axis + row_index(degree, azimuth, 0), row] += value_re
        if azimuth:
            out[96 + 64 * axis + row_index(degree, azimuth, 1), row] += value_im

    for degree in range(TOP + 1):
        for azimuth in range(degree + 1):
            for imaginary in range(2 if azimuth else 1):
                row = row_index(degree, azimuth, imaginary)
                w = row_weight(degree, azimuth)
                out[row, row] = w
                below = degree - 1
                if imaginary:
                    add(2, row, below, azimuth, 0.0, w)
                    add(0, row, below, azimuth + 1, 0.0, 0.5 * w)
                    add(0, row, below, azimuth - 1, 0.0, -0.5 * w)
                    add(1, row, below, azimuth + 1, -0.5 * w, 0.0)
                    add(1, row, below, azimuth - 1, -0.5 * w, 0.0)
                elif azimuth:
                    add(2, row, below, azimuth, w, 0.0)
                    add(0, row, below, azimuth + 1, 0.5 * w, 0.0)
                    add(0, row, below, azimuth - 1, -0.5 * w, 0.0)
                    add(1, row, below, azimuth + 1, 0.0, 0.5 * w)
                    add(1, row, below, azimuth - 1, 0.0, 0.5 * w)
                else:
                    add(2, row, below, 0, w, 0.0)
                    add(0, row, below, 1, w, 0.0)
                    add(1, row, below, 1, 0.0, w)
    return out.astype(np.float32)


def iota(shape, dim):
    return lax.broadcasted_iota(jnp.int32, shape, dim)


def moments_kernel(pos_ref, q_ref, leaf_ref, table_ref, weight_ref, packed_ref, place_ref, turned, acc, rows):
    blocks = leaf_ref.shape[1]
    leaf = leaf_ref[...]
    high = (iota((64, blocks), 0) == (leaf >> 7)).astype(jnp.float32)
    lines = dot(table_ref[...].astype(jnp.float32), high, ((0,), (0,)))
    slot = jnp.sum(
        jnp.where(iota((LANES, blocks), 0) == (leaf & 127), lines, 0.0), axis=0, keepdims=True
    ).astype(jnp.int32)
    owner = slot >> 8
    hits = iota((32, blocks), 0) == owner
    earlier = (iota((blocks, blocks), 0) < iota((blocks, blocks), 1)).astype(jnp.float32)
    before = dot(hits.astype(jnp.float32), earlier)
    rank = jnp.sum(jnp.where(hits, before, 0.0), axis=0, keepdims=True).astype(jnp.int32)
    place = owner * CAP + rank
    place_ref[...] = place

    for d in range(3):
        turned[d] = pos_ref[d].T
    turned[3] = q_ref[...].T
    acc[...] = jnp.zeros_like(acc)

    def chunk(i, carry):
        at = pl.ds(pl.multiple_of(i * 32, 32), 32)
        x, y, z, q = (turned[d, at, :] for d in range(4))

        def emit(row, degree, value):
            part = q * value
            acc[row] += (part[0:8] + part[8:16]) + (part[16:24] + part[24:32])

        harmonics(x, y, z, emit)
        return carry

    lax.fori_loop(0, 4, chunk, 0)
    rows[...] = jnp.zeros_like(rows)
    for k in range(COEF):
        rows[k : k + 1, :] = jnp.sum(acc[k], axis=0, keepdims=True)
    rows[...] = rows[...] * weight_ref[...]
    rows[127:128, :] = ((slot & 63) + 1).astype(jnp.float32)
    moments = rows[...].T
    spread = (iota((32 * CAP, blocks), 0) == place).astype(jnp.float32)
    packed_ref[...] = dot(spread, moments)


def block_moments(coords, charge, leaf, table):
    blocks = coords.shape[1]
    whole = pl.BlockSpec(memory_space=VMEM)
    return pl.pallas_call(
        moments_kernel,
        out_shape=(
            jax.ShapeDtypeStruct((32 * CAP, LANES), jnp.float32),
            jax.ShapeDtypeStruct((1, blocks), jnp.int32),
        ),
        in_specs=[whole] * 5,
        out_specs=(whole, whole),
        scratch_shapes=[
            VMEM((4, LANES, blocks), jnp.float32),
            VMEM((COEF, 8, blocks), jnp.float32),
            VMEM((LANES, blocks), jnp.float32),
        ],
        compiler_params=pltpu.CompilerParams(vmem_limit_bytes=16 * MIB),
        name="block_moments",
    )(coords, charge, leaf, table, jnp.asarray(weight_column()))


def leaves_kernel(arrived_ref, table_ref, ops_ref, leaf_ref, parent_ref, ids_ref):
    group = lax.axis_index("lvl")
    first = (lax.axis_index("dom") * GROUP + group) * LEAF_DEV
    arrived = arrived_ref[...]
    tags = arrived[:, 127:128].astype(jnp.int32)
    member = (iota((arrived.shape[0], LEAF_DEV), 1) + 1 == tags).astype(jnp.float32)
    leaf = dot(member, arrived, ((0,), (0,)))
    leaf = jnp.where(iota(leaf.shape, 1) < COEF, leaf, 0.0)
    leaf_ref[...] = leaf
    slots = first + iota((LEAF_DEV, LANES), 0)
    found = jnp.zeros((LEAF_DEV, LANES), jnp.int32)
    lane = iota((LEAF_DEV, LANES), 1)
    table = table_ref[pl.ds(pl.multiple_of(group * 16, 16), 16), :]
    for h in range(16):
        number = (group * 16 + h) * 128 + lane
        found = found + jnp.where(table[h : h + 1, :] == slots, number, 0)
    ids = jnp.sum(found.astype(jnp.float32), axis=1, keepdims=True).astype(jnp.int32)
    ids_ref[...] = jnp.broadcast_to(ids, (LEAF_DEV, LANES))
    octant = ids & 7
    children = jnp.zeros((LEAF_DEV, LANES), jnp.float32)
    for o in range(8):
        children = children + dot(jnp.where(octant == o, leaf, 0.0), ops_ref[o], ((1,), (1,)))
    within = (ids >> 3) - group * 256
    picks = (iota((LEAF_DEV, 256), 1) == within).astype(jnp.float32)
    parent_ref[...] = dot(picks, children, ((0,), (0,)))


def leaves(arrived, table, ops):
    whole = pl.BlockSpec(memory_space=VMEM)
    return pl.pallas_call(
        leaves_kernel,
        out_shape=(
            jax.ShapeDtypeStruct((LEAF_DEV, LANES), jnp.float32),
            jax.ShapeDtypeStruct((256, LANES), jnp.float32),
            jax.ShapeDtypeStruct((LEAF_DEV, LANES), jnp.int32),
        ),
        in_specs=[whole] * 3,
        out_specs=(whole,) * 3,
        compiler_params=pltpu.CompilerParams(vmem_limit_bytes=16 * MIB),
        name="leaf_moments",
    )(arrived, table, ops)


def bitonic(x):
    rows = x.shape[0]
    index = iota(x.shape, 0) * LANES + iota(x.shape, 1)
    size = rows * LANES
    span = 2
    while span <= size:
        step = span // 2
        while step >= 1:
            axis, shift, extent = (1, step, LANES) if step < LANES else (0, step // LANES, rows)
            second = (index & step) != 0
            other = jnp.where(
                second, pltpu.roll(x, shift, axis), pltpu.roll(x, extent - shift, axis)
            )
            ascending = (index & span) == 0
            take_small = ascending != second
            x = jnp.where(take_small, jnp.minimum(x, other), jnp.maximum(x, other))
            step //= 2
        span *= 2
    return x


def order_kernel(leaf_ref, coarse_ref, leaf_out, coarse_out):
    leaf_out[...] = bitonic(leaf_ref[...])
    coarse_out[...] = bitonic(coarse_ref[...])


def listed(target, source, offset, targets, none, room):
    key = (target << 23) | (source << 9) | offset
    numbers = jnp.arange(targets, dtype=jnp.int32)
    count = jnp.sum((target[:, None] == numbers[None, :]).astype(jnp.int32), axis=0)
    fours = (count + 3) >> 2
    missing = fours * 4 - count
    turn = jnp.arange(3, dtype=jnp.int32)[:, None]
    fill_target = jnp.where(turn < missing[None, :], numbers[None, :], targets - 1)
    fill = ((fill_target << 23) | (none << 9)).reshape(-1)
    rest = jnp.full((room - key.shape[0] - fill.shape[0],), ((targets - 1) << 23) | (none << 9), jnp.int32)
    keys = jnp.concatenate([key, fill, rest]).reshape(room // LANES, LANES)
    return keys, jnp.sum(fours).reshape(1)


def ordered(leaf_keys, coarse_keys):
    whole = pl.BlockSpec(memory_space=VMEM)
    return pl.pallas_call(
        order_kernel,
        out_shape=(
            jax.ShapeDtypeStruct(leaf_keys.shape, jnp.int32),
            jax.ShapeDtypeStruct(coarse_keys.shape, jnp.int32),
        ),
        in_specs=[whole] * 2,
        out_specs=(whole,) * 2,
        name="order",
    )(leaf_keys, coarse_keys)


def translate_kernel(targets, sources, keys, count, src_hbm, ops_hbm, out_ref, ops, src, acc, sems):
    load_ops = pltpu.make_async_copy(ops_hbm, ops, sems.at[0])
    load_src = pltpu.make_async_copy(src_hbm, src.at[pl.ds(0, sources)], sems.at[1])
    load_ops.start()
    load_src.start()
    src[pl.ds(sources, 8), :] = jnp.zeros((8, LANES), jnp.float32)

    def clear(t, carry):
        acc[t] = jnp.zeros(acc.shape[1:], jnp.float32)
        return carry

    lax.fori_loop(0, targets, clear, 0)
    load_ops.wait()
    load_src.wait()

    def term(at):
        key = keys[at]
        row = src[pl.ds((key >> 9) & 16383, 1), :][:, :COEF]
        return ops[key & 511] * row

    def step(i, carry):
        for u in range(2):
            at = i * 8 + u * 4
            target = keys[at] >> 23
            total = (term(at) + term(at + 1)) + (term(at + 2) + term(at + 3))
            acc[target] += total
        return carry

    lax.fori_loop(0, (count[0] + 1) // 2, step, 0)
    diagonal = iota((COEF, LANES), 0) == iota((COEF, LANES), 1)

    def finish(i, carry):
        for u in range(4):
            t = i * 4 + u
            sums = jnp.sum(acc[t], axis=1, keepdims=True)
            out_ref[pl.ds(t, 1), :] = jnp.sum(
                jnp.where(diagonal, sums, 0.0), axis=0, keepdims=True
            )
        return carry

    lax.fori_loop(0, targets // 4, finish, 0)


def translate(keys, count, table, ops, targets):
    sources = table.shape[0]
    smem = pl.BlockSpec(memory_space=pltpu.SMEM)
    far = pl.BlockSpec(memory_space=pl.ANY)
    return pl.pallas_call(
        functools.partial(translate_kernel, targets, sources),
        out_shape=jax.ShapeDtypeStruct((targets, LANES), jnp.float32),
        in_specs=[smem, smem, far, far],
        out_specs=pl.BlockSpec(memory_space=VMEM),
        scratch_shapes=[
            VMEM(ops.shape, jnp.float32),
            VMEM((sources + 8, LANES), jnp.float32),
            VMEM((targets, COEF, COEF), jnp.float32),
            pltpu.SemaphoreType.DMA((2,)),
        ],
        compiler_params=pltpu.CompilerParams(vmem_limit_bytes=48 * MIB),
        name="translate",
    )(keys.reshape(-1), count, table, ops)


def near_kernel(pos_ref, q_ref, out_ref):
    def group(g, carry):
        at = pl.ds(pl.multiple_of(g * 8, 8), 8)
        rows = [pos_ref[d, at, :] for d in range(3)] + [q_ref[at, :]]
        columns = [r.T for r in rows]
        for b in range(8):
            xj, yj, zj, qj = (r[b : b + 1, :] for r in rows)
            xi, yi, zi, qi = (c[:, b : b + 1] for c in columns)
            sums = [jnp.zeros((8, LANES), jnp.float32) for _ in range(4)]
            for c in range(4):
                part = slice(c * 32, c * 32 + 32)
                dx = xj - xi[part]
                dy = yj - yi[part]
                dz = zj - zi[part]
                inverse = lax.rsqrt(dx * dx + dy * dy + dz * dz + SOFTENING)
                same = iota((32, LANES), 0) + c * 32 == iota((32, LANES), 1)
                weighted = jnp.where(same, 0.0, inverse * qi[part])
                strength = weighted * (inverse * inverse)
                for n, term in enumerate((strength * dx, strength * dy, strength * dz, weighted)):
                    sums[n] = sums[n] + ((term[0:8] + term[8:16]) + (term[16:24] + term[24:32]))
            for n in range(4):
                line = jnp.sum(sums[n], axis=0, keepdims=True)
                if n < 3:
                    line = line * qj
                out_ref[n, pl.ds(g * 8 + b, 1), :] = line
        return carry

    lax.fori_loop(0, q_ref.shape[0] // 8, group, 0)


def near_field(coords, charge):
    whole = pl.BlockSpec(memory_space=VMEM)
    return pl.pallas_call(
        near_kernel,
        out_shape=jax.ShapeDtypeStruct((4,) + charge.shape, jnp.float32),
        in_specs=[whole] * 2,
        out_specs=whole,
        compiler_params=pltpu.CompilerParams(vmem_limit_bytes=16 * MIB),
        cost_estimate=pl.CostEstimate(flops=60_000_000, bytes_accessed=1 << 19, transcendentals=2_000_000),
        name="near_field",
    )(coords, charge)


def locals_kernel(leaf_ref, parent_ref, ids_ref, arrived_ref, ops_ref, out_ref):
    octant = ids_ref[...] & 7
    parent = parent_ref[...]
    total = leaf_ref[...]
    for o in range(8):
        total = total + dot(jnp.where(octant == o, parent, 0.0), ops_ref[o], ((1,), (1,)))
    tags = arrived_ref[:, 127:128].astype(jnp.int32)
    member = (iota((arrived_ref.shape[0], LEAF_DEV), 1) + 1 == tags).astype(jnp.float32)
    out_ref[...] = dot(member, total)


def slot_locals(leaf_locals, parent_locals, ids, arrived, ops):
    whole = pl.BlockSpec(memory_space=VMEM)
    return pl.pallas_call(
        locals_kernel,
        out_shape=jax.ShapeDtypeStruct(arrived.shape, jnp.float32),
        in_specs=[whole] * 5,
        out_specs=whole,
        compiler_params=pltpu.CompilerParams(vmem_limit_bytes=16 * MIB),
        name="slot_locals",
    )(leaf_locals, parent_locals, ids, arrived, ops)


def far_kernel(pos_ref, q_ref, place_ref, returned_ref, near_ref, matrix_ref, force_ref, phi_ref, turned, lines):
    blocks = q_ref.shape[0]
    spread = (iota((32 * CAP, blocks), 0) == place_ref[...]).astype(jnp.float32)
    columns = dot(returned_ref[...], spread, ((0,), (0,)))
    lines[...] = dot(matrix_ref[...], columns)
    for d in range(3):
        turned[d] = pos_ref[d].T

    def chunk(i, carry):
        at = pl.ds(pl.multiple_of(i * 32, 32), 32)
        x, y, z = (turned[d, at, :] for d in range(3))
        sums = [None] * 4

        def emit(row, degree, value):
            starts = [(3, 0)] + ([(d, 96 + 64 * d) for d in range(3)] if degree < TOP else [])
            for n, start in starts:
                term = lines[start + row : start + row + 1, :] * value
                sums[n] = term if sums[n] is None else sums[n] + term

        harmonics(x, y, z, emit)
        for n in range(4):
            turned[n, at, :] = sums[n]
        return carry

    lax.fori_loop(0, 4, chunk, 0)
    charge = q_ref[...]
    for d in range(3):
        force_ref[d] = near_ref[d] - charge * turned[d].T
    phi_ref[...] = near_ref[3] + turned[3].T


def far_field(coords, charge, place, returned, near):
    whole = pl.BlockSpec(memory_space=VMEM)
    return pl.pallas_call(
        far_kernel,
        out_shape=(
            jax.ShapeDtypeStruct(coords.shape, jnp.float32),
            jax.ShapeDtypeStruct(charge.shape, jnp.float32),
        ),
        in_specs=[whole] * 6,
        out_specs=(whole, whole),
        scratch_shapes=[
            VMEM((4,) + charge.shape, jnp.float32),
            VMEM((G_ROWS, LANES), jnp.float32),
        ],
        compiler_params=pltpu.CompilerParams(vmem_limit_bytes=16 * MIB),
        name="far_field",
    )(coords, charge, place, returned, near, jnp.asarray(gradient_matrix()))


def padded(ops):
    return jnp.pad(ops, ((0, 0), (0, LANES - COEF), (0, LANES - COEF)))


def shards(
    positions,
    charges,
    block_leaf,
    leaf_slot,
    m2m_ops,
    l2l_ops,
    m2l_ops,
    item_target,
    item_source,
    item_offset,
    coarse_target,
    coarse_source,
    coarse_offset,
):
    blocks = block_leaf.shape[0]
    leaves_all = leaf_slot.shape[0]
    parents_all = leaves_all // 8
    coords = positions.reshape(3, blocks, LANES)
    charge = charges.reshape(blocks, LANES)
    table = leaf_slot.reshape(leaves_all // LANES, LANES)

    packed, place = block_moments(coords, charge, block_leaf.reshape(1, blocks), table)
    arrived = lax.all_to_all(packed, "dom", split_axis=0, concat_axis=0, tiled=True)
    leaf_moments, parents_part, ids = leaves(arrived, table, padded(m2m_ops))
    source_table = lax.all_gather(leaf_moments, ("dom", "lvl"), axis=0, tiled=True)
    parents_own = lax.psum_scatter(parents_part, "dom", scatter_dimension=0, tiled=True)
    parent_table = lax.all_gather(parents_own, ("lvl", "dom"), axis=0, tiled=True)

    leaf_keys, leaf_count = listed(
        item_target.reshape(-1), item_source.reshape(-1), item_offset.reshape(-1), 4 * LEAF_DEV, leaves_all, 8192
    )
    coarse_keys, coarse_count = listed(
        coarse_target.reshape(-1), coarse_source.reshape(-1), coarse_offset.reshape(-1), LEAF_DEV, parents_all, 4096
    )
    leaf_keys, coarse_keys = ordered(leaf_keys, coarse_keys)
    near = near_field(coords, charge)

    helper_terms = translate(leaf_keys, leaf_count, source_table, m2l_ops, 4 * LEAF_DEV)
    leaf_locals = lax.psum_scatter(helper_terms, "lvl", scatter_dimension=0, tiled=True)
    parent_locals = translate(coarse_keys, coarse_count, parent_table, m2l_ops, LEAF_DEV)
    sent = slot_locals(leaf_locals, parent_locals, ids, arrived, padded(l2l_ops))
    returned = lax.all_to_all(sent, "dom", split_axis=0, concat_axis=0, tiled=True)
    forces, potential = far_field(coords, charge, place, returned, near)
    return forces.reshape(3, blocks * LANES), potential.reshape(blocks * LANES)


def solution(mesh):
    in_specs = (
        P(None, ("dom", "lvl")),
        P(("dom", "lvl")),
        P(("dom", "lvl")),
        P(),
        P(),
        P(),
        P(),
        P("dom", "lvl", None),
        P("dom", "lvl", None),
        P("dom", "lvl", None),
        P("dom", "lvl", None),
        P("dom", "lvl", None),
        P("dom", "lvl", None),
    )
    out_specs = (P(None, ("dom", "lvl")), P(("dom", "lvl")))
    return jax.shard_map(shards, mesh=mesh, in_specs=in_specs, out_specs=out_specs, check_vma=False)
```

```python
import functools
import math

import jax
import jax.numpy as jnp
import numpy as np
from jax import lax
from jax.experimental import pallas as pl
from jax.experimental.pallas import tpu as pltpu
from jax.sharding import PartitionSpec as P

COEF = 81
TOP = 8
LANES = 128
LEAF_DEV = 64
CAP = 8
GROUP = 4
SOFTENING = 0.04
HIGH = lax.Precision.HIGHEST
VMEM = pltpu.VMEM
MIB = 1 << 20
MESH = pl.DeviceIdType.MESH


def dot(a, b, contract=((1,), (0,))):
    return lax.dot_general(
        a, b, (contract, ((), ())), precision=HIGH, preferred_element_type=jnp.float32
    )


def row_index(degree, azimuth, imaginary):
    start = degree * degree
    return start if azimuth == 0 else start + 2 * azimuth - 1 + int(imaginary)


def row_weight(degree, azimuth):
    return math.sqrt(math.factorial(degree + azimuth) * math.factorial(degree - azimuth))


def harmonics(x, y, z, emit):
    squared = x * x + y * y + z * z
    diag_re, diag_im = None, None
    for azimuth in range(TOP + 1):
        if azimuth == 1:
            diag_re, diag_im = -0.5 * x, -0.5 * y
        elif azimuth > 1:
            factor = -1.0 / (2.0 * azimuth)
            fx, fy = factor * x, factor * y
            diag_re, diag_im = fx * diag_re - fy * diag_im, fx * diag_im + fy * diag_re
        if azimuth == 0:
            parts = [jnp.ones_like(x)]
        else:
            parts = [diag_re, diag_im]
        for which, value in enumerate(parts):
            lower, upper = None, value
            for degree in range(azimuth, TOP + 1):
                if degree > azimuth:
                    factor = 1.0 / ((degree + azimuth) * (degree - azimuth))
                    if degree == 1 and azimuth == 0:
                        fresh = z
                    elif lower is None:
                        fresh = (factor * (2 * degree - 1)) * z * upper
                    else:
                        fresh = (factor * (2 * degree - 1)) * z * upper - (factor * squared) * lower
                    lower, upper = upper, fresh
                emit(row_index(degree, azimuth, which == 1), degree, upper)


def weight_column():
    out = np.zeros((LANES, 1), np.float32)
    for degree in range(TOP + 1):
        for azimuth in range(degree + 1):
            for imaginary in range(2 if azimuth else 1):
                out[row_index(degree, azimuth, imaginary), 0] = row_weight(degree, azimuth)
    return out


G_ROWS = 96 + 3 * 64


def gradient_matrix():
    out = np.zeros((G_ROWS, LANES), np.float64)

    def add(axis, row, degree, azimuth, value_re, value_im):
        if degree < 0 or azimuth > degree:
            return
        out[96 + 64 * axis + row_index(degree, azimuth, 0), row] += value_re
        if azimuth:
            out[96 + 64 * axis + row_index(degree, azimuth, 1), row] += value_im

    for degree in range(TOP + 1):
        for azimuth in range(degree + 1):
            for imaginary in range(2 if azimuth else 1):
                row = row_index(degree, azimuth, imaginary)
                w = row_weight(degree, azimuth)
                out[row, row] = w
                below = degree - 1
                if imaginary:
                    add(2, row, below, azimuth, 0.0, w)
                    add(0, row, below, azimuth + 1, 0.0, 0.5 * w)
                    add(0, row, below, azimuth - 1, 0.0, -0.5 * w)
                    add(1, row, below, azimuth + 1, -0.5 * w, 0.0)
                    add(1, row, below, azimuth - 1, -0.5 * w, 0.0)
                elif azimuth:
                    add(2, row, below, azimuth, w, 0.0)
                    add(0, row, below, azimuth + 1, 0.5 * w, 0.0)
                    add(0, row, below, azimuth - 1, -0.5 * w, 0.0)
                    add(1, row, below, azimuth + 1, 0.0, 0.5 * w)
                    add(1, row, below, azimuth - 1, 0.0, 0.5 * w)
                else:
                    add(2, row, below, 0, w, 0.0)
                    add(0, row, below, 1, w, 0.0)
                    add(1, row, below, 1, 0.0, w)
    return out.astype(np.float32)


def iota(shape, dim):
    return lax.broadcasted_iota(jnp.int32, shape, dim)


def moments_kernel(pos_ref, q_ref, leaf_ref, table_ref, weight_ref, packed_ref, place_ref, turned, acc, rows):
    blocks = leaf_ref.shape[1]
    leaf = leaf_ref[...]
    high = (iota((64, blocks), 0) == (leaf >> 7)).astype(jnp.float32)
    lines = dot(table_ref[...].astype(jnp.float32), high, ((0,), (0,)))
    slot = jnp.sum(
        jnp.where(iota((LANES, blocks), 0) == (leaf & 127), lines, 0.0), axis=0, keepdims=True
    ).astype(jnp.int32)
    owner = slot >> 8
    hits = iota((32, blocks), 0) == owner
    earlier = (iota((blocks, blocks), 0) < iota((blocks, blocks), 1)).astype(jnp.float32)
    before = dot(hits.astype(jnp.float32), earlier)
    rank = jnp.sum(jnp.where(hits, before, 0.0), axis=0, keepdims=True).astype(jnp.int32)
    place = owner * CAP + rank
    place_ref[...] = place

    for d in range(3):
        turned[d] = pos_ref[d].T
    turned[3] = q_ref[...].T
    acc[...] = jnp.zeros_like(acc)

    def chunk(i, carry):
        at = pl.ds(pl.multiple_of(i * 32, 32), 32)
        x, y, z, q = (turned[d, at, :] for d in range(4))

        def emit(row, degree, value):
            part = q * value
            acc[row] += (part[0:8] + part[8:16]) + (part[16:24] + part[24:32])

        harmonics(x, y, z, emit)
        return carry

    lax.fori_loop(0, 4, chunk, 0)
    rows[...] = jnp.zeros_like(rows)
    for k in range(COEF):
        rows[k : k + 1, :] = jnp.sum(acc[k], axis=0, keepdims=True)
    rows[...] = rows[...] * weight_ref[...]
    rows[127:128, :] = ((slot & 63) + 1).astype(jnp.float32)
    moments = rows[...].T
    spread = (iota((32 * CAP, blocks), 0) == place).astype(jnp.float32)
    packed_ref[...] = dot(spread, moments)


def block_moments(coords, charge, leaf, table):
    blocks = coords.shape[1]
    whole = pl.BlockSpec(memory_space=VMEM)
    return pl.pallas_call(
        moments_kernel,
        out_shape=(
            jax.ShapeDtypeStruct((32 * CAP, LANES), jnp.float32),
            jax.ShapeDtypeStruct((1, blocks), jnp.int32),
        ),
        in_specs=[whole] * 5,
        out_specs=(whole, whole),
        scratch_shapes=[
            VMEM((4, LANES, blocks), jnp.float32),
            VMEM((COEF, 8, blocks), jnp.float32),
            VMEM((LANES, blocks), jnp.float32),
        ],
        compiler_params=pltpu.CompilerParams(vmem_limit_bytes=16 * MIB),
        name="block_moments",
    )(coords, charge, leaf, table, jnp.asarray(weight_column()))


def leaves_kernel(arrived_ref, table_ref, ops_ref, leaf_ref, parent_ref, ids_ref):
    group = lax.axis_index("lvl")
    first = (lax.axis_index("dom") * GROUP + group) * LEAF_DEV
    arrived = arrived_ref[...]
    tags = arrived[:, 127:128].astype(jnp.int32)
    member = (iota((arrived.shape[0], LEAF_DEV), 1) + 1 == tags).astype(jnp.float32)
    leaf = dot(member, arrived, ((0,), (0,)))
    leaf = jnp.where(iota(leaf.shape, 1) < COEF, leaf, 0.0)
    leaf_ref[...] = leaf
    slots = first + iota((LEAF_DEV, LANES), 0)
    found = jnp.zeros((LEAF_DEV, LANES), jnp.int32)
    lane = iota((LEAF_DEV, LANES), 1)
    table = table_ref[pl.ds(pl.multiple_of(group * 16, 16), 16), :]
    for h in range(16):
        number = (group * 16 + h) * 128 + lane
        found = found + jnp.where(table[h : h + 1, :] == slots, number, 0)
    ids = jnp.sum(found.astype(jnp.float32), axis=1, keepdims=True).astype(jnp.int32)
    ids_ref[...] = jnp.broadcast_to(ids, (LEAF_DEV, LANES))
    octant = ids & 7
    children = jnp.zeros((LEAF_DEV, LANES), jnp.float32)
    for o in range(8):
        children = children + dot(jnp.where(octant == o, leaf, 0.0), ops_ref[o], ((1,), (1,)))
    within = (ids >> 3) - group * 256
    picks = (iota((LEAF_DEV, 256), 1) == within).astype(jnp.float32)
    parent_ref[...] = dot(picks, children, ((0,), (0,)))


def leaves(arrived, table, ops):
    whole = pl.BlockSpec(memory_space=VMEM)
    return pl.pallas_call(
        leaves_kernel,
        out_shape=(
            jax.ShapeDtypeStruct((LEAF_DEV, LANES), jnp.float32),
            jax.ShapeDtypeStruct((256, LANES), jnp.float32),
            jax.ShapeDtypeStruct((LEAF_DEV, LANES), jnp.int32),
        ),
        in_specs=[whole] * 3,
        out_specs=(whole,) * 3,
        compiler_params=pltpu.CompilerParams(vmem_limit_bytes=16 * MIB),
        name="leaf_moments",
    )(arrived, table, ops)


def bitonic(x):
    rows = x.shape[0]
    index = iota(x.shape, 0) * LANES + iota(x.shape, 1)
    size = rows * LANES
    span = 2
    while span <= size:
        step = span // 2
        while step >= 1:
            axis, shift, extent = (1, step, LANES) if step < LANES else (0, step // LANES, rows)
            second = (index & step) != 0
            other = jnp.where(
                second, pltpu.roll(x, shift, axis), pltpu.roll(x, extent - shift, axis)
            )
            ascending = (index & span) == 0
            take_small = ascending != second
            x = jnp.where(take_small, jnp.minimum(x, other), jnp.maximum(x, other))
            step //= 2
        span *= 2
    return x


def order_kernel(leaf_ref, coarse_ref, leaf_out, coarse_out):
    leaf_out[...] = bitonic(leaf_ref[...])
    coarse_out[...] = bitonic(coarse_ref[...])


def listed(target, source, offset, targets, none, room):
    key = (target << 23) | (source << 9) | offset
    numbers = jnp.arange(targets, dtype=jnp.int32)
    count = jnp.sum((target[:, None] == numbers[None, :]).astype(jnp.int32), axis=0)
    fours = (count + 3) >> 2
    missing = fours * 4 - count
    turn = jnp.arange(3, dtype=jnp.int32)[:, None]
    fill_target = jnp.where(turn < missing[None, :], numbers[None, :], targets - 1)
    fill = ((fill_target << 23) | (none << 9)).reshape(-1)
    rest = jnp.full((room - key.shape[0] - fill.shape[0],), ((targets - 1) << 23) | (none << 9), jnp.int32)
    keys = jnp.concatenate([key, fill, rest]).reshape(room // LANES, LANES)
    return keys, jnp.sum(fours).reshape(1)


def ordered(leaf_keys, coarse_keys):
    whole = pl.BlockSpec(memory_space=VMEM)
    return pl.pallas_call(
        order_kernel,
        out_shape=(
            jax.ShapeDtypeStruct(leaf_keys.shape, jnp.int32),
            jax.ShapeDtypeStruct(coarse_keys.shape, jnp.int32),
        ),
        in_specs=[whole] * 2,
        out_specs=(whole,) * 2,
        name="order",
    )(leaf_keys, coarse_keys)


def translate_kernel(targets, sources, keys, count, src_hbm, ops_hbm, out_ref, ops, src, acc, sems):
    load_ops = pltpu.make_async_copy(ops_hbm, ops, sems.at[0])
    load_src = pltpu.make_async_copy(src_hbm, src.at[pl.ds(0, sources)], sems.at[1])
    load_ops.start()
    load_src.start()
    src[pl.ds(sources, 8), :] = jnp.zeros((8, LANES), jnp.float32)

    def clear(t, carry):
        acc[t] = jnp.zeros(acc.shape[1:], jnp.float32)
        return carry

    lax.fori_loop(0, targets, clear, 0)
    load_ops.wait()
    load_src.wait()

    def term(at):
        key = keys[at]
        row = src[pl.ds((key >> 9) & 16383, 1), :][:, :COEF]
        return ops[key & 511] * row

    def step(i, carry):
        for u in range(2):
            at = i * 8 + u * 4
            target = keys[at] >> 23
            total = (term(at) + term(at + 1)) + (term(at + 2) + term(at + 3))
            acc[target] += total
        return carry

    lax.fori_loop(0, (count[0] + 1) // 2, step, 0)
    diagonal = iota((COEF, LANES), 0) == iota((COEF, LANES), 1)

    def finish(i, carry):
        for u in range(4):
            t = i * 4 + u
            sums = jnp.sum(acc[t], axis=1, keepdims=True)
            out_ref[pl.ds(t, 1), :] = jnp.sum(
                jnp.where(diagonal, sums, 0.0), axis=0, keepdims=True
            )
        return carry

    lax.fori_loop(0, targets // 4, finish, 0)


def translate(keys, count, table, ops, targets):
    sources = table.shape[0]
    smem = pl.BlockSpec(memory_space=pltpu.SMEM)
    far = pl.BlockSpec(memory_space=pl.ANY)
    return pl.pallas_call(
        functools.partial(translate_kernel, targets, sources),
        out_shape=jax.ShapeDtypeStruct((targets, LANES), jnp.float32),
        in_specs=[smem, smem, far, far],
        out_specs=pl.BlockSpec(memory_space=VMEM),
        scratch_shapes=[
            VMEM(ops.shape, jnp.float32),
            VMEM((sources + 8, LANES), jnp.float32),
            VMEM((targets, COEF, COEF), jnp.float32),
            pltpu.SemaphoreType.DMA((2,)),
        ],
        compiler_params=pltpu.CompilerParams(vmem_limit_bytes=48 * MIB),
        name="translate",
    )(keys.reshape(-1), count, table, ops)


def near_groups(pos_ref, q_ref, out_ref, low, high):
    def group(g, carry):
        at = pl.ds(pl.multiple_of(g * 8, 8), 8)
        rows = [pos_ref[d, at, :] for d in range(3)] + [q_ref[at, :]]
        columns = [r.T for r in rows]
        for b in range(8):
            xj, yj, zj, qj = (r[b : b + 1, :] for r in rows)
            xi, yi, zi, qi = (c[:, b : b + 1] for c in columns)
            sums = [jnp.zeros((8, LANES), jnp.float32) for _ in range(4)]
            for c in range(4):
                part = slice(c * 32, c * 32 + 32)
                dx = xj - xi[part]
                dy = yj - yi[part]
                dz = zj - zi[part]
                inverse = lax.rsqrt(dx * dx + dy * dy + dz * dz + SOFTENING)
                same = iota((32, LANES), 0) + c * 32 == iota((32, LANES), 1)
                weighted = jnp.where(same, 0.0, inverse * qi[part])
                strength = weighted * (inverse * inverse)
                for n, term in enumerate((strength * dx, strength * dy, strength * dz, weighted)):
                    sums[n] = sums[n] + ((term[0:8] + term[8:16]) + (term[16:24] + term[24:32]))
            for n in range(4):
                line = jnp.sum(sums[n], axis=0, keepdims=True)
                if n < 3:
                    line = line * qj
                out_ref[n, pl.ds(g * 8 + b, 1), :] = line
        return carry

    lax.fori_loop(low, high, group, 0)


PARTS = ((0, 16, 24, (2, 0, 1)), (24, 32, 48, (0, 1, 2)), (48, 56, 64, (1, 2, 0)))
COPIES = 81


def gather_kernel(leaf_ref, part_ref, pos_ref, q_ref, all_ref, parent_ref, near_ref, got_c, got_x, got_y, sum_c, sum_x, send_sem, recv_sem):
    dom = lax.axis_index("dom")
    here = (dom // 8, (dom // 2) % 4, lax.axis_index("lvl"))
    core = dom % 2

    def device(place, which):
        return ((place[0] * 4 + place[1]) * 2 + which, place[2])

    def moved(axis, by):
        return tuple((v + by) % 4 if n == axis else v for n, v in enumerate(here))

    twin = device(here, 1 - core)
    barrier = pltpu.get_barrier_semaphore()
    for axis in range(3):
        for by in (1, 2, 3):
            pl.semaphore_signal(barrier, inc=1, device_id=device(moved(axis, by), core), device_id_type=MESH)
    pl.semaphore_signal(barrier, inc=1, device_id=twin, device_id_type=MESH)
    all_ref[here[0], here[1], core, here[2]] = leaf_ref[...]
    pl.semaphore_wait(barrier, 10)

    started = []

    def send(source, target, where):
        n = len(started)
        copy = pltpu.make_async_remote_copy(
            src_ref=source,
            dst_ref=target,
            send_sem=send_sem.at[n],
            recv_sem=recv_sem.at[n],
            device_id=where,
            device_id_type=MESH,
        )
        copy.start()
        started.append(copy)
        return copy

    def block(done, axis, by, low, high):
        y, x, z = (
            slice(None) if n in done else ((here[n] + by) % 4 if n == axis else here[n]) for n in range(3)
        )
        return all_ref.at[y, x, core, z, slice(low, high)]

    def put(ref, where):
        return send(ref, ref, where)

    def parents(done):
        y, x, z = (slice(None) if n in done else here[n] for n in range(3))
        return parent_ref.at[z, y, x, core]

    waiting = {}

    def stage(n):
        if n == 0:
            waiting["p"] = [send(part_ref.at[:, :, 1 - core], got_c, twin)]
            return
        for copy in waiting["p"]:
            copy.wait_recv()
        if n == 1:
            sum_c[...] = part_ref[:, :, core] + got_c[...]
            waiting["p"] = [
                send(sum_c.at[:, (here[1] + by) % 4], got_x.at[by - 1], device(moved(1, by), core)) for by in (1, 2, 3)
            ]
        elif n == 2:
            sum_x[...] = (sum_c[:, here[1]] + got_x[0]) + (got_x[1] + got_x[2])
            waiting["p"] = [
                send(sum_x.at[(here[0] + by) % 4], got_y.at[by - 1], device(moved(0, by), core)) for by in (1, 2, 3)
            ]
        elif n == 3:
            parent_ref[here[2], here[0], here[1], core] = (sum_x[here[0]] + got_y[0]) + (got_y[1] + got_y[2])
            waiting["p"] = [put(parents(()), device(moved(2, by), core)) for by in (1, 2, 3)]
        elif n == 4:
            waiting["p"] = [put(parents((2,)), device(moved(0, by), core)) for by in (1, 2, 3)]
        elif n == 5:
            waiting["p"] = [put(parents((2, 0)), device(moved(1, by), core)) for by in (1, 2, 3)]
        elif n == 6:
            waiting["p"] = [put(parents((2, 0, 1)), twin)]

    fill = ((0, 1), (1, 3), (3, 5), (5, 8), (8, 12), (12, 16))
    last = [put(block((), 0, 0, 0, 64), twin)]
    for phase in range(3):
        first = []
        for low, middle, high, order in PARTS:
            axis, done = order[phase], order[:phase]
            first.append(
                [put(block(done, axis, 0, low, high), device(moved(axis, by), core)) for by in (1, 3)]
            )
        stage(2 * phase)
        near_groups(pos_ref, q_ref, near_ref, *fill[2 * phase])
        second = []
        for (low, middle, high, order), (right, left) in zip(PARTS, first):
            axis, done = order[phase], order[:phase]
            right.wait_recv()
            a = put(block(done, axis, 3, low, middle), device(moved(axis, 1), core))
            left.wait_recv()
            b = put(block(done, axis, 1, middle, high), device(moved(axis, 3), core))
            second.append((a, b))
            last.append(put(block(done, axis, 3, low, high), twin))
            last.append(put(block(done, axis, 1, low, high), twin))
        stage(2 * phase + 1)
        near_groups(pos_ref, q_ref, near_ref, *fill[2 * phase + 1])
        for (low, middle, high, order), pair in zip(PARTS, second):
            axis, done = order[phase], order[:phase]
            for copy in pair:
                copy.wait_recv()
            last.append(put(block(done, axis, 2, low, high), twin))
    stage(6)
    for copy in last:
        copy.wait_recv()
    for copy in waiting["p"]:
        copy.wait_recv()
    for copy in started:
        copy.wait_send()
    assert len(started) == COPIES


def gather(leaf, parts, coords, charge):
    whole = pl.BlockSpec(memory_space=VMEM)
    f32 = jnp.float32
    return pl.pallas_call(
        gather_kernel,
        out_shape=(
            jax.ShapeDtypeStruct((4, 4, 2, 4, LEAF_DEV, LANES), f32),
            jax.ShapeDtypeStruct((4, 4, 4, 2, 8, LANES), f32),
            jax.ShapeDtypeStruct((4,) + charge.shape, f32),
        ),
        in_specs=[whole] * 4,
        out_specs=(whole,) * 3,
        scratch_shapes=[
            VMEM((4, 4, 8, LANES), f32),
            VMEM((3, 4, 8, LANES), f32),
            VMEM((3, 8, LANES), f32),
            VMEM((4, 4, 8, LANES), f32),
            VMEM((4, 8, LANES), f32),
            pltpu.SemaphoreType.DMA((COPIES,)),
            pltpu.SemaphoreType.DMA((COPIES,)),
        ],
        compiler_params=pltpu.CompilerParams(collective_id=0, has_side_effects=True, vmem_limit_bytes=24 * MIB),
        name="gather",
    )(leaf, parts.reshape(4, 4, 2, 8, LANES), coords, charge)


def locals_kernel(leaf_ref, parent_ref, ids_ref, arrived_ref, ops_ref, out_ref):
    octant = ids_ref[...] & 7
    parent = parent_ref[...]
    total = leaf_ref[...]
    for o in range(8):
        total = total + dot(jnp.where(octant == o, parent, 0.0), ops_ref[o], ((1,), (1,)))
    tags = arrived_ref[:, 127:128].astype(jnp.int32)
    member = (iota((arrived_ref.shape[0], LEAF_DEV), 1) + 1 == tags).astype(jnp.float32)
    out_ref[...] = dot(member, total)


def slot_locals(leaf_locals, parent_locals, ids, arrived, ops):
    whole = pl.BlockSpec(memory_space=VMEM)
    return pl.pallas_call(
        locals_kernel,
        out_shape=jax.ShapeDtypeStruct(arrived.shape, jnp.float32),
        in_specs=[whole] * 5,
        out_specs=whole,
        compiler_params=pltpu.CompilerParams(vmem_limit_bytes=16 * MIB),
        name="slot_locals",
    )(leaf_locals, parent_locals, ids, arrived, ops)


def far_kernel(pos_ref, q_ref, place_ref, returned_ref, near_ref, matrix_ref, force_ref, phi_ref, turned, lines):
    blocks = q_ref.shape[0]
    spread = (iota((32 * CAP, blocks), 0) == place_ref[...]).astype(jnp.float32)
    columns = dot(returned_ref[...], spread, ((0,), (0,)))
    lines[...] = dot(matrix_ref[...], columns)
    for d in range(3):
        turned[d] = pos_ref[d].T

    def chunk(i, carry):
        at = pl.ds(pl.multiple_of(i * 32, 32), 32)
        x, y, z = (turned[d, at, :] for d in range(3))
        sums = [None] * 4

        def emit(row, degree, value):
            starts = [(3, 0)] + ([(d, 96 + 64 * d) for d in range(3)] if degree < TOP else [])
            for n, start in starts:
                term = lines[start + row : start + row + 1, :] * value
                sums[n] = term if sums[n] is None else sums[n] + term

        harmonics(x, y, z, emit)
        for n in range(4):
            turned[n, at, :] = sums[n]
        return carry

    lax.fori_loop(0, 4, chunk, 0)
    charge = q_ref[...]
    for d in range(3):
        force_ref[d] = near_ref[d] - charge * turned[d].T
    phi_ref[...] = near_ref[3] + turned[3].T


def far_field(coords, charge, place, returned, near):
    whole = pl.BlockSpec(memory_space=VMEM)
    return pl.pallas_call(
        far_kernel,
        out_shape=(
            jax.ShapeDtypeStruct(coords.shape, jnp.float32),
            jax.ShapeDtypeStruct(charge.shape, jnp.float32),
        ),
        in_specs=[whole] * 6,
        out_specs=(whole, whole),
        scratch_shapes=[
            VMEM((4,) + charge.shape, jnp.float32),
            VMEM((G_ROWS, LANES), jnp.float32),
        ],
        compiler_params=pltpu.CompilerParams(vmem_limit_bytes=16 * MIB),
        name="far_field",
    )(coords, charge, place, returned, near, jnp.asarray(gradient_matrix()))


def padded(ops):
    return jnp.pad(ops, ((0, 0), (0, LANES - COEF), (0, LANES - COEF)))


def shards(
    positions,
    charges,
    block_leaf,
    leaf_slot,
    m2m_ops,
    l2l_ops,
    m2l_ops,
    item_target,
    item_source,
    item_offset,
    coarse_target,
    coarse_source,
    coarse_offset,
):
    blocks = block_leaf.shape[0]
    leaves_all = leaf_slot.shape[0]
    parents_all = leaves_all // 8
    coords = positions.reshape(3, blocks, LANES)
    charge = charges.reshape(blocks, LANES)
    table = leaf_slot.reshape(leaves_all // LANES, LANES)

    packed, place = block_moments(coords, charge, block_leaf.reshape(1, blocks), table)
    arrived = lax.all_to_all(packed, "dom", split_axis=0, concat_axis=0, tiled=True)
    leaf_moments, parents_part, ids = leaves(arrived, table, padded(m2m_ops))
    source_table, parent_table, near = gather(leaf_moments, parents_part, coords, charge)
    source_table = source_table.reshape(leaves_all, LANES)
    parent_table = parent_table.reshape(parents_all, LANES)
    leaf_keys, leaf_count = listed(
        item_target.reshape(-1), item_source.reshape(-1), item_offset.reshape(-1), 4 * LEAF_DEV, leaves_all, 8192
    )
    coarse_keys, coarse_count = listed(
        coarse_target.reshape(-1), coarse_source.reshape(-1), coarse_offset.reshape(-1), LEAF_DEV, parents_all, 4096
    )
    leaf_keys, coarse_keys = ordered(leaf_keys, coarse_keys)

    helper_terms = translate(leaf_keys, leaf_count, source_table, m2l_ops, 4 * LEAF_DEV)
    leaf_locals = lax.psum_scatter(helper_terms, "lvl", scatter_dimension=0, tiled=True)
    parent_locals = translate(coarse_keys, coarse_count, parent_table, m2l_ops, LEAF_DEV)
    sent = slot_locals(leaf_locals, parent_locals, ids, arrived, padded(l2l_ops))
    returned = lax.all_to_all(sent, "dom", split_axis=0, concat_axis=0, tiled=True)
    forces, potential = far_field(coords, charge, place, returned, near)
    return forces.reshape(3, blocks * LANES), potential.reshape(blocks * LANES)


def solution(mesh):
    in_specs = (
        P(None, ("dom", "lvl")),
        P(("dom", "lvl")),
        P(("dom", "lvl")),
        P(),
        P(),
        P(),
        P(),
        P("dom", "lvl", None),
        P("dom", "lvl", None),
        P("dom", "lvl", None),
        P("dom", "lvl", None),
        P("dom", "lvl", None),
        P("dom", "lvl", None),
    )
    out_specs = (P(None, ("dom", "lvl")), P(("dom", "lvl")))
    return jax.shard_map(shards, mesh=mesh, in_specs=in_specs, out_specs=out_specs, check_vma=False)
```

```python
import functools
import itertools
import math

import jax
import jax.numpy as jnp
import numpy as np
from jax import lax
from jax.experimental import pallas as pl
from jax.experimental.pallas import tpu as pltpu
from jax.sharding import PartitionSpec as P

COEF = 81
TOP = 8
LANES = 128
LEAF_DEV = 64
CAP = 8
GROUP = 4
SOFTENING = 0.04
HIGH = lax.Precision.HIGHEST
VMEM = pltpu.VMEM
MIB = 1 << 20
MESH = pl.DeviceIdType.MESH


def dot(a, b, contract=((1,), (0,))):
    return lax.dot_general(
        a, b, (contract, ((), ())), precision=HIGH, preferred_element_type=jnp.float32
    )


def row_index(degree, azimuth, imaginary):
    start = degree * degree
    return start if azimuth == 0 else start + 2 * azimuth - 1 + int(imaginary)


def row_weight(degree, azimuth):
    return math.sqrt(math.factorial(degree + azimuth) * math.factorial(degree - azimuth))


def harmonics(x, y, z, emit):
    squared = x * x + y * y + z * z
    diag_re, diag_im = None, None
    for azimuth in range(TOP + 1):
        if azimuth == 1:
            diag_re, diag_im = -0.5 * x, -0.5 * y
        elif azimuth > 1:
            factor = -1.0 / (2.0 * azimuth)
            fx, fy = factor * x, factor * y
            diag_re, diag_im = fx * diag_re - fy * diag_im, fx * diag_im + fy * diag_re
        if azimuth == 0:
            parts = [jnp.ones_like(x)]
        else:
            parts = [diag_re, diag_im]
        for which, value in enumerate(parts):
            lower, upper = None, value
            for degree in range(azimuth, TOP + 1):
                if degree > azimuth:
                    factor = 1.0 / ((degree + azimuth) * (degree - azimuth))
                    if degree == 1 and azimuth == 0:
                        fresh = z
                    elif lower is None:
                        fresh = (factor * (2 * degree - 1)) * z * upper
                    else:
                        fresh = (factor * (2 * degree - 1)) * z * upper - (factor * squared) * lower
                    lower, upper = upper, fresh
                emit(row_index(degree, azimuth, which == 1), degree, upper)


def weight_column():
    out = np.zeros((LANES, 1), np.float32)
    for degree in range(TOP + 1):
        for azimuth in range(degree + 1):
            for imaginary in range(2 if azimuth else 1):
                out[row_index(degree, azimuth, imaginary), 0] = row_weight(degree, azimuth)
    return out


G_ROWS = 96 + 3 * 64


def gradient_matrix():
    out = np.zeros((G_ROWS, LANES), np.float64)

    def add(axis, row, degree, azimuth, value_re, value_im):
        if degree < 0 or azimuth > degree:
            return
        out[96 + 64 * axis + row_index(degree, azimuth, 0), row] += value_re
        if azimuth:
            out[96 + 64 * axis + row_index(degree, azimuth, 1), row] += value_im

    for degree in range(TOP + 1):
        for azimuth in range(degree + 1):
            for imaginary in range(2 if azimuth else 1):
                row = row_index(degree, azimuth, imaginary)
                w = row_weight(degree, azimuth)
                out[row, row] = w
                below = degree - 1
                if imaginary:
                    add(2, row, below, azimuth, 0.0, w)
                    add(0, row, below, azimuth + 1, 0.0, 0.5 * w)
                    add(0, row, below, azimuth - 1, 0.0, -0.5 * w)
                    add(1, row, below, azimuth + 1, -0.5 * w, 0.0)
                    add(1, row, below, azimuth - 1, -0.5 * w, 0.0)
                elif azimuth:
                    add(2, row, below, azimuth, w, 0.0)
                    add(0, row, below, azimuth + 1, 0.5 * w, 0.0)
                    add(0, row, below, azimuth - 1, -0.5 * w, 0.0)
                    add(1, row, below, azimuth + 1, 0.0, 0.5 * w)
                    add(1, row, below, azimuth - 1, 0.0, 0.5 * w)
                else:
                    add(2, row, below, 0, w, 0.0)
                    add(0, row, below, 1, w, 0.0)
                    add(1, row, below, 1, 0.0, w)
    return out.astype(np.float32)


def iota(shape, dim):
    return lax.broadcasted_iota(jnp.int32, shape, dim)


def moments_kernel(pos_ref, q_ref, leaf_ref, table_ref, weight_ref, packed_ref, place_ref, turned, acc, rows):
    blocks = leaf_ref.shape[1]
    leaf = leaf_ref[...]
    high = (iota((64, blocks), 0) == (leaf >> 7)).astype(jnp.float32)
    lines = dot(table_ref[...].astype(jnp.float32), high, ((0,), (0,)))
    slot = jnp.sum(
        jnp.where(iota((LANES, blocks), 0) == (leaf & 127), lines, 0.0), axis=0, keepdims=True
    ).astype(jnp.int32)
    owner = slot >> 8
    hits = iota((32, blocks), 0) == owner
    earlier = (iota((blocks, blocks), 0) < iota((blocks, blocks), 1)).astype(jnp.float32)
    before = dot(hits.astype(jnp.float32), earlier)
    rank = jnp.sum(jnp.where(hits, before, 0.0), axis=0, keepdims=True).astype(jnp.int32)
    place = owner * CAP + rank
    place_ref[...] = place

    for d in range(3):
        turned[d] = pos_ref[d].T
    turned[3] = q_ref[...].T
    acc[...] = jnp.zeros_like(acc)

    def chunk(i, carry):
        at = pl.ds(pl.multiple_of(i * 32, 32), 32)
        x, y, z, q = (turned[d, at, :] for d in range(4))

        def emit(row, degree, value):
            part = q * value
            acc[row] += (part[0:8] + part[8:16]) + (part[16:24] + part[24:32])

        harmonics(x, y, z, emit)
        return carry

    lax.fori_loop(0, 4, chunk, 0)
    rows[...] = jnp.zeros_like(rows)
    for k in range(COEF):
        rows[k : k + 1, :] = jnp.sum(acc[k], axis=0, keepdims=True)
    rows[...] = rows[...] * weight_ref[...]
    rows[127:128, :] = ((slot & 63) + 1).astype(jnp.float32)
    moments = rows[...].T
    spread = (iota((32 * CAP, blocks), 0) == place).astype(jnp.float32)
    packed_ref[...] = dot(spread, moments)


def block_moments(coords, charge, leaf, table):
    blocks = coords.shape[1]
    whole = pl.BlockSpec(memory_space=VMEM)
    return pl.pallas_call(
        moments_kernel,
        out_shape=(
            jax.ShapeDtypeStruct((32 * CAP, LANES), jnp.float32),
            jax.ShapeDtypeStruct((1, blocks), jnp.int32),
        ),
        in_specs=[whole] * 5,
        out_specs=(whole, whole),
        scratch_shapes=[
            VMEM((4, LANES, blocks), jnp.float32),
            VMEM((COEF, 8, blocks), jnp.float32),
            VMEM((LANES, blocks), jnp.float32),
        ],
        compiler_params=pltpu.CompilerParams(vmem_limit_bytes=16 * MIB),
        name="block_moments",
    )(coords, charge, leaf, table, jnp.asarray(weight_column()))


def leaves_kernel(arrived_ref, table_ref, ops_ref, leaf_ref, parent_ref, ids_ref):
    group = lax.axis_index("lvl")
    first = (lax.axis_index("dom") * GROUP + group) * LEAF_DEV
    arrived = arrived_ref[...]
    tags = arrived[:, 127:128].astype(jnp.int32)
    member = (iota((arrived.shape[0], LEAF_DEV), 1) + 1 == tags).astype(jnp.float32)
    leaf = dot(member, arrived, ((0,), (0,)))
    leaf = jnp.where(iota(leaf.shape, 1) < COEF, leaf, 0.0)
    leaf_ref[...] = leaf
    slots = first + iota((LEAF_DEV, LANES), 0)
    found = jnp.zeros((LEAF_DEV, LANES), jnp.int32)
    lane = iota((LEAF_DEV, LANES), 1)
    table = table_ref[pl.ds(pl.multiple_of(group * 16, 16), 16), :]
    for h in range(16):
        number = (group * 16 + h) * 128 + lane
        found = found + jnp.where(table[h : h + 1, :] == slots, number, 0)
    ids = jnp.sum(found.astype(jnp.float32), axis=1, keepdims=True).astype(jnp.int32)
    ids_ref[...] = jnp.broadcast_to(ids, (LEAF_DEV, LANES))
    octant = ids & 7
    children = jnp.zeros((LEAF_DEV, LANES), jnp.float32)
    for o in range(8):
        children = children + dot(jnp.where(octant == o, leaf, 0.0), ops_ref[o], ((1,), (1,)))
    within = (ids >> 3) - group * 256
    picks = (iota((LEAF_DEV, 256), 1) == within).astype(jnp.float32)
    parent_ref[...] = dot(picks, children, ((0,), (0,)))


def leaves(arrived, table, ops):
    whole = pl.BlockSpec(memory_space=VMEM)
    return pl.pallas_call(
        leaves_kernel,
        out_shape=(
            jax.ShapeDtypeStruct((LEAF_DEV, LANES), jnp.float32),
            jax.ShapeDtypeStruct((256, LANES), jnp.float32),
            jax.ShapeDtypeStruct((LEAF_DEV, LANES), jnp.int32),
        ),
        in_specs=[whole] * 3,
        out_specs=(whole,) * 3,
        compiler_params=pltpu.CompilerParams(vmem_limit_bytes=16 * MIB),
        name="leaf_moments",
    )(arrived, table, ops)


def bitonic_stages(size):
    out, span = [], 2
    while span <= size:
        step = span // 2
        while step >= 1:
            out.append((span, step))
            step //= 2
        span *= 2
    return out


def bitonic_stage(x, span, step):
    rows = x.shape[0]
    index = iota(x.shape, 0) * LANES + iota(x.shape, 1)
    axis, shift, extent = (1, step, LANES) if step < LANES else (0, step // LANES, rows)
    second = (index & step) != 0
    other = jnp.where(second, pltpu.roll(x, shift, axis), pltpu.roll(x, extent - shift, axis))
    take_small = ((index & span) == 0) != second
    return jnp.where(take_small, jnp.minimum(x, other), jnp.maximum(x, other))


def write_keys(items, targets, none, keys_ref, count_ref):
    target_ref, source_ref, offset_ref = items
    rows = target_ref.shape[0]
    keys_ref[...] = jnp.full(keys_ref.shape, ((targets - 1) << 23) | (none << 9), jnp.int32)
    keys_ref[0:rows, :] = (target_ref[...] << 23) | (source_ref[...] << 9) | offset_ref[...]
    numbers = iota((targets, LANES), 0)
    count = jnp.zeros((targets, LANES), jnp.float32)
    for r in range(rows):
        count = count + (numbers == target_ref[r : r + 1, :]).astype(jnp.float32)
    count = jnp.sum(count, axis=1, keepdims=True)
    fours = jnp.zeros((1, 1), jnp.int32)
    for p in range((targets + LANES - 1) // LANES):
        size = min(LANES, targets - p * LANES)
        part = count[p * LANES : p * LANES + size]
        diagonal = iota((size, LANES), 0) == iota((size, LANES), 1)
        line = jnp.sum(jnp.where(diagonal, part, 0.0), axis=0, keepdims=True).astype(jnp.int32)
        filled = (line + 3) >> 2
        fours = fours + jnp.sum(filled.astype(jnp.float32), axis=1, keepdims=True).astype(jnp.int32)
        own = iota((1, LANES), 1) + p * LANES
        for turn in range(3):
            goal = jnp.where(turn < filled * 4 - line, own, targets - 1)
            at = rows + 3 * p + turn
            keys_ref[at : at + 1, :] = (goal << 23) | (none << 9)
    count_ref[...] = jnp.broadcast_to(fours, count_ref.shape)


def translate_kernel(targets, sources, keys, count, src_hbm, ops_hbm, out_ref, ops, src, acc, sems):
    load_ops = pltpu.make_async_copy(ops_hbm, ops, sems.at[0])
    load_src = pltpu.make_async_copy(src_hbm, src.at[pl.ds(0, sources)], sems.at[1])
    load_ops.start()
    load_src.start()
    src[pl.ds(sources, 8), :] = jnp.zeros((8, LANES), jnp.float32)

    def clear(t, carry):
        acc[t] = jnp.zeros(acc.shape[1:], jnp.float32)
        return carry

    lax.fori_loop(0, targets, clear, 0)
    load_ops.wait()
    load_src.wait()

    def term(at):
        key = keys[at]
        row = src[pl.ds((key >> 9) & 16383, 1), :][:, :COEF]
        return ops[key & 511] * row

    def step(i, carry):
        for u in range(2):
            at = i * 8 + u * 4
            target = keys[at] >> 23
            total = (term(at) + term(at + 1)) + (term(at + 2) + term(at + 3))
            acc[target] += total
        return carry

    lax.fori_loop(0, (count[0, 0] + 1) // 2, step, 0)
    diagonal = iota((COEF, LANES), 0) == iota((COEF, LANES), 1)

    def finish(i, carry):
        for u in range(4):
            t = i * 4 + u
            sums = jnp.sum(acc[t], axis=1, keepdims=True)
            out_ref[pl.ds(t, 1), :] = jnp.sum(
                jnp.where(diagonal, sums, 0.0), axis=0, keepdims=True
            )
        return carry

    lax.fori_loop(0, targets // 4, finish, 0)


def translate(keys, count, table, ops, targets):
    sources = table.shape[0]
    smem = pl.BlockSpec(memory_space=pltpu.SMEM)
    far = pl.BlockSpec(memory_space=pl.ANY)
    return pl.pallas_call(
        functools.partial(translate_kernel, targets, sources),
        out_shape=jax.ShapeDtypeStruct((targets, LANES), jnp.float32),
        in_specs=[smem, smem, far, far],
        out_specs=pl.BlockSpec(memory_space=VMEM),
        scratch_shapes=[
            VMEM(ops.shape, jnp.float32),
            VMEM((sources + 8, LANES), jnp.float32),
            VMEM((targets, COEF, COEF), jnp.float32),
            pltpu.SemaphoreType.DMA((2,)),
        ],
        compiler_params=pltpu.CompilerParams(vmem_limit_bytes=48 * MIB),
        name="translate",
    )(keys.reshape(-1), count, table, ops)


def near_groups(pos_ref, q_ref, out_ref, low, high):
    def group(g, carry):
        at = pl.ds(pl.multiple_of(g * 8, 8), 8)
        rows = [pos_ref[d, at, :] for d in range(3)] + [q_ref[at, :]]
        columns = [r.T for r in rows]
        for b in range(8):
            xj, yj, zj, qj = (r[b : b + 1, :] for r in rows)
            xi, yi, zi, qi = (c[:, b : b + 1] for c in columns)
            sums = [jnp.zeros((8, LANES), jnp.float32) for _ in range(4)]
            for c in range(4):
                part = slice(c * 32, c * 32 + 32)
                dx = xj - xi[part]
                dy = yj - yi[part]
                dz = zj - zi[part]
                inverse = lax.rsqrt(dx * dx + dy * dy + dz * dz + SOFTENING)
                same = iota((32, LANES), 0) + c * 32 == iota((32, LANES), 1)
                weighted = jnp.where(same, 0.0, inverse * qi[part])
                strength = weighted * (inverse * inverse)
                for n, term in enumerate((strength * dx, strength * dy, strength * dz, weighted)):
                    sums[n] = sums[n] + ((term[0:8] + term[8:16]) + (term[16:24] + term[24:32]))
            for n in range(4):
                line = jnp.sum(sums[n], axis=0, keepdims=True)
                if n < 3:
                    line = line * qj
                out_ref[n, pl.ds(g * 8 + b, 1), :] = line
        return carry

    lax.fori_loop(low, high, group, 0)


PARTS = ((0, 16, 24, (2, 0, 1)), (24, 32, 48, (0, 1, 2)), (48, 56, 64, (1, 2, 0)))
COPIES = 81


def gather_kernel(
    leaf_ref, part_ref, pos_ref, q_ref, lt_ref, ls_ref, lo_ref, ct_ref, cs_ref, co_ref,
    all_ref, parent_ref, near_ref, lkeys_ref, lcount_ref, ckeys_ref, ccount_ref, got_c, got_x, got_y, sum_c, sum_x, send_sem, recv_sem
):
    dom = lax.axis_index("dom")
    here = (dom // 8, (dom // 2) % 4, lax.axis_index("lvl"))
    core = dom % 2

    def device(place, which):
        return ((place[0] * 4 + place[1]) * 2 + which, place[2])

    def moved(axis, by):
        return tuple((v + by) % 4 if n == axis else v for n, v in enumerate(here))

    twin = device(here, 1 - core)
    barrier = pltpu.get_barrier_semaphore()
    for axis in range(3):
        for by in (1, 2, 3):
            pl.semaphore_signal(barrier, inc=1, device_id=device(moved(axis, by), core), device_id_type=MESH)
    pl.semaphore_signal(barrier, inc=1, device_id=twin, device_id_type=MESH)
    all_ref[here[0], here[1], core, here[2]] = leaf_ref[...]
    pl.semaphore_wait(barrier, 10)

    started = []

    def send(source, target, where):
        n = len(started)
        copy = pltpu.make_async_remote_copy(
            src_ref=source,
            dst_ref=target,
            send_sem=send_sem.at[n],
            recv_sem=recv_sem.at[n],
            device_id=where,
            device_id_type=MESH,
        )
        copy.start()
        started.append(copy)
        return copy

    def block(done, axis, by, low, high):
        y, x, z = (
            slice(None) if n in done else ((here[n] + by) % 4 if n == axis else here[n]) for n in range(3)
        )
        return all_ref.at[y, x, core, z, slice(low, high)]

    def put(ref, where):
        return send(ref, ref, where)

    def parents(done):
        y, x, z = (slice(None) if n in done else here[n] for n in range(3))
        return parent_ref.at[z, y, x, core]

    waiting = {}

    def stage(n):
        if n == 0:
            waiting["p"] = [send(part_ref.at[:, :, 1 - core], got_c, twin)]
            return
        for copy in waiting["p"]:
            copy.wait_recv()
        if n == 1:
            sum_c[...] = part_ref[:, :, core] + got_c[...]
            waiting["p"] = [
                send(sum_c.at[:, (here[1] + by) % 4], got_x.at[by - 1], device(moved(1, by), core)) for by in (1, 2, 3)
            ]
        elif n == 2:
            sum_x[...] = (sum_c[:, here[1]] + got_x[0]) + (got_x[1] + got_x[2])
            waiting["p"] = [
                send(sum_x.at[(here[0] + by) % 4], got_y.at[by - 1], device(moved(0, by), core)) for by in (1, 2, 3)
            ]
        elif n == 3:
            parent_ref[here[2], here[0], here[1], core] = (sum_x[here[0]] + got_y[0]) + (got_y[1] + got_y[2])
            waiting["p"] = [put(parents(()), device(moved(2, by), core)) for by in (1, 2, 3)]
        elif n == 4:
            waiting["p"] = [put(parents((2,)), device(moved(0, by), core)) for by in (1, 2, 3)]
        elif n == 5:
            waiting["p"] = [put(parents((2, 0)), device(moved(1, by), core)) for by in (1, 2, 3)]
        elif n == 6:
            waiting["p"] = [put(parents((2, 0, 1)), twin)]

    sorts = [
        (keys, stage)
        for pair in itertools.zip_longest(
            *([(keys, stage) for stage in bitonic_stages(keys.shape[0] * LANES)] for keys in (lkeys_ref, ckeys_ref))
        )
        for keys, stage in filter(None, pair)
    ]

    def sort(low, high):
        now = {}
        for keys, stage in sorts[low:high]:
            name = id(keys)
            if name not in now:
                now[name] = (keys, keys[...])
            now[name] = (keys, bitonic_stage(now[name][1], *stage))
        for keys, value in now.values():
            keys[...] = value

    def fill(n):
        if n == 0:
            write_keys((lt_ref, ls_ref, lo_ref), 4 * LEAF_DEV, 8192, lkeys_ref, lcount_ref)
            write_keys((ct_ref, cs_ref, co_ref), LEAF_DEV, 1024, ckeys_ref, ccount_ref)
        elif n < 4:
            sort(60 * (n - 1), 60 * n)
        else:
            near_groups(pos_ref, q_ref, near_ref, *((0, 7), (7, 14), (14, 16))[n - 4])

    last = [put(block((), 0, 0, 0, 64), twin)]
    for phase in range(3):
        first = []
        for low, middle, high, order in PARTS:
            axis, done = order[phase], order[:phase]
            first.append(
                [put(block(done, axis, 0, low, high), device(moved(axis, by), core)) for by in (1, 3)]
            )
        stage(2 * phase)
        fill(2 * phase)
        second = []
        for (low, middle, high, order), (right, left) in zip(PARTS, first):
            axis, done = order[phase], order[:phase]
            right.wait_recv()
            a = put(block(done, axis, 3, low, middle), device(moved(axis, 1), core))
            left.wait_recv()
            b = put(block(done, axis, 1, middle, high), device(moved(axis, 3), core))
            second.append((a, b))
            last.append(put(block(done, axis, 3, low, high), twin))
            last.append(put(block(done, axis, 1, low, high), twin))
        stage(2 * phase + 1)
        fill(2 * phase + 1)
        for (low, middle, high, order), pair in zip(PARTS, second):
            axis, done = order[phase], order[:phase]
            for copy in pair:
                copy.wait_recv()
            last.append(put(block(done, axis, 2, low, high), twin))
    stage(6)
    fill(6)
    for copy in last:
        copy.wait_recv()
    for copy in waiting["p"]:
        copy.wait_recv()
    for copy in started:
        copy.wait_send()
    assert len(started) == COPIES


def gather(leaf, parts, coords, charge, leaf_items, coarse_items):
    whole = pl.BlockSpec(memory_space=VMEM)
    f32 = jnp.float32
    return pl.pallas_call(
        gather_kernel,
        out_shape=(
            jax.ShapeDtypeStruct((4, 4, 2, 4, LEAF_DEV, LANES), f32),
            jax.ShapeDtypeStruct((4, 4, 4, 2, 8, LANES), f32),
            jax.ShapeDtypeStruct((4,) + charge.shape, f32),
            jax.ShapeDtypeStruct((64, LANES), jnp.int32),
            jax.ShapeDtypeStruct((1, LANES), jnp.int32),
            jax.ShapeDtypeStruct((32, LANES), jnp.int32),
            jax.ShapeDtypeStruct((1, LANES), jnp.int32),
        ),
        in_specs=[whole] * 10,
        out_specs=(whole,) * 7,
        scratch_shapes=[
            VMEM((4, 4, 8, LANES), f32),
            VMEM((3, 4, 8, LANES), f32),
            VMEM((3, 8, LANES), f32),
            VMEM((4, 4, 8, LANES), f32),
            VMEM((4, 8, LANES), f32),
            pltpu.SemaphoreType.DMA((COPIES,)),
            pltpu.SemaphoreType.DMA((COPIES,)),
        ],
        compiler_params=pltpu.CompilerParams(collective_id=0, has_side_effects=True, vmem_limit_bytes=24 * MIB),
        name="gather",
    )(
        leaf, parts.reshape(4, 4, 2, 8, LANES), coords, charge,
        *(a.reshape(-1, LANES) for a in leaf_items + coarse_items),
    )


def far_kernel(
    terms_ref, parent_ref, ids_ref, arrived_ref, ops_ref, pos_ref, q_ref, place_ref, near_ref, matrix_ref,
    force_ref, phi_ref, got, sent, returned, turned, lines, send_sem, recv_sem
):
    dom, lvl = lax.axis_index("dom"), lax.axis_index("lvl")
    blocks = q_ref.shape[0]
    barrier = pltpu.get_barrier_semaphore()

    def greet(d, carry):
        pl.semaphore_signal(barrier, inc=1, device_id=((dom + d) % 32, lvl), device_id_type=MESH)
        return carry

    for by in (1, 2, 3):
        pl.semaphore_signal(barrier, inc=1, device_id=(dom, (lvl + by) % 4), device_id_type=MESH)
    lax.fori_loop(1, 32, greet, 0)
    pl.semaphore_wait(barrier, 34)

    shared = []
    for by in (1, 2, 3):
        goal = (lvl + by) % 4
        copy = pltpu.make_async_remote_copy(
            src_ref=terms_ref.at[goal],
            dst_ref=got.at[by - 1],
            send_sem=send_sem.at[31 + by],
            recv_sem=recv_sem.at[31 + by],
            device_id=(dom, goal),
            device_id_type=MESH,
        )
        copy.start()
        shared.append(copy)

    octant = ids_ref[...] & 7
    parent = parent_ref[...]
    total = terms_ref[lvl]
    for o in range(8):
        total = total + dot(jnp.where(octant == o, parent, 0.0), ops_ref[o], ((1,), (1,)))
    tags = arrived_ref[:, 127:128].astype(jnp.int32)
    member = (iota((arrived_ref.shape[0], LEAF_DEV), 1) + 1 == tags).astype(jnp.float32)
    for copy in shared:
        copy.wait_recv()
    total = (total + got[0]) + (got[1] + got[2])
    sent[...] = dot(member, total).reshape(sent.shape)

    def message(d):
        goal = (dom + d) % 32
        return pltpu.make_async_remote_copy(
            src_ref=sent.at[goal],
            dst_ref=returned.at[dom],
            send_sem=send_sem.at[d],
            recv_sem=recv_sem.at[d],
            device_id=(goal, lvl),
            device_id_type=MESH,
        )

    def start(d, carry):
        message(d).start()
        return carry

    lax.fori_loop(1, 32, start, 0)
    returned[dom] = sent[dom]
    for d in range(3):
        turned[d] = pos_ref[d].T
    spread = (iota((32 * CAP, blocks), 0) == place_ref[...]).astype(jnp.float32)

    def receive(d, carry):
        message(d).wait_recv()
        return carry

    lax.fori_loop(1, 32, receive, 0)
    columns = dot(returned[...].reshape(32 * CAP, LANES), spread, ((0,), (0,)))
    lines[...] = dot(matrix_ref[...], columns)

    def chunk(i, carry):
        at = pl.ds(pl.multiple_of(i * 32, 32), 32)
        x, y, z = (turned[d, at, :] for d in range(3))
        sums = [None] * 4

        def emit(row, degree, value):
            starts = [(3, 0)] + ([(d, 96 + 64 * d) for d in range(3)] if degree < TOP else [])
            for n, start in starts:
                term = lines[start + row : start + row + 1, :] * value
                sums[n] = term if sums[n] is None else sums[n] + term

        harmonics(x, y, z, emit)
        for n in range(4):
            turned[n, at, :] = sums[n]
        return carry

    lax.fori_loop(0, 4, chunk, 0)
    charge = q_ref[...]
    for d in range(3):
        force_ref[d] = near_ref[d] - charge * turned[d].T
    phi_ref[...] = near_ref[3] + turned[3].T

    def leave(d, carry):
        message(d).wait_send()
        return carry

    lax.fori_loop(1, 32, leave, 0)
    for copy in shared:
        copy.wait_send()


def far_field(terms, parent_locals, ids, arrived, ops, coords, charge, place, near):
    whole = pl.BlockSpec(memory_space=VMEM)
    f32 = jnp.float32
    return pl.pallas_call(
        far_kernel,
        out_shape=(
            jax.ShapeDtypeStruct(coords.shape, f32),
            jax.ShapeDtypeStruct(charge.shape, f32),
        ),
        in_specs=[whole] * 10,
        out_specs=(whole, whole),
        scratch_shapes=[
            VMEM((3, LEAF_DEV, LANES), f32),
            VMEM((32, CAP, LANES), f32),
            VMEM((32, CAP, LANES), f32),
            VMEM((4,) + charge.shape, f32),
            VMEM((G_ROWS, LANES), f32),
            pltpu.SemaphoreType.DMA((35,)),
            pltpu.SemaphoreType.DMA((35,)),
        ],
        compiler_params=pltpu.CompilerParams(collective_id=1, has_side_effects=True, vmem_limit_bytes=16 * MIB),
        name="far_field",
    )(
        terms.reshape(GROUP, LEAF_DEV, LANES), parent_locals, ids, arrived, ops, coords, charge, place, near,
        jnp.asarray(gradient_matrix()),
    )


def padded(ops):
    return jnp.pad(ops, ((0, 0), (0, LANES - COEF), (0, LANES - COEF)))


def shards(
    positions,
    charges,
    block_leaf,
    leaf_slot,
    m2m_ops,
    l2l_ops,
    m2l_ops,
    item_target,
    item_source,
    item_offset,
    coarse_target,
    coarse_source,
    coarse_offset,
):
    blocks = block_leaf.shape[0]
    leaves_all = leaf_slot.shape[0]
    parents_all = leaves_all // 8
    coords = positions.reshape(3, blocks, LANES)
    charge = charges.reshape(blocks, LANES)
    table = leaf_slot.reshape(leaves_all // LANES, LANES)

    packed, place = block_moments(coords, charge, block_leaf.reshape(1, blocks), table)
    arrived = lax.all_to_all(packed, "dom", split_axis=0, concat_axis=0, tiled=True)
    leaf_moments, parents_part, ids = leaves(arrived, table, padded(m2m_ops))
    source_table, parent_table, near, leaf_keys, leaf_count, coarse_keys, coarse_count = gather(
        leaf_moments,
        parents_part,
        coords,
        charge,
        (item_target, item_source, item_offset),
        (coarse_target, coarse_source, coarse_offset),
    )
    source_table = source_table.reshape(leaves_all, LANES)
    parent_table = parent_table.reshape(parents_all, LANES)
    parent_locals = translate(coarse_keys, coarse_count, parent_table, m2l_ops, LEAF_DEV)
    terms = translate(leaf_keys, leaf_count, source_table, m2l_ops, 4 * LEAF_DEV)
    forces, potential = far_field(
        terms, parent_locals, ids, arrived, padded(l2l_ops), coords, charge, place, near
    )
    return forces.reshape(3, blocks * LANES), potential.reshape(blocks * LANES)


def solution(mesh):
    in_specs = (
        P(None, ("dom", "lvl")),
        P(("dom", "lvl")),
        P(("dom", "lvl")),
        P(),
        P(),
        P(),
        P(),
        P("dom", "lvl", None),
        P("dom", "lvl", None),
        P("dom", "lvl", None),
        P("dom", "lvl", None),
        P("dom", "lvl", None),
        P("dom", "lvl", None),
    )
    out_specs = (P(None, ("dom", "lvl")), P(("dom", "lvl")))
    return jax.shard_map(shards, mesh=mesh, in_specs=in_specs, out_specs=out_specs, check_vma=False)
```

```python
import functools
import itertools
import math

import jax
import jax.numpy as jnp
import numpy as np
from jax import lax
from jax.experimental import pallas as pl
from jax.experimental.pallas import tpu as pltpu
from jax.sharding import PartitionSpec as P

COEF = 81
OFFSETS = 316
ROWS = 88
TOP = 8
LANES = 128
LEAF_DEV = 64
CAP = 8
GROUP = 4
SOFTENING = 0.04
HIGH = lax.Precision.HIGHEST
VMEM = pltpu.VMEM
MIB = 1 << 20
MESH = pl.DeviceIdType.MESH


def dot(a, b, contract=((1,), (0,))):
    return lax.dot_general(
        a, b, (contract, ((), ())), precision=HIGH, preferred_element_type=jnp.float32
    )


def row_index(degree, azimuth, imaginary):
    start = degree * degree
    return start if azimuth == 0 else start + 2 * azimuth - 1 + int(imaginary)


def row_weight(degree, azimuth):
    return math.sqrt(math.factorial(degree + azimuth) * math.factorial(degree - azimuth))


def harmonics(x, y, z, emit):
    squared = x * x + y * y + z * z
    diag_re, diag_im = None, None
    for azimuth in range(TOP + 1):
        if azimuth == 1:
            diag_re, diag_im = -0.5 * x, -0.5 * y
        elif azimuth > 1:
            factor = -1.0 / (2.0 * azimuth)
            fx, fy = factor * x, factor * y
            diag_re, diag_im = fx * diag_re - fy * diag_im, fx * diag_im + fy * diag_re
        if azimuth == 0:
            parts = [jnp.ones_like(x)]
        else:
            parts = [diag_re, diag_im]
        for which, value in enumerate(parts):
            lower, upper = None, value
            for degree in range(azimuth, TOP + 1):
                if degree > azimuth:
                    factor = 1.0 / ((degree + azimuth) * (degree - azimuth))
                    if degree == 1 and azimuth == 0:
                        fresh = z
                    elif lower is None:
                        fresh = (factor * (2 * degree - 1)) * z * upper
                    else:
                        fresh = (factor * (2 * degree - 1)) * z * upper - (factor * squared) * lower
                    lower, upper = upper, fresh
                emit(row_index(degree, azimuth, which == 1), degree, upper)


def weight_column():
    out = np.zeros((LANES, 1), np.float32)
    for degree in range(TOP + 1):
        for azimuth in range(degree + 1):
            for imaginary in range(2 if azimuth else 1):
                out[row_index(degree, azimuth, imaginary), 0] = row_weight(degree, azimuth)
    return out


G_ROWS = 96 + 3 * 64


def gradient_matrix():
    out = np.zeros((G_ROWS, LANES), np.float64)

    def add(axis, row, degree, azimuth, value_re, value_im):
        if degree < 0 or azimuth > degree:
            return
        out[96 + 64 * axis + row_index(degree, azimuth, 0), row] += value_re
        if azimuth:
            out[96 + 64 * axis + row_index(degree, azimuth, 1), row] += value_im

    for degree in range(TOP + 1):
        for azimuth in range(degree + 1):
            for imaginary in range(2 if azimuth else 1):
                row = row_index(degree, azimuth, imaginary)
                w = row_weight(degree, azimuth)
                out[row, row] = w
                below = degree - 1
                if imaginary:
                    add(2, row, below, azimuth, 0.0, w)
                    add(0, row, below, azimuth + 1, 0.0, 0.5 * w)
                    add(0, row, below, azimuth - 1, 0.0, -0.5 * w)
                    add(1, row, below, azimuth + 1, -0.5 * w, 0.0)
                    add(1, row, below, azimuth - 1, -0.5 * w, 0.0)
                elif azimuth:
                    add(2, row, below, azimuth, w, 0.0)
                    add(0, row, below, azimuth + 1, 0.5 * w, 0.0)
                    add(0, row, below, azimuth - 1, -0.5 * w, 0.0)
                    add(1, row, below, azimuth + 1, 0.0, 0.5 * w)
                    add(1, row, below, azimuth - 1, 0.0, 0.5 * w)
                else:
                    add(2, row, below, 0, w, 0.0)
                    add(0, row, below, 1, w, 0.0)
                    add(1, row, below, 1, 0.0, w)
    return out.astype(np.float32)


def iota(shape, dim):
    return lax.broadcasted_iota(jnp.int32, shape, dim)


def moments_kernel(pos_ref, q_ref, leaf_ref, table_ref, weight_ref, packed_ref, place_ref, turned, acc, rows):
    blocks = leaf_ref.shape[1]
    leaf = leaf_ref[...]
    high = (iota((64, blocks), 0) == (leaf >> 7)).astype(jnp.float32)
    lines = dot(table_ref[...].astype(jnp.float32), high, ((0,), (0,)))
    slot = jnp.sum(
        jnp.where(iota((LANES, blocks), 0) == (leaf & 127), lines, 0.0), axis=0, keepdims=True
    ).astype(jnp.int32)
    owner = slot >> 8
    hits = iota((32, blocks), 0) == owner
    earlier = (iota((blocks, blocks), 0) < iota((blocks, blocks), 1)).astype(jnp.float32)
    before = dot(hits.astype(jnp.float32), earlier)
    rank = jnp.sum(jnp.where(hits, before, 0.0), axis=0, keepdims=True).astype(jnp.int32)
    place = owner * CAP + rank
    place_ref[...] = place

    for d in range(3):
        turned[d] = pos_ref[d].T
    turned[3] = q_ref[...].T
    acc[...] = jnp.zeros_like(acc)

    def chunk(i, carry):
        at = pl.ds(pl.multiple_of(i * 32, 32), 32)
        x, y, z, q = (turned[d, at, :] for d in range(4))

        def emit(row, degree, value):
            part = q * value
            acc[row] += (part[0:8] + part[8:16]) + (part[16:24] + part[24:32])

        harmonics(x, y, z, emit)
        return carry

    lax.fori_loop(0, 4, chunk, 0)
    rows[...] = jnp.zeros_like(rows)
    for k in range(COEF):
        rows[k : k + 1, :] = jnp.sum(acc[k], axis=0, keepdims=True)
    rows[...] = rows[...] * weight_ref[...]
    rows[127:128, :] = ((slot & 63) + 1).astype(jnp.float32)
    moments = rows[...].T
    spread = (iota((32 * CAP, blocks), 0) == place).astype(jnp.float32)
    packed_ref[...] = dot(spread, moments)


def block_moments(coords, charge, leaf, table):
    blocks = coords.shape[1]
    whole = pl.BlockSpec(memory_space=VMEM)
    return pl.pallas_call(
        moments_kernel,
        out_shape=(
            jax.ShapeDtypeStruct((32 * CAP, LANES), jnp.float32),
            jax.ShapeDtypeStruct((1, blocks), jnp.int32),
        ),
        in_specs=[whole] * 5,
        out_specs=(whole, whole),
        scratch_shapes=[
            VMEM((4, LANES, blocks), jnp.float32),
            VMEM((COEF, 8, blocks), jnp.float32),
            VMEM((LANES, blocks), jnp.float32),
        ],
        compiler_params=pltpu.CompilerParams(vmem_limit_bytes=16 * MIB),
        name="block_moments",
    )(coords, charge, leaf, table, jnp.asarray(weight_column()))


def leaves_kernel(arrived_ref, table_ref, ops_ref, leaf_ref, parent_ref, ids_ref):
    group = lax.axis_index("lvl")
    first = (lax.axis_index("dom") * GROUP + group) * LEAF_DEV
    arrived = arrived_ref[...]
    tags = arrived[:, 127:128].astype(jnp.int32)
    member = (iota((arrived.shape[0], LEAF_DEV), 1) + 1 == tags).astype(jnp.float32)
    leaf = dot(member, arrived, ((0,), (0,)))
    leaf = jnp.where(iota(leaf.shape, 1) < COEF, leaf, 0.0)
    leaf_ref[...] = leaf
    slots = first + iota((LEAF_DEV, LANES), 0)
    found = jnp.zeros((LEAF_DEV, LANES), jnp.int32)
    lane = iota((LEAF_DEV, LANES), 1)
    table = table_ref[pl.ds(pl.multiple_of(group * 16, 16), 16), :]
    for h in range(16):
        number = (group * 16 + h) * 128 + lane
        found = found + jnp.where(table[h : h + 1, :] == slots, number, 0)
    ids = jnp.sum(found.astype(jnp.float32), axis=1, keepdims=True).astype(jnp.int32)
    ids_ref[...] = jnp.broadcast_to(ids, (LEAF_DEV, LANES))
    octant = ids & 7
    children = jnp.zeros((LEAF_DEV, LANES), jnp.float32)
    for o in range(8):
        children = children + dot(jnp.where(octant == o, leaf, 0.0), ops_ref[o], ((1,), (1,)))
    within = (ids >> 3) - group * 256
    picks = (iota((LEAF_DEV, 256), 1) == within).astype(jnp.float32)
    parent_ref[...] = dot(picks, children, ((0,), (0,)))


def leaves(arrived, table, ops):
    whole = pl.BlockSpec(memory_space=VMEM)
    return pl.pallas_call(
        leaves_kernel,
        out_shape=(
            jax.ShapeDtypeStruct((LEAF_DEV, LANES), jnp.float32),
            jax.ShapeDtypeStruct((256, LANES), jnp.float32),
            jax.ShapeDtypeStruct((LEAF_DEV, LANES), jnp.int32),
        ),
        in_specs=[whole] * 3,
        out_specs=(whole,) * 3,
        compiler_params=pltpu.CompilerParams(vmem_limit_bytes=16 * MIB),
        name="leaf_moments",
    )(arrived, table, ops)


def bitonic_stages(size):
    out, span = [], 2
    while span <= size:
        step = span // 2
        while step >= 1:
            out.append((span, step))
            step //= 2
        span *= 2
    return out


def bitonic_stage(x, span, step):
    rows = x.shape[0]
    index = iota(x.shape, 0) * LANES + iota(x.shape, 1)
    axis, shift, extent = (1, step, LANES) if step < LANES else (0, step // LANES, rows)
    second = (index & step) != 0
    other = jnp.where(second, pltpu.roll(x, shift, axis), pltpu.roll(x, extent - shift, axis))
    take_small = ((index & span) == 0) != second
    return jnp.where(take_small, jnp.minimum(x, other), jnp.maximum(x, other))


def write_keys(items, targets, sources, keys_ref, count_ref):
    target_ref, source_ref, offset_ref = items
    rows = target_ref.shape[0]
    none = ((sources - 1) << 9) | OFFSETS
    keys_ref[...] = jnp.full(keys_ref.shape, ((targets - 1) << 23) | none, jnp.int32)
    keys_ref[0:rows, :] = (target_ref[...] << 23) | (source_ref[...] << 9) | offset_ref[...]
    numbers = iota((targets, LANES), 0)
    count = jnp.zeros((targets, LANES), jnp.float32)
    for r in range(rows):
        count = count + (numbers == target_ref[r : r + 1, :]).astype(jnp.float32)
    count = jnp.sum(count, axis=1, keepdims=True)
    fours = jnp.zeros((1, 1), jnp.int32)
    for p in range((targets + LANES - 1) // LANES):
        size = min(LANES, targets - p * LANES)
        part = count[p * LANES : p * LANES + size]
        diagonal = iota((size, LANES), 0) == iota((size, LANES), 1)
        line = jnp.sum(jnp.where(diagonal, part, 0.0), axis=0, keepdims=True).astype(jnp.int32)
        filled = (line + 3) >> 2
        fours = fours + jnp.sum(filled.astype(jnp.float32), axis=1, keepdims=True).astype(jnp.int32)
        own = iota((1, LANES), 1) + p * LANES
        for turn in range(3):
            goal = jnp.where(turn < filled * 4 - line, own, targets - 1)
            at = rows + 3 * p + turn
            keys_ref[at : at + 1, :] = (goal << 23) | none
    count_ref[...] = jnp.broadcast_to(fours, count_ref.shape)


def translate_kernel(leaf_keys, leaf_count, coarse_keys, coarse_count, leaf_src, coarse_src, ops, leaf_out, coarse_out, acc):
    def work(keys, count, src, out):
        targets = out.shape[0]

        def clear(t, carry):
            for u in range(4):
                acc[t * 4 + u] = jnp.zeros(acc.shape[1:], jnp.float32)
            return carry

        lax.fori_loop(0, targets // 4, clear, 0)

        def term(key):
            row = src[pl.ds((key >> 9) & (src.shape[0] - 1), 1), :][:, :COEF]
            return ops[key & 511, :COEF, :COEF] * row

        def step(i, carry):
            for u in range(4):
                four = [keys[i * 16 + u * 4 + n] for n in range(4)]
                total = (term(four[0]) + term(four[1])) + (term(four[2]) + term(four[3]))
                acc[four[0] >> 23, :COEF, :COEF] += total
            return carry

        lax.fori_loop(0, (count[0, 0] + 3) // 4, step, 0)
        lane = iota((ROWS, LANES), 1)
        for low in range(0, targets, LANES):
            size = min(LANES, targets - low)

            def finish(i, columns):
                for u in range(8):
                    t = i * 8 + u
                    columns = jnp.where(lane == t, jnp.sum(acc[low + t], axis=1, keepdims=True), columns)
                return columns

            columns = lax.fori_loop(0, size // 8, finish, jnp.zeros((ROWS, LANES), jnp.float32))
            padded = jnp.concatenate([columns, jnp.zeros((LANES - ROWS, LANES), jnp.float32)], axis=0)
            out[low : low + size, :] = padded.T[:size]

    work(coarse_keys, coarse_count, coarse_src, coarse_out)
    work(leaf_keys, leaf_count, leaf_src, leaf_out)


def translate(leaf_keys, leaf_count, coarse_keys, coarse_count, leaf_table, coarse_table, ops):
    smem = pl.BlockSpec(memory_space=pltpu.SMEM)
    whole = pl.BlockSpec(memory_space=VMEM)
    return pl.pallas_call(
        translate_kernel,
        out_shape=(
            jax.ShapeDtypeStruct((4 * LEAF_DEV, LANES), jnp.float32),
            jax.ShapeDtypeStruct((LEAF_DEV, LANES), jnp.float32),
        ),
        in_specs=[smem] * 4 + [whole] * 3,
        out_specs=(whole, whole),
        scratch_shapes=[VMEM((4 * LEAF_DEV, ROWS, LANES), jnp.float32)],
        compiler_params=pltpu.CompilerParams(vmem_limit_bytes=36 * MIB),
        name="translate",
    )(leaf_keys.reshape(-1), leaf_count, coarse_keys.reshape(-1), coarse_count, leaf_table, coarse_table, ops)


def near_groups(pos_ref, q_ref, out_ref, low, high):
    def group(g, carry):
        at = pl.ds(pl.multiple_of(g * 8, 8), 8)
        rows = [pos_ref[d, at, :] for d in range(3)] + [q_ref[at, :]]
        columns = [r.T for r in rows]
        for b in range(8):
            xj, yj, zj, qj = (r[b : b + 1, :] for r in rows)
            xi, yi, zi, qi = (c[:, b : b + 1] for c in columns)
            sums = [jnp.zeros((8, LANES), jnp.float32) for _ in range(4)]
            for c in range(4):
                part = slice(c * 32, c * 32 + 32)
                dx = xj - xi[part]
                dy = yj - yi[part]
                dz = zj - zi[part]
                inverse = lax.rsqrt(dx * dx + dy * dy + dz * dz + SOFTENING)
                same = iota((32, LANES), 0) + c * 32 == iota((32, LANES), 1)
                weighted = jnp.where(same, 0.0, inverse * qi[part])
                strength = weighted * (inverse * inverse)
                for n, term in enumerate((strength * dx, strength * dy, strength * dz, weighted)):
                    sums[n] = sums[n] + ((term[0:8] + term[8:16]) + (term[16:24] + term[24:32]))
            for n in range(4):
                line = jnp.sum(sums[n], axis=0, keepdims=True)
                if n < 3:
                    line = line * qj
                out_ref[n, pl.ds(g * 8 + b, 1), :] = line
        return carry

    lax.fori_loop(low, high, group, 0)


PARTS = ((0, 16, 24, (2, 0, 1)), (24, 32, 48, (0, 1, 2)), (48, 56, 64, (1, 2, 0)))
COPIES = 81
SLABS = 9


def gather_kernel(
    leaf_ref, part_ref, pos_ref, q_ref, lt_ref, ls_ref, lo_ref, ct_ref, cs_ref, co_ref, m2l_hbm,
    all_ref, parent_ref, near_ref, lkeys_ref, lcount_ref, ckeys_ref, ccount_ref, m2l_ref, got_c, got_x, got_y, sum_c, sum_x, slabs, send_sem, recv_sem, slab_sem
):
    dom = lax.axis_index("dom")
    here = (dom // 8, (dom // 2) % 4, lax.axis_index("lvl"))
    core = dom % 2

    def device(place, which):
        return ((place[0] * 4 + place[1]) * 2 + which, place[2])

    def moved(axis, by):
        return tuple((v + by) % 4 if n == axis else v for n, v in enumerate(here))

    def slab(g, slot):
        return pltpu.make_async_copy(m2l_hbm.at[pl.ds(g * SLABS, SLABS)], slabs.at[slot], slab_sem.at[slot])

    twin = device(here, 1 - core)
    barrier = pltpu.get_barrier_semaphore()
    for axis in range(3):
        for by in (1, 2, 3):
            pl.semaphore_signal(barrier, inc=1, device_id=device(moved(axis, by), core), device_id_type=MESH)
    pl.semaphore_signal(barrier, inc=1, device_id=twin, device_id_type=MESH)
    all_ref[here[0], here[1], core, here[2]] = leaf_ref[...]
    m2l_ref[OFFSETS * ROWS :, :] = jnp.zeros((ROWS, LANES), jnp.float32)
    slab(0, 0).start()
    pl.semaphore_wait(barrier, 10)

    started = []

    def send(source, target, where):
        n = len(started)
        copy = pltpu.make_async_remote_copy(
            src_ref=source,
            dst_ref=target,
            send_sem=send_sem.at[n],
            recv_sem=recv_sem.at[n],
            device_id=where,
            device_id_type=MESH,
        )
        copy.start()
        started.append(copy)
        return copy

    def block(done, axis, by, low, high):
        y, x, z = (
            slice(None) if n in done else ((here[n] + by) % 4 if n == axis else here[n]) for n in range(3)
        )
        return all_ref.at[y, x, core, z, slice(low, high)]

    def put(ref, where):
        return send(ref, ref, where)

    def parents(done):
        y, x, z = (slice(None) if n in done else here[n] for n in range(3))
        return parent_ref.at[z, y, x, core]

    waiting = {}

    def stage(n):
        if n == 0:
            waiting["p"] = [send(part_ref.at[:, :, 1 - core], got_c, twin)]
            return
        for copy in waiting["p"]:
            copy.wait_recv()
        if n == 1:
            sum_c[...] = part_ref[:, :, core] + got_c[...]
            waiting["p"] = [
                send(sum_c.at[:, (here[1] + by) % 4], got_x.at[by - 1], device(moved(1, by), core)) for by in (1, 2, 3)
            ]
        elif n == 2:
            sum_x[...] = (sum_c[:, here[1]] + got_x[0]) + (got_x[1] + got_x[2])
            waiting["p"] = [
                send(sum_x.at[(here[0] + by) % 4], got_y.at[by - 1], device(moved(0, by), core)) for by in (1, 2, 3)
            ]
        elif n == 3:
            parent_ref[here[2], here[0], here[1], core] = (sum_x[here[0]] + got_y[0]) + (got_y[1] + got_y[2])
            waiting["p"] = [put(parents(()), device(moved(2, by), core)) for by in (1, 2, 3)]
        elif n == 4:
            waiting["p"] = [put(parents((2,)), device(moved(0, by), core)) for by in (1, 2, 3)]
        elif n == 5:
            waiting["p"] = [put(parents((2, 0)), device(moved(1, by), core)) for by in (1, 2, 3)]
        elif n == 6:
            waiting["p"] = [put(parents((2, 0, 1)), twin)]

    sorts = [
        (keys, stage)
        for pair in itertools.zip_longest(
            *([(keys, stage) for stage in bitonic_stages(keys.shape[0] * LANES)] for keys in (lkeys_ref, ckeys_ref))
        )
        for keys, stage in filter(None, pair)
    ]

    def sort(low, high):
        now = {}
        for keys, stage in sorts[low:high]:
            name = id(keys)
            if name not in now:
                now[name] = (keys, keys[...])
            now[name] = (keys, bitonic_stage(now[name][1], *stage))
        for keys, value in now.values():
            keys[...] = value

    def turn(low, high):
        def group(g, carry):
            slot = g % 2

            @pl.when(g < COEF // SLABS - 1)
            def _():
                slab(g + 1, 1 - slot).start()

            slab(g, slot).wait()
            for u in range(SLABS):
                for p in range(3):
                    wide = min(LANES, OFFSETS - p * LANES)
                    lines = slabs[slot, u, :, p * LANES : p * LANES + wide].T
                    start = p * LANES * ROWS + g * SLABS + u
                    even = wide // 8 * 8
                    m2l_ref[pl.ds(start, even, stride=ROWS), 0:COEF] = lines[:even]
                    if even < wide:
                        m2l_ref[pl.ds(start + even * ROWS, wide - even, stride=ROWS), 0:COEF] = lines[even:]
            return carry

        lax.fori_loop(low, high, group, 0)

    def fill(n):
        if n == 0:
            write_keys((lt_ref, ls_ref, lo_ref), 4 * LEAF_DEV, 8192, lkeys_ref, lcount_ref)
            write_keys((ct_ref, cs_ref, co_ref), LEAF_DEV, 1024, ckeys_ref, ccount_ref)
        elif n < 4:
            sort(60 * (n - 1), 60 * n)
        turn(*((0, 1), (1, 1), (1, 1), (1, 2), (2, 6), (6, 9), (9, 9))[n])
        near_groups(pos_ref, q_ref, near_ref, *((0, 0), (0, 0), (0, 0), (0, 0), (0, 0), (0, 2), (2, 16))[n])

    last = [put(block((), 0, 0, 0, 64), twin)]
    for phase in range(3):
        first = []
        for low, middle, high, order in PARTS:
            axis, done = order[phase], order[:phase]
            first.append(
                [put(block(done, axis, 0, low, high), device(moved(axis, by), core)) for by in (1, 3)]
            )
        stage(2 * phase)
        fill(2 * phase)
        second = []
        for (low, middle, high, order), (right, left) in zip(PARTS, first):
            axis, done = order[phase], order[:phase]
            right.wait_recv()
            a = put(block(done, axis, 3, low, middle), device(moved(axis, 1), core))
            left.wait_recv()
            b = put(block(done, axis, 1, middle, high), device(moved(axis, 3), core))
            second.append((a, b))
            last.append(put(block(done, axis, 3, low, high), twin))
            last.append(put(block(done, axis, 1, low, high), twin))
        stage(2 * phase + 1)
        fill(2 * phase + 1)
        for (low, middle, high, order), pair in zip(PARTS, second):
            axis, done = order[phase], order[:phase]
            for copy in pair:
                copy.wait_recv()
            last.append(put(block(done, axis, 2, low, high), twin))
    stage(6)
    fill(6)
    for copy in last:
        copy.wait_recv()
    for copy in waiting["p"]:
        copy.wait_recv()
    for copy in started:
        copy.wait_send()
    assert len(started) == COPIES


def gather(leaf, parts, coords, charge, leaf_items, coarse_items, ops):
    whole = pl.BlockSpec(memory_space=VMEM)
    f32 = jnp.float32
    return pl.pallas_call(
        gather_kernel,
        out_shape=(
            jax.ShapeDtypeStruct((4, 4, 2, 4, LEAF_DEV, LANES), f32),
            jax.ShapeDtypeStruct((4, 4, 4, 2, 8, LANES), f32),
            jax.ShapeDtypeStruct((4,) + charge.shape, f32),
            jax.ShapeDtypeStruct((64, LANES), jnp.int32),
            jax.ShapeDtypeStruct((1, LANES), jnp.int32),
            jax.ShapeDtypeStruct((32, LANES), jnp.int32),
            jax.ShapeDtypeStruct((1, LANES), jnp.int32),
            jax.ShapeDtypeStruct(((OFFSETS + 1) * ROWS, LANES), f32),
        ),
        in_specs=[whole] * 10 + [pl.BlockSpec(memory_space=pl.ANY)],
        out_specs=(whole,) * 8,
        scratch_shapes=[
            VMEM((4, 4, 8, LANES), f32),
            VMEM((3, 4, 8, LANES), f32),
            VMEM((3, 8, LANES), f32),
            VMEM((4, 4, 8, LANES), f32),
            VMEM((4, 8, LANES), f32),
            VMEM((2, SLABS, COEF, OFFSETS), f32),
            pltpu.SemaphoreType.DMA((COPIES,)),
            pltpu.SemaphoreType.DMA((COPIES,)),
            pltpu.SemaphoreType.DMA((2,)),
        ],
        compiler_params=pltpu.CompilerParams(collective_id=0, has_side_effects=True, vmem_limit_bytes=42 * MIB),
        name="gather",
    )(
        leaf, parts.reshape(4, 4, 2, 8, LANES), coords, charge,
        *(a.reshape(-1, LANES) for a in leaf_items + coarse_items), ops.transpose(1, 2, 0),
    )


def far_kernel(
    terms_ref, parent_ref, ids_ref, arrived_ref, ops_ref, pos_ref, q_ref, place_ref, near_ref, matrix_ref,
    force_ref, phi_ref, got, sent, returned, turned, lines, send_sem, recv_sem
):
    dom, lvl = lax.axis_index("dom"), lax.axis_index("lvl")
    blocks = q_ref.shape[0]
    barrier = pltpu.get_barrier_semaphore()

    def greet(d, carry):
        pl.semaphore_signal(barrier, inc=1, device_id=((dom + d) % 32, lvl), device_id_type=MESH)
        return carry

    for by in (1, 2, 3):
        pl.semaphore_signal(barrier, inc=1, device_id=(dom, (lvl + by) % 4), device_id_type=MESH)
    lax.fori_loop(1, 32, greet, 0)
    pl.semaphore_wait(barrier, 34)

    shared = []
    for by in (1, 2, 3):
        goal = (lvl + by) % 4
        copy = pltpu.make_async_remote_copy(
            src_ref=terms_ref.at[goal],
            dst_ref=got.at[by - 1],
            send_sem=send_sem.at[31 + by],
            recv_sem=recv_sem.at[31 + by],
            device_id=(dom, goal),
            device_id_type=MESH,
        )
        copy.start()
        shared.append(copy)

    octant = ids_ref[...] & 7
    parent = parent_ref[...]
    total = terms_ref[lvl]
    for o in range(8):
        total = total + dot(jnp.where(octant == o, parent, 0.0), ops_ref[o], ((1,), (1,)))
    tags = arrived_ref[:, 127:128].astype(jnp.int32)
    member = (iota((arrived_ref.shape[0], LEAF_DEV), 1) + 1 == tags).astype(jnp.float32)
    for copy in shared:
        copy.wait_recv()
    total = (total + got[0]) + (got[1] + got[2])
    sent[...] = dot(member, total).reshape(sent.shape)

    def message(d):
        goal = (dom + d) % 32
        return pltpu.make_async_remote_copy(
            src_ref=sent.at[goal],
            dst_ref=returned.at[dom],
            send_sem=send_sem.at[d],
            recv_sem=recv_sem.at[d],
            device_id=(goal, lvl),
            device_id_type=MESH,
        )

    def start(d, carry):
        message(d).start()
        return carry

    lax.fori_loop(1, 32, start, 0)
    returned[dom] = sent[dom]
    for d in range(3):
        turned[d] = pos_ref[d].T
    spread = (iota((32 * CAP, blocks), 0) == place_ref[...]).astype(jnp.float32)

    def receive(d, carry):
        message(d).wait_recv()
        return carry

    lax.fori_loop(1, 32, receive, 0)
    columns = dot(returned[...].reshape(32 * CAP, LANES), spread, ((0,), (0,)))
    lines[...] = dot(matrix_ref[...], columns)

    def chunk(i, carry):
        at = pl.ds(pl.multiple_of(i * 32, 32), 32)
        x, y, z = (turned[d, at, :] for d in range(3))
        sums = [None] * 4

        def emit(row, degree, value):
            starts = [(3, 0)] + ([(d, 96 + 64 * d) for d in range(3)] if degree < TOP else [])
            for n, start in starts:
                term = lines[start + row : start + row + 1, :] * value
                sums[n] = term if sums[n] is None else sums[n] + term

        harmonics(x, y, z, emit)
        for n in range(4):
            turned[n, at, :] = sums[n]
        return carry

    lax.fori_loop(0, 4, chunk, 0)
    charge = q_ref[...]
    for d in range(3):
        force_ref[d] = near_ref[d] - charge * turned[d].T
    phi_ref[...] = near_ref[3] + turned[3].T

    def leave(d, carry):
        message(d).wait_send()
        return carry

    lax.fori_loop(1, 32, leave, 0)
    for copy in shared:
        copy.wait_send()


def far_field(terms, parent_locals, ids, arrived, ops, coords, charge, place, near):
    whole = pl.BlockSpec(memory_space=VMEM)
    f32 = jnp.float32
    return pl.pallas_call(
        far_kernel,
        out_shape=(
            jax.ShapeDtypeStruct(coords.shape, f32),
            jax.ShapeDtypeStruct(charge.shape, f32),
        ),
        in_specs=[whole] * 10,
        out_specs=(whole, whole),
        scratch_shapes=[
            VMEM((3, LEAF_DEV, LANES), f32),
            VMEM((32, CAP, LANES), f32),
            VMEM((32, CAP, LANES), f32),
            VMEM((4,) + charge.shape, f32),
            VMEM((G_ROWS, LANES), f32),
            pltpu.SemaphoreType.DMA((35,)),
            pltpu.SemaphoreType.DMA((35,)),
        ],
        compiler_params=pltpu.CompilerParams(collective_id=1, has_side_effects=True, vmem_limit_bytes=16 * MIB),
        name="far_field",
    )(
        terms.reshape(GROUP, LEAF_DEV, LANES), parent_locals, ids, arrived, ops, coords, charge, place, near,
        jnp.asarray(gradient_matrix()),
    )


def padded(ops):
    return jnp.pad(ops, ((0, 0), (0, LANES - COEF), (0, LANES - COEF)))


def shards(
    positions,
    charges,
    block_leaf,
    leaf_slot,
    m2m_ops,
    l2l_ops,
    m2l_ops,
    item_target,
    item_source,
    item_offset,
    coarse_target,
    coarse_source,
    coarse_offset,
):
    blocks = block_leaf.shape[0]
    leaves_all = leaf_slot.shape[0]
    parents_all = leaves_all // 8
    coords = positions.reshape(3, blocks, LANES)
    charge = charges.reshape(blocks, LANES)
    table = leaf_slot.reshape(leaves_all // LANES, LANES)

    packed, place = block_moments(coords, charge, block_leaf.reshape(1, blocks), table)
    arrived = lax.all_to_all(packed, "dom", split_axis=0, concat_axis=0, tiled=True)
    leaf_moments, parents_part, ids = leaves(arrived, table, padded(m2m_ops))
    source_table, parent_table, near, leaf_keys, leaf_count, coarse_keys, coarse_count, turned_ops = gather(
        leaf_moments,
        parents_part,
        coords,
        charge,
        (item_target, item_source, item_offset),
        (coarse_target, coarse_source, coarse_offset),
        m2l_ops,
    )
    source_table = source_table.reshape(leaves_all, LANES)
    parent_table = parent_table.reshape(parents_all, LANES)
    terms, parent_locals = translate(
        leaf_keys,
        leaf_count,
        coarse_keys,
        coarse_count,
        source_table,
        parent_table,
        turned_ops.reshape(OFFSETS + 1, ROWS, LANES),
    )
    forces, potential = far_field(
        terms, parent_locals, ids, arrived, padded(l2l_ops), coords, charge, place, near
    )
    return forces.reshape(3, blocks * LANES), potential.reshape(blocks * LANES)


def solution(mesh):
    in_specs = (
        P(None, ("dom", "lvl")),
        P(("dom", "lvl")),
        P(("dom", "lvl")),
        P(),
        P(),
        P(),
        P(),
        P("dom", "lvl", None),
        P("dom", "lvl", None),
        P("dom", "lvl", None),
        P("dom", "lvl", None),
        P("dom", "lvl", None),
        P("dom", "lvl", None),
    )
    out_specs = (P(None, ("dom", "lvl")), P(("dom", "lvl")))
    return jax.shard_map(shards, mesh=mesh, in_specs=in_specs, out_specs=out_specs, check_vma=False)
```

```python
import functools
import itertools
import math

import jax
import jax.numpy as jnp
import numpy as np
from jax import lax
from jax.experimental import pallas as pl
from jax.experimental.pallas import tpu as pltpu
from jax.sharding import PartitionSpec as P

COEF = 81
OFFSETS = 316
ROWS = 88
TOP = 8
LANES = 128
LEAF_DEV = 64
CAP = 8
GROUP = 4
SOFTENING = 0.04
HIGH = lax.Precision.HIGHEST
VMEM = pltpu.VMEM
MIB = 1 << 20
MESH = pl.DeviceIdType.MESH


def dot(a, b, contract=((1,), (0,))):
    return lax.dot_general(
        a, b, (contract, ((), ())), precision=HIGH, preferred_element_type=jnp.float32
    )


def row_index(degree, azimuth, imaginary):
    start = degree * degree
    return start if azimuth == 0 else start + 2 * azimuth - 1 + int(imaginary)


def row_weight(degree, azimuth):
    return math.sqrt(math.factorial(degree + azimuth) * math.factorial(degree - azimuth))


def harmonics(x, y, z, emit):
    squared = x * x + y * y + z * z
    diag_re, diag_im = None, None
    for azimuth in range(TOP + 1):
        if azimuth == 1:
            diag_re, diag_im = -0.5 * x, -0.5 * y
        elif azimuth > 1:
            factor = -1.0 / (2.0 * azimuth)
            fx, fy = factor * x, factor * y
            diag_re, diag_im = fx * diag_re - fy * diag_im, fx * diag_im + fy * diag_re
        if azimuth == 0:
            parts = [jnp.ones_like(x)]
        else:
            parts = [diag_re, diag_im]
        for which, value in enumerate(parts):
            lower, upper = None, value
            for degree in range(azimuth, TOP + 1):
                if degree > azimuth:
                    factor = 1.0 / ((degree + azimuth) * (degree - azimuth))
                    if degree == 1 and azimuth == 0:
                        fresh = z
                    elif lower is None:
                        fresh = (factor * (2 * degree - 1)) * z * upper
                    else:
                        fresh = (factor * (2 * degree - 1)) * z * upper - (factor * squared) * lower
                    lower, upper = upper, fresh
                emit(row_index(degree, azimuth, which == 1), degree, upper)


G_ROWS = 96 + 3 * 64


def gradient_matrix():
    out = np.zeros((G_ROWS, LANES), np.float64)

    def add(axis, row, degree, azimuth, value_re, value_im):
        if degree < 0 or azimuth > degree:
            return
        out[96 + 64 * axis + row_index(degree, azimuth, 0), row] += value_re
        if azimuth:
            out[96 + 64 * axis + row_index(degree, azimuth, 1), row] += value_im

    for degree in range(TOP + 1):
        for azimuth in range(degree + 1):
            for imaginary in range(2 if azimuth else 1):
                row = row_index(degree, azimuth, imaginary)
                w = row_weight(degree, azimuth)
                out[row, row] = w
                below = degree - 1
                if imaginary:
                    add(2, row, below, azimuth, 0.0, w)
                    add(0, row, below, azimuth + 1, 0.0, 0.5 * w)
                    add(0, row, below, azimuth - 1, 0.0, -0.5 * w)
                    add(1, row, below, azimuth + 1, -0.5 * w, 0.0)
                    add(1, row, below, azimuth - 1, -0.5 * w, 0.0)
                elif azimuth:
                    add(2, row, below, azimuth, w, 0.0)
                    add(0, row, below, azimuth + 1, 0.5 * w, 0.0)
                    add(0, row, below, azimuth - 1, -0.5 * w, 0.0)
                    add(1, row, below, azimuth + 1, 0.0, 0.5 * w)
                    add(1, row, below, azimuth - 1, 0.0, 0.5 * w)
                else:
                    add(2, row, below, 0, w, 0.0)
                    add(0, row, below, 1, w, 0.0)
                    add(1, row, below, 1, 0.0, w)
    return out.astype(np.float32)


def iota(shape, dim):
    return lax.broadcasted_iota(jnp.int32, shape, dim)


WEIGHTS = [row_weight(l, (row - l * l + 1) // 2) for l in range(TOP + 1) for row in range(l * l, (l + 1) * (l + 1))]


def block_moments(atoms_ref, table, leaf, place_ref, packed_ref, turned, acc, rows):
    blocks = leaf.shape[1]
    high = (iota((64, blocks), 0) == (leaf >> 7)).astype(jnp.float32)
    lines = dot(table.astype(jnp.float32), high, ((0,), (0,)))
    slot = jnp.sum(
        jnp.where(iota((LANES, blocks), 0) == (leaf & 127), lines, 0.0), axis=0, keepdims=True
    ).astype(jnp.int32)
    owner = slot >> 8
    hits = iota((32, blocks), 0) == owner
    earlier = (iota((blocks, blocks), 0) < iota((blocks, blocks), 1)).astype(jnp.float32)
    before = dot(hits.astype(jnp.float32), earlier)
    rank = jnp.sum(jnp.where(hits, before, 0.0), axis=0, keepdims=True).astype(jnp.int32)
    place = owner * CAP + rank
    place_ref[...] = place

    for d in range(4):
        turned[d] = atoms_ref[d].T
    acc[...] = jnp.zeros_like(acc)

    def chunk(i, carry):
        at = pl.ds(pl.multiple_of(i * 32, 32), 32)
        x, y, z, q = (turned[d, at, :] for d in range(4))

        def emit(row, degree, value):
            part = q * value
            acc[row] += (part[0:8] + part[8:16]) + (part[16:24] + part[24:32])

        harmonics(x, y, z, emit)
        return carry

    lax.fori_loop(0, 4, chunk, 0)
    rows[...] = jnp.zeros_like(rows)
    for k in range(COEF):
        rows[k : k + 1, :] = WEIGHTS[k] * jnp.sum(acc[k], axis=0, keepdims=True)
    rows[127:128, :] = ((slot & 63) + 1).astype(jnp.float32)
    spread = (iota((32 * CAP, blocks), 0) == place).astype(jnp.float32)
    packed_ref[...] = dot(spread, rows[...].T).reshape(packed_ref.shape)


def by_octant(values, ops_ref, octant):
    lines = ops_ref.shape[0] * 8
    moved = dot(values[:, :COEF], ops_ref[...].reshape(lines, COEF), ((1,), (1,)))
    moved = jnp.where(iota(moved.shape, 1) & 7 == octant, moved, 0.0)
    fold = (iota((lines, LANES), 0) >> 3 == iota((lines, LANES), 1)).astype(jnp.float32)
    return dot(moved, fold)


def leaf_moments(arrived, table_ref, ops_ref, group, first, part_ref, ids_ref):
    tags = arrived[:, 127:128].astype(jnp.int32)
    member = (iota((arrived.shape[0], LEAF_DEV), 1) + 1 == tags).astype(jnp.float32)
    leaf = dot(member, arrived, ((0,), (0,)))
    leaf = jnp.where(iota(leaf.shape, 1) < COEF, leaf, 0.0)
    slots = first + iota((LEAF_DEV, LANES), 0)
    found = jnp.zeros((LEAF_DEV, LANES), jnp.int32)
    lane = iota((LEAF_DEV, LANES), 1)
    table = table_ref[pl.ds(pl.multiple_of(group * 16, 16), 16), :]
    for h in range(16):
        number = (group * 16 + h) * 128 + lane
        found = found + jnp.where(table[h : h + 1, :] == slots, number, 0)
    ids = jnp.sum(found.astype(jnp.float32), axis=1, keepdims=True).astype(jnp.int32)
    ids_ref[...] = jnp.broadcast_to(ids, (LEAF_DEV, LANES))
    children = by_octant(leaf, ops_ref, ids & 7)
    within = (ids >> 3) - group * 256
    picks = (iota((LEAF_DEV, 256), 1) == within).astype(jnp.float32)
    part_ref[...] = dot(picks, children, ((0,), (0,))).reshape(part_ref.shape)
    return leaf


def bitonic_stages(size):
    out, span = [], 2
    while span <= size:
        step = span // 2
        while step >= 1:
            out.append((span, step))
            step //= 2
        span *= 2
    return out


def bitonic_stage(x, span, step):
    rows = x.shape[0]
    index = iota(x.shape, 0) * LANES + iota(x.shape, 1)
    axis, shift, extent = (1, step, LANES) if step < LANES else (0, step // LANES, rows)
    second = (index & step) != 0
    other = jnp.where(second, pltpu.roll(x, shift, axis), pltpu.roll(x, extent - shift, axis))
    take_small = ((index & span) == 0) != second
    return jnp.where(take_small, jnp.minimum(x, other), jnp.maximum(x, other))


def write_keys(items, targets, sources, keys_ref, count_ref):
    target_ref, source_ref, offset_ref = items
    rows = target_ref.shape[0]
    none = ((sources - 1) << 9) | OFFSETS
    keys_ref[...] = jnp.full(keys_ref.shape, ((targets - 1) << 23) | none, jnp.int32)
    keys_ref[0:rows, :] = (target_ref[...] << 23) | (source_ref[...] << 9) | offset_ref[...]
    numbers = iota((targets, LANES), 0)
    count = jnp.zeros((targets, LANES), jnp.float32)
    for r in range(rows):
        count = count + (numbers == target_ref[r : r + 1, :]).astype(jnp.float32)
    count = jnp.sum(count, axis=1, keepdims=True)
    fours = jnp.zeros((1, 1), jnp.int32)
    for p in range((targets + LANES - 1) // LANES):
        size = min(LANES, targets - p * LANES)
        part = count[p * LANES : p * LANES + size]
        diagonal = iota((size, LANES), 0) == iota((size, LANES), 1)
        line = jnp.sum(jnp.where(diagonal, part, 0.0), axis=0, keepdims=True).astype(jnp.int32)
        filled = (line + 3) >> 2
        fours = fours + jnp.sum(filled.astype(jnp.float32), axis=1, keepdims=True).astype(jnp.int32)
        own = iota((1, LANES), 1) + p * LANES
        for turn in range(3):
            goal = jnp.where(turn < filled * 4 - line, own, targets - 1)
            at = rows + 3 * p + turn
            keys_ref[at : at + 1, :] = (goal << 23) | none
    count_ref[...] = jnp.broadcast_to(fours, count_ref.shape)


def translate_kernel(leaf_keys, leaf_count, coarse_keys, coarse_count, leaf_src, coarse_src, ops, leaf_out, coarse_out, acc):
    def work(keys, count, src, out):
        targets = out.shape[0]

        def clear(t, carry):
            for u in range(4):
                acc[t * 4 + u] = jnp.zeros(acc.shape[1:], jnp.float32)
            return carry

        lax.fori_loop(0, targets // 4, clear, 0)

        def term(key):
            row = src[pl.ds((key >> 9) & (src.shape[0] - 1), 1), :][:, :COEF]
            return ops[key & 511, :COEF, :COEF] * row

        def step(i, carry):
            for u in range(4):
                four = [keys[i * 16 + u * 4 + n] for n in range(4)]
                total = (term(four[0]) + term(four[1])) + (term(four[2]) + term(four[3]))
                acc[four[0] >> 23, :COEF, :COEF] += total
            return carry

        lax.fori_loop(0, (count[0, 0] + 3) // 4, step, 0)
        lane = iota((ROWS, LANES), 1)
        for low in range(0, targets, LANES):
            size = min(LANES, targets - low)

            def finish(i, columns):
                for u in range(8):
                    t = i * 8 + u
                    columns = jnp.where(lane == t, jnp.sum(acc[low + t], axis=1, keepdims=True), columns)
                return columns

            columns = lax.fori_loop(0, size // 8, finish, jnp.zeros((ROWS, LANES), jnp.float32))
            padded = jnp.concatenate([columns, jnp.zeros((LANES - ROWS, LANES), jnp.float32)], axis=0)
            out[low : low + size, :] = padded.T[:size]

    work(coarse_keys, coarse_count, coarse_src, coarse_out)
    work(leaf_keys, leaf_count, leaf_src, leaf_out)


def translate(leaf_keys, leaf_count, coarse_keys, coarse_count, leaf_table, coarse_table, ops):
    smem = pl.BlockSpec(memory_space=pltpu.SMEM)
    whole = pl.BlockSpec(memory_space=VMEM)
    return pl.pallas_call(
        translate_kernel,
        out_shape=(
            jax.ShapeDtypeStruct((4 * LEAF_DEV, LANES), jnp.float32),
            jax.ShapeDtypeStruct((LEAF_DEV, LANES), jnp.float32),
        ),
        in_specs=[smem] * 4 + [whole] * 3,
        out_specs=(whole, whole),
        scratch_shapes=[VMEM((4 * LEAF_DEV, ROWS, LANES), jnp.float32)],
        compiler_params=pltpu.CompilerParams(vmem_limit_bytes=36 * MIB),
        name="translate",
    )(leaf_keys.reshape(-1), leaf_count, coarse_keys.reshape(-1), coarse_count, leaf_table, coarse_table, ops)


def near_groups(pos_ref, q_ref, out_ref, low, high):
    def group(g, carry):
        at = pl.ds(pl.multiple_of(g * 8, 8), 8)
        rows = [pos_ref[d, at, :] for d in range(3)] + [q_ref[at, :]]
        columns = [r.T for r in rows]
        for b in range(8):
            xj, yj, zj, qj = (r[b : b + 1, :] for r in rows)
            xi, yi, zi, qi = (c[:, b : b + 1] for c in columns)
            sums = [jnp.zeros((8, LANES), jnp.float32) for _ in range(4)]
            for c in range(4):
                part = slice(c * 32, c * 32 + 32)
                dx = xj - xi[part]
                dy = yj - yi[part]
                dz = zj - zi[part]
                inverse = lax.rsqrt(dx * dx + dy * dy + dz * dz + SOFTENING)
                same = iota((32, LANES), 0) + c * 32 == iota((32, LANES), 1)
                weighted = jnp.where(same, 0.0, inverse * qi[part])
                strength = weighted * (inverse * inverse)
                for n, term in enumerate((strength * dx, strength * dy, strength * dz, weighted)):
                    sums[n] = sums[n] + ((term[0:8] + term[8:16]) + (term[16:24] + term[24:32]))
            for n in range(4):
                line = jnp.sum(sums[n], axis=0, keepdims=True)
                if n < 3:
                    line = line * qj
                out_ref[n, pl.ds(g * 8 + b, 1), :] = line
        return carry

    lax.fori_loop(low, high, group, 0)


PARTS = ((0, 16, 24, (2, 0, 1)), (24, 32, 48, (0, 1, 2)), (48, 56, 64, (1, 2, 0)))
COPIES = 68
SLABS = 9


def gather_kernel(
    atoms_ref, whole_ref, m2m_ref, m2l_hbm,
    all_ref, parent_ref, near_ref, lkeys_ref, lcount_ref, ckeys_ref, ccount_ref, m2l_ref, arrived_ref, place_ref, ids_ref,
    packed, turned, acc, rows, part_ref, got_c, got_x, got_y, sum_c, sum_x, slabs, send_sem, recv_sem, slab_sem, out_sem, in_sem
):
    dom, lvl = lax.axis_index("dom"), lax.axis_index("lvl")
    here = (dom // 8, (dom // 2) % 4, lvl)
    core = dom % 2
    table_ref = whole_ref.at[0:64]
    leaf_items = [whole_ref.at[64 + 32 * n : 96 + 32 * n] for n in range(3)]
    coarse_items = [whole_ref.at[160 + 16 * n : 176 + 16 * n] for n in range(3)]

    def device(place, which):
        return ((place[0] * 4 + place[1]) * 2 + which, place[2])

    def moved(axis, by):
        return tuple((v + by) % 4 if n == axis else v for n, v in enumerate(here))

    def slab(g, slot):
        return pltpu.make_async_copy(m2l_hbm.at[pl.ds(g * SLABS, SLABS)], slabs.at[slot], slab_sem.at[slot])

    twin = device(here, 1 - core)
    m2l_ref[OFFSETS * ROWS :, :] = jnp.zeros((ROWS, LANES), jnp.float32)
    slab(0, 0).start()
    barrier = pltpu.get_barrier_semaphore()

    def greet(d, carry):
        pl.semaphore_signal(barrier, inc=1, device_id=((dom + d) % 32, lvl), device_id_type=MESH)
        return carry

    lax.fori_loop(1, 32, greet, 0)
    for by in (1, 2, 3):
        pl.semaphore_signal(barrier, inc=1, device_id=(dom, (lvl + by) % 4), device_id_type=MESH)
    block_moments(atoms_ref, table_ref[...], whole_ref[208:209, :], place_ref, packed, turned, acc, rows)
    pl.semaphore_wait(barrier, 34)

    started = []

    def send(source, target, where):
        n = len(started)
        copy = pltpu.make_async_remote_copy(
            src_ref=source,
            dst_ref=target,
            send_sem=send_sem.at[n],
            recv_sem=recv_sem.at[n],
            device_id=where,
            device_id_type=MESH,
        )
        copy.start()
        started.append(copy)
        return copy

    def block(done, axis, by, low, high):
        y, x, z = (
            slice(None) if n in done else ((here[n] + by) % 4 if n == axis else here[n]) for n in range(3)
        )
        return all_ref.at[y, x, core, z, slice(low, high)]

    def put(ref, where):
        return send(ref, ref, where)

    def parents(done):
        y, x, z = (slice(None) if n in done else here[n] for n in range(3))
        return parent_ref.at[z, y, x, core]

    waiting = {}

    def stage(n):
        if n == 0:
            waiting["p"] = [send(part_ref.at[:, :, 1 - core], got_c, twin)]
            return
        for copy in waiting["p"]:
            copy.wait_recv()
        if n == 1:
            sum_c[...] = part_ref[:, :, core] + got_c[...]
            waiting["p"] = [
                send(sum_c.at[:, (here[1] + by) % 4], got_x.at[by - 1], device(moved(1, by), core)) for by in (1, 2, 3)
            ]
        elif n == 2:
            sum_x[...] = (sum_c[:, here[1]] + got_x[0]) + (got_x[1] + got_x[2])
            waiting["p"] = [
                send(sum_x.at[(here[0] + by) % 4], got_y.at[by - 1], device(moved(0, by), core)) for by in (1, 2, 3)
            ]
        elif n == 3:
            parent_ref[here[2], here[0], here[1], core] = (sum_x[here[0]] + got_y[0]) + (got_y[1] + got_y[2])
            waiting["p"] = [put(parents(()), device(moved(2, by), core)) for by in (1, 2, 3)]
        elif n == 4:
            waiting["p"] = [put(parents((2,)), device(moved(0, by), core)) for by in (1, 2, 3)]
        elif n == 5:
            waiting["p"] = [put(parents((2, 0)), device(moved(1, by), core)) for by in (1, 2, 3)]
        elif n == 6:
            waiting["p"] = [put(parents((2, 0, 1)), twin)]

    sorts = [
        (keys, stage)
        for pair in itertools.zip_longest(
            *([(keys, stage) for stage in bitonic_stages(keys.shape[0] * LANES)] for keys in (lkeys_ref, ckeys_ref))
        )
        for keys, stage in filter(None, pair)
    ]

    def sort(low, high):
        now = {}
        for keys, stage in sorts[low:high]:
            name = id(keys)
            if name not in now:
                now[name] = (keys, keys[...])
            now[name] = (keys, bitonic_stage(now[name][1], *stage))
        for keys, value in now.values():
            keys[...] = value

    def turn(low, high):
        def group(g, carry):
            slot = g % 2

            @pl.when(g < COEF // SLABS - 1)
            def _():
                slab(g + 1, 1 - slot).start()

            slab(g, slot).wait()
            for u in range(SLABS):
                for p in range(3):
                    wide = min(LANES, OFFSETS - p * LANES)
                    lines = slabs[slot, u, :, p * LANES : p * LANES + wide].T
                    start = p * LANES * ROWS + g * SLABS + u
                    even = wide // 8 * 8
                    m2l_ref[pl.ds(start, even, stride=ROWS), 0:COEF] = lines[:even]
                    if even < wide:
                        m2l_ref[pl.ds(start + even * ROWS, wide - even, stride=ROWS), 0:COEF] = lines[even:]
            return carry

        lax.fori_loop(low, high, group, 0)

    def fill(n):
        if n < 3:
            sort(60 * n, 60 * n + 60)
        turn(*((0, 0), (0, 0), (0, 0), (0, 4), (4, 7), (7, 9), (9, 9), (9, 9))[n])
        near_groups(atoms_ref, atoms_ref.at[3], near_ref, *((0, 0), (0, 0), (0, 0), (0, 0), (0, 0), (0, 2), (2, 6), (6, 16))[n])

    def message(d):
        goal = (dom + d) % 32
        return pltpu.make_async_remote_copy(
            src_ref=packed.at[goal],
            dst_ref=arrived_ref.at[dom],
            send_sem=out_sem.at[d],
            recv_sem=in_sem.at[d],
            device_id=(goal, lvl),
            device_id_type=MESH,
        )

    def each(act):
        def one(d, carry):
            act(message(d))
            return carry

        lax.fori_loop(1, 32, one, 0)

    each(lambda copy: copy.start())
    arrived_ref[dom] = packed[dom]
    write_keys(leaf_items, 4 * LEAF_DEV, 8192, lkeys_ref, lcount_ref)
    write_keys(coarse_items, LEAF_DEV, 1024, ckeys_ref, ccount_ref)
    fill(0)
    each(lambda copy: copy.wait_recv())
    all_ref[here[0], here[1], core, here[2]] = leaf_moments(
        arrived_ref[...].reshape(32 * CAP, LANES), table_ref, m2m_ref, lvl, (dom * GROUP + lvl) * LEAF_DEV, part_ref, ids_ref
    )

    last = []
    for phase in range(2):
        direct = []
        for low, middle, high, order in PARTS:
            axis, done = order[phase], order[:phase]
            direct.append([put(block(done, axis, 0, low, high), device(moved(axis, by), core)) for by in (1, 3, 2)])
        stage(phase)
        fill(phase + 1)
        for (low, middle, high, order), copies in zip(PARTS, direct):
            axis, done = order[phase], order[:phase]
            for by, copy in zip((3, 1, 2), copies):
                copy.wait_recv()
                if phase:
                    last.append(put(block(done, axis, by, low, high), twin))
            if not phase:
                last.append(put(block((axis,), axis, 0, low, high), twin))
    first, second = [], []
    for low, middle, high, order in PARTS:
        axis, done = order[2], order[:2]
        first.append([put(block(done, axis, 0, low, high), device(moved(axis, by), core)) for by in (1, 3)])
    stage(2)
    fill(3)
    for (low, middle, high, order), (right, left) in zip(PARTS, first):
        axis, done = order[2], order[:2]
        right.wait_recv()
        a = put(block(done, axis, 3, low, middle), device(moved(axis, 1), core))
        left.wait_recv()
        b = put(block(done, axis, 1, middle, high), device(moved(axis, 3), core))
        second.append((a, b))
        last.append(put(block(done, axis, 3, low, high), twin))
        last.append(put(block(done, axis, 1, low, high), twin))
    stage(3)
    fill(4)
    for (low, middle, high, order), pair in zip(PARTS, second):
        axis, done = order[2], order[:2]
        for copy in pair:
            copy.wait_recv()
        last.append(put(block(done, axis, 2, low, high), twin))
    stage(4)
    fill(5)
    stage(5)
    fill(6)
    stage(6)
    fill(7)
    for copy in last:
        copy.wait_recv()
    for copy in waiting["p"]:
        copy.wait_recv()
    for copy in started:
        copy.wait_send()
    each(lambda copy: copy.wait_send())
    assert len(started) == COPIES


def gather(atoms, integers, m2m_ops, m2l_ops):
    whole = pl.BlockSpec(memory_space=VMEM)
    f32, i32 = jnp.float32, jnp.int32
    blocks = atoms.shape[1]
    return pl.pallas_call(
        gather_kernel,
        out_shape=(
            jax.ShapeDtypeStruct((4, 4, 2, 4, LEAF_DEV, LANES), f32),
            jax.ShapeDtypeStruct((4, 4, 4, 2, 8, LANES), f32),
            jax.ShapeDtypeStruct(atoms.shape, f32),
            jax.ShapeDtypeStruct((64, LANES), i32),
            jax.ShapeDtypeStruct((1, LANES), i32),
            jax.ShapeDtypeStruct((32, LANES), i32),
            jax.ShapeDtypeStruct((1, LANES), i32),
            jax.ShapeDtypeStruct(((OFFSETS + 1) * ROWS, LANES), f32),
            jax.ShapeDtypeStruct((32, CAP, LANES), f32),
            jax.ShapeDtypeStruct((1, blocks), i32),
            jax.ShapeDtypeStruct((LEAF_DEV, LANES), i32),
        ),
        in_specs=[whole] * 3 + [pl.BlockSpec(memory_space=pl.ANY)],
        out_specs=(whole,) * 11,
        scratch_shapes=[
            VMEM((32, CAP, LANES), f32),
            VMEM((4, LANES, blocks), f32),
            VMEM((COEF, 8, blocks), f32),
            VMEM((LANES, blocks), f32),
            VMEM((4, 4, 2, 8, LANES), f32),
            VMEM((4, 4, 8, LANES), f32),
            VMEM((3, 4, 8, LANES), f32),
            VMEM((3, 8, LANES), f32),
            VMEM((4, 4, 8, LANES), f32),
            VMEM((4, 8, LANES), f32),
            VMEM((2, SLABS, COEF, OFFSETS), f32),
            pltpu.SemaphoreType.DMA((COPIES,)),
            pltpu.SemaphoreType.DMA((COPIES,)),
            pltpu.SemaphoreType.DMA((2,)),
            pltpu.SemaphoreType.DMA((32,)),
            pltpu.SemaphoreType.DMA((32,)),
        ],
        compiler_params=pltpu.CompilerParams(collective_id=0, has_side_effects=True, vmem_limit_bytes=42 * MIB),
        name="gather",
    )(atoms, integers, m2m_ops.transpose(1, 0, 2), m2l_ops.transpose(1, 2, 0))


def far_kernel(
    terms_ref, parent_ref, ids_ref, arrived_ref, ops_ref, atoms_ref, place_ref, near_ref, matrix_ref,
    force_ref, phi_ref, basis, got, sent, returned, turned, lines, send_sem, recv_sem
):
    dom, lvl = lax.axis_index("dom"), lax.axis_index("lvl")
    blocks = atoms_ref.shape[1]
    barrier = pltpu.get_barrier_semaphore()

    def greet(d, carry):
        pl.semaphore_signal(barrier, inc=1, device_id=((dom + d) % 32, lvl), device_id_type=MESH)
        return carry

    for by in (1, 2, 3):
        pl.semaphore_signal(barrier, inc=1, device_id=(dom, (lvl + by) % 4), device_id_type=MESH)
    lax.fori_loop(1, 32, greet, 0)
    for d in range(3):
        turned[d] = atoms_ref[d].T
    shifted = by_octant(parent_ref[...], ops_ref, ids_ref[...][:, 0:1] & 7)
    pl.semaphore_wait(barrier, 34)

    shared = []
    for by in (1, 2, 3):
        goal = (lvl + by) % 4
        copy = pltpu.make_async_remote_copy(
            src_ref=terms_ref.at[goal],
            dst_ref=got.at[by - 1],
            send_sem=send_sem.at[31 + by],
            recv_sem=recv_sem.at[31 + by],
            device_id=(dom, goal),
            device_id_type=MESH,
        )
        copy.start()
        shared.append(copy)

    total = shifted + terms_ref[lvl]

    def prepare(i, carry):
        at = pl.ds(pl.multiple_of(i * 32, 32), 32)

        def emit(row, degree, value):
            basis[row, at, :] = value

        harmonics(turned[0, at, :], turned[1, at, :], turned[2, at, :], emit)
        return carry

    lax.fori_loop(0, 2, prepare, 0)
    tags = arrived_ref[...].reshape(32 * CAP, LANES)[:, 127:128].astype(jnp.int32)
    member = (iota((32 * CAP, LEAF_DEV), 1) + 1 == tags).astype(jnp.float32)
    for copy in shared:
        copy.wait_recv()
    total = (total + got[0]) + (got[1] + got[2])
    sent[...] = dot(member, total).reshape(sent.shape)

    def message(d):
        goal = (dom + d) % 32
        return pltpu.make_async_remote_copy(
            src_ref=sent.at[goal],
            dst_ref=returned.at[dom],
            send_sem=send_sem.at[d],
            recv_sem=recv_sem.at[d],
            device_id=(goal, lvl),
            device_id_type=MESH,
        )

    def start(d, carry):
        message(d).start()
        return carry

    lax.fori_loop(1, 32, start, 0)
    returned[dom] = sent[dom]
    lax.fori_loop(2, 4, prepare, 0)
    spread = (iota((32 * CAP, blocks), 0) == place_ref[...]).astype(jnp.float32)

    def receive(d, carry):
        message(d).wait_recv()
        return carry

    lax.fori_loop(1, 32, receive, 0)
    columns = dot(returned[...].reshape(32 * CAP, LANES), spread, ((0,), (0,)))
    lines[...] = dot(matrix_ref[...], columns)

    def chunk(i, carry):
        at = pl.ds(pl.multiple_of(i * 32, 32), 32)
        sums = [None] * 4
        for row in range(COEF):
            value = basis[row, at, :]
            starts = [(3, 0)] + ([(d, 96 + 64 * d) for d in range(3)] if row < TOP * TOP else [])
            for n, start in starts:
                term = lines[start + row : start + row + 1, :] * value
                sums[n] = term if sums[n] is None else sums[n] + term
        for n in range(4):
            turned[n, at, :] = sums[n]
        return carry

    lax.fori_loop(0, 4, chunk, 0)
    charge = atoms_ref[3]
    for d in range(3):
        force_ref[d] = near_ref[d] - charge * turned[d].T
    phi_ref[...] = near_ref[3] + turned[3].T

    def leave(d, carry):
        message(d).wait_send()
        return carry

    lax.fori_loop(1, 32, leave, 0)
    for copy in shared:
        copy.wait_send()


def far_field(terms, parent_locals, ids, arrived, l2l_ops, atoms, place, near):
    whole = pl.BlockSpec(memory_space=VMEM)
    f32 = jnp.float32
    return pl.pallas_call(
        far_kernel,
        out_shape=(
            jax.ShapeDtypeStruct((3,) + atoms.shape[1:], f32),
            jax.ShapeDtypeStruct(atoms.shape[1:], f32),
        ),
        in_specs=[whole] * 9,
        out_specs=(whole, whole),
        scratch_shapes=[
            VMEM((COEF,) + atoms.shape[1:], f32),
            VMEM((3, LEAF_DEV, LANES), f32),
            VMEM((32, CAP, LANES), f32),
            VMEM((32, CAP, LANES), f32),
            VMEM(atoms.shape, f32),
            VMEM((G_ROWS, LANES), f32),
            pltpu.SemaphoreType.DMA((35,)),
            pltpu.SemaphoreType.DMA((35,)),
        ],
        compiler_params=pltpu.CompilerParams(collective_id=1, has_side_effects=True, vmem_limit_bytes=20 * MIB),
        name="far_field",
    )(
        terms.reshape(GROUP, LEAF_DEV, LANES), parent_locals, ids, arrived, l2l_ops.transpose(1, 0, 2), atoms, place, near,
        jnp.asarray(gradient_matrix()),
    )


def shards(
    positions,
    charges,
    block_leaf,
    leaf_slot,
    m2m_ops,
    l2l_ops,
    m2l_ops,
    item_target,
    item_source,
    item_offset,
    coarse_target,
    coarse_source,
    coarse_offset,
):
    blocks = block_leaf.shape[0]
    leaves_all = leaf_slot.shape[0]
    parents_all = leaves_all // 8
    atoms = jnp.concatenate([positions.reshape(3, blocks, LANES), charges.reshape(1, blocks, LANES)])
    integers = [leaf_slot, item_target, item_source, item_offset, coarse_target, coarse_source, coarse_offset, block_leaf]
    integers = jnp.concatenate([a.reshape(-1, LANES) for a in integers])
    (
        source_table, parent_table, near, leaf_keys, leaf_count, coarse_keys, coarse_count, turned_ops, arrived, place, ids
    ) = gather(atoms, integers, m2m_ops, m2l_ops)
    source_table = source_table.reshape(leaves_all, LANES)
    parent_table = parent_table.reshape(parents_all, LANES)
    terms, parent_locals = translate(
        leaf_keys,
        leaf_count,
        coarse_keys,
        coarse_count,
        source_table,
        parent_table,
        turned_ops.reshape(OFFSETS + 1, ROWS, LANES),
    )
    forces, potential = far_field(terms, parent_locals, ids, arrived, l2l_ops, atoms, place, near)
    return forces.reshape(3, blocks * LANES), potential.reshape(blocks * LANES)


def solution(mesh):
    in_specs = (
        P(None, ("dom", "lvl")),
        P(("dom", "lvl")),
        P(("dom", "lvl")),
        P(),
        P(),
        P(),
        P(),
        P("dom", "lvl", None),
        P("dom", "lvl", None),
        P("dom", "lvl", None),
        P("dom", "lvl", None),
        P("dom", "lvl", None),
        P("dom", "lvl", None),
    )
    out_specs = (P(None, ("dom", "lvl")), P(("dom", "lvl")))
    return jax.shard_map(shards, mesh=mesh, in_specs=in_specs, out_specs=out_specs, check_vma=False)
```

```python
import functools
import itertools
import math

import jax
import jax.numpy as jnp
import numpy as np
from jax import lax
from jax.experimental import pallas as pl
from jax.experimental.pallas import tpu as pltpu
from jax.sharding import PartitionSpec as P

COEF = 81
OFFSETS = 316
ROWS = 88
TOP = 8
LANES = 128
LEAF_DEV = 64
CAP = 8
GROUP = 4
SOFTENING = 0.04
HIGH = lax.Precision.HIGHEST
VMEM = pltpu.VMEM
MIB = 1 << 20
MESH = pl.DeviceIdType.MESH


def dot(a, b, contract=((1,), (0,))):
    return lax.dot_general(
        a, b, (contract, ((), ())), precision=HIGH, preferred_element_type=jnp.float32
    )


def row_index(degree, azimuth, imaginary):
    start = degree * degree
    return start if azimuth == 0 else start + 2 * azimuth - 1 + int(imaginary)


def row_weight(degree, azimuth):
    return math.sqrt(math.factorial(degree + azimuth) * math.factorial(degree - azimuth))


def harmonics(x, y, z, emit):
    squared = x * x + y * y + z * z
    diag_re, diag_im = None, None
    for azimuth in range(TOP + 1):
        if azimuth == 1:
            diag_re, diag_im = -0.5 * x, -0.5 * y
        elif azimuth > 1:
            factor = -1.0 / (2.0 * azimuth)
            fx, fy = factor * x, factor * y
            diag_re, diag_im = fx * diag_re - fy * diag_im, fx * diag_im + fy * diag_re
        if azimuth == 0:
            parts = [jnp.ones_like(x)]
        else:
            parts = [diag_re, diag_im]
        for which, value in enumerate(parts):
            lower, upper = None, value
            for degree in range(azimuth, TOP + 1):
                if degree > azimuth:
                    factor = 1.0 / ((degree + azimuth) * (degree - azimuth))
                    if degree == 1 and azimuth == 0:
                        fresh = z
                    elif lower is None:
                        fresh = (factor * (2 * degree - 1)) * z * upper
                    else:
                        fresh = (factor * (2 * degree - 1)) * z * upper - (factor * squared) * lower
                    lower, upper = upper, fresh
                emit(row_index(degree, azimuth, which == 1), degree, upper)


G_ROWS = 96 + 3 * 64


def gradient_matrix():
    out = np.zeros((G_ROWS, LANES), np.float64)

    def add(axis, row, degree, azimuth, value_re, value_im):
        if degree < 0 or azimuth > degree:
            return
        out[96 + 64 * axis + row_index(degree, azimuth, 0), row] += value_re
        if azimuth:
            out[96 + 64 * axis + row_index(degree, azimuth, 1), row] += value_im

    for degree in range(TOP + 1):
        for azimuth in range(degree + 1):
            for imaginary in range(2 if azimuth else 1):
                row = row_index(degree, azimuth, imaginary)
                w = row_weight(degree, azimuth)
                out[row, row] = w
                below = degree - 1
                if imaginary:
                    add(2, row, below, azimuth, 0.0, w)
                    add(0, row, below, azimuth + 1, 0.0, 0.5 * w)
                    add(0, row, below, azimuth - 1, 0.0, -0.5 * w)
                    add(1, row, below, azimuth + 1, -0.5 * w, 0.0)
                    add(1, row, below, azimuth - 1, -0.5 * w, 0.0)
                elif azimuth:
                    add(2, row, below, azimuth, w, 0.0)
                    add(0, row, below, azimuth + 1, 0.5 * w, 0.0)
                    add(0, row, below, azimuth - 1, -0.5 * w, 0.0)
                    add(1, row, below, azimuth + 1, 0.0, 0.5 * w)
                    add(1, row, below, azimuth - 1, 0.0, 0.5 * w)
                else:
                    add(2, row, below, 0, w, 0.0)
                    add(0, row, below, 1, w, 0.0)
                    add(1, row, below, 1, 0.0, w)
    return out.astype(np.float32)


def iota(shape, dim):
    return lax.broadcasted_iota(jnp.int32, shape, dim)


WEIGHTS = [row_weight(l, (row - l * l + 1) // 2) for l in range(TOP + 1) for row in range(l * l, (l + 1) * (l + 1))]


def block_moments(atoms_ref, table, leaf, place_ref, packed_ref, turned, acc, rows):
    blocks = leaf.shape[1]
    high = (iota((64, blocks), 0) == (leaf >> 7)).astype(jnp.float32)
    lines = dot(table.astype(jnp.float32), high, ((0,), (0,)))
    slot = jnp.sum(
        jnp.where(iota((LANES, blocks), 0) == (leaf & 127), lines, 0.0), axis=0, keepdims=True
    ).astype(jnp.int32)
    owner = slot >> 8
    hits = iota((32, blocks), 0) == owner
    earlier = (iota((blocks, blocks), 0) < iota((blocks, blocks), 1)).astype(jnp.float32)
    before = dot(hits.astype(jnp.float32), earlier)
    rank = jnp.sum(jnp.where(hits, before, 0.0), axis=0, keepdims=True).astype(jnp.int32)
    place = owner * CAP + rank
    place_ref[...] = place

    for d in range(4):
        turned[d] = atoms_ref[d].T
    acc[...] = jnp.zeros_like(acc)

    def chunk(i, carry):
        at = pl.ds(pl.multiple_of(i * 32, 32), 32)
        x, y, z, q = (turned[d, at, :] for d in range(4))

        def emit(row, degree, value):
            part = q * value
            acc[row] += (part[0:8] + part[8:16]) + (part[16:24] + part[24:32])

        harmonics(x, y, z, emit)
        return carry

    lax.fori_loop(0, 4, chunk, 0)
    rows[...] = jnp.zeros_like(rows)
    for k in range(COEF):
        rows[k : k + 1, :] = WEIGHTS[k] * jnp.sum(acc[k], axis=0, keepdims=True)
    rows[127:128, :] = ((slot & 63) + 1).astype(jnp.float32)
    spread = (iota((32 * CAP, blocks), 0) == place).astype(jnp.float32)
    packed_ref[...] = dot(spread, rows[...].T).reshape(packed_ref.shape)


def by_octant(values, ops_ref, octant):
    lines = ops_ref.shape[0] * 8
    moved = dot(values[:, :COEF], ops_ref[...].reshape(lines, COEF), ((1,), (1,)))
    moved = jnp.where(iota(moved.shape, 1) & 7 == octant, moved, 0.0)
    fold = (iota((lines, LANES), 0) >> 3 == iota((lines, LANES), 1)).astype(jnp.float32)
    return dot(moved, fold)


def leaf_moments(arrived, table_ref, ops_ref, group, first, part_ref, ids_ref):
    tags = arrived[:, 127:128].astype(jnp.int32)
    member = (iota((arrived.shape[0], LEAF_DEV), 1) + 1 == tags).astype(jnp.float32)
    leaf = dot(member, arrived, ((0,), (0,)))
    leaf = jnp.where(iota(leaf.shape, 1) < COEF, leaf, 0.0)
    slots = first + iota((LEAF_DEV, LANES), 0)
    found = jnp.zeros((LEAF_DEV, LANES), jnp.int32)
    lane = iota((LEAF_DEV, LANES), 1)
    table = table_ref[pl.ds(pl.multiple_of(group * 16, 16), 16), :]
    for h in range(16):
        number = (group * 16 + h) * 128 + lane
        found = found + jnp.where(table[h : h + 1, :] == slots, number, 0)
    ids = jnp.sum(found.astype(jnp.float32), axis=1, keepdims=True).astype(jnp.int32)
    ids_ref[...] = jnp.broadcast_to(ids, (LEAF_DEV, LANES))
    children = by_octant(leaf, ops_ref, ids & 7)
    within = (ids >> 3) - group * 256
    picks = (iota((LEAF_DEV, 256), 1) == within).astype(jnp.float32)
    part_ref[...] = dot(picks, children, ((0,), (0,))).reshape(part_ref.shape)
    return leaf


def bitonic_stages(size):
    out, span = [], 2
    while span <= size:
        step = span // 2
        while step >= 1:
            out.append((span, step))
            step //= 2
        span *= 2
    return out


def bitonic_stage(x, span, step):
    rows = x.shape[0]
    index = iota(x.shape, 0) * LANES + iota(x.shape, 1)
    axis, shift, extent = (1, step, LANES) if step < LANES else (0, step // LANES, rows)
    second = (index & step) != 0
    other = jnp.where(second, pltpu.roll(x, shift, axis), pltpu.roll(x, extent - shift, axis))
    take_small = ((index & span) == 0) != second
    return jnp.where(take_small, jnp.minimum(x, other), jnp.maximum(x, other))


def write_keys(items, targets, sources, keys_ref, count_ref):
    target_ref, source_ref, offset_ref = items
    rows = target_ref.shape[0]
    none = ((sources - 1) << 9) | OFFSETS
    keys_ref[...] = jnp.full(keys_ref.shape, ((targets - 1) << 23) | none, jnp.int32)
    keys_ref[0:rows, :] = (target_ref[...] << 23) | (source_ref[...] << 9) | offset_ref[...]
    numbers = iota((targets, LANES), 0)
    count = jnp.zeros((targets, LANES), jnp.float32)
    for r in range(rows):
        count = count + (numbers == target_ref[r : r + 1, :]).astype(jnp.float32)
    count = jnp.sum(count, axis=1, keepdims=True)
    fours = jnp.zeros((1, 1), jnp.int32)
    for p in range((targets + LANES - 1) // LANES):
        size = min(LANES, targets - p * LANES)
        part = count[p * LANES : p * LANES + size]
        diagonal = iota((size, LANES), 0) == iota((size, LANES), 1)
        line = jnp.sum(jnp.where(diagonal, part, 0.0), axis=0, keepdims=True).astype(jnp.int32)
        filled = (line + 3) >> 2
        fours = fours + jnp.sum(filled.astype(jnp.float32), axis=1, keepdims=True).astype(jnp.int32)
        own = iota((1, LANES), 1) + p * LANES
        for turn in range(3):
            goal = jnp.where(turn < filled * 4 - line, own, targets - 1)
            at = rows + 3 * p + turn
            keys_ref[at : at + 1, :] = (goal << 23) | none
    count_ref[...] = jnp.broadcast_to(fours, count_ref.shape)


def translate_kernel(
    leaf_list, leaf_count, coarse_list, coarse_count, leaf_src, coarse_src, ops, leaf_out, coarse_out, acc, leaf_keys, coarse_keys, sems
):
    loads = [
        pltpu.make_async_copy(listing.at[pl.ds(0, keys.shape[0])], keys, sems.at[n])
        for n, (listing, keys) in enumerate(((coarse_list, coarse_keys), (leaf_list, leaf_keys)))
    ]
    for load in loads:
        load.start()

    def work(load, keys, count, src, out):
        targets = out.shape[0]

        def clear(t, carry):
            for u in range(4):
                acc[t * 4 + u] = jnp.zeros(acc.shape[1:], jnp.float32)
            return carry

        lax.fori_loop(0, targets // 4, clear, 0)
        load.wait()

        def term(key):
            row = src[pl.ds((key >> 9) & (src.shape[0] - 1), 1), :][:, :COEF]
            return ops[key & 511, :COEF, :COEF] * row

        def step(i, carry):
            for u in range(4):
                four = [keys[i * 16 + u * 4 + n] for n in range(4)]
                total = (term(four[0]) + term(four[1])) + (term(four[2]) + term(four[3]))
                acc[four[0] >> 23, :COEF, :COEF] += total
            return carry

        lax.fori_loop(0, (count[0, 0] + 3) // 4, step, 0)
        lane = iota((ROWS, LANES), 1)
        for low in range(0, targets, LANES):
            size = min(LANES, targets - low)

            def finish(i, columns):
                for u in range(8):
                    t = i * 8 + u
                    columns = jnp.where(lane == t, jnp.sum(acc[low + t], axis=1, keepdims=True), columns)
                return columns

            columns = lax.fori_loop(0, size // 8, finish, jnp.zeros((ROWS, LANES), jnp.float32))
            padded = jnp.concatenate([columns, jnp.zeros((LANES - ROWS, LANES), jnp.float32)], axis=0)
            out[low : low + size, :] = padded.T[:size]

    work(loads[0], coarse_keys, coarse_count, coarse_src, coarse_out)
    work(loads[1], leaf_keys, leaf_count, leaf_src, leaf_out)


def translate(leaf_keys, leaf_count, coarse_keys, coarse_count, leaf_table, coarse_table, ops):
    smem = pl.BlockSpec(memory_space=pltpu.SMEM)
    whole = pl.BlockSpec(memory_space=VMEM)
    return pl.pallas_call(
        translate_kernel,
        out_shape=(
            jax.ShapeDtypeStruct((4 * LEAF_DEV, LANES), jnp.float32),
            jax.ShapeDtypeStruct((LEAF_DEV, LANES), jnp.float32),
        ),
        in_specs=[pl.BlockSpec(memory_space=pl.ANY), smem] * 2 + [whole] * 3,
        out_specs=(whole, whole),
        scratch_shapes=[
            VMEM((4 * LEAF_DEV, ROWS, LANES), jnp.float32),
            pltpu.SMEM((5120,), jnp.int32),
            pltpu.SMEM((3072,), jnp.int32),
            pltpu.SemaphoreType.DMA((2,)),
        ],
        compiler_params=pltpu.CompilerParams(vmem_limit_bytes=36 * MIB),
        name="translate",
    )(leaf_keys.reshape(-1), leaf_count, coarse_keys.reshape(-1), coarse_count, leaf_table, coarse_table, ops)


def near_groups(pos_ref, q_ref, out_ref, low, high):
    def group(g, carry):
        at = pl.ds(pl.multiple_of(g * 8, 8), 8)
        rows = [pos_ref[d, at, :] for d in range(3)] + [q_ref[at, :]]
        columns = [r.T for r in rows]
        for b in range(8):
            xj, yj, zj, qj = (r[b : b + 1, :] for r in rows)
            xi, yi, zi, qi = (c[:, b : b + 1] for c in columns)
            sums = [jnp.zeros((8, LANES), jnp.float32) for _ in range(4)]
            for c in range(4):
                part = slice(c * 32, c * 32 + 32)
                dx = xj - xi[part]
                dy = yj - yi[part]
                dz = zj - zi[part]
                inverse = lax.rsqrt(dx * dx + dy * dy + dz * dz + SOFTENING)
                same = iota((32, LANES), 0) + c * 32 == iota((32, LANES), 1)
                weighted = jnp.where(same, 0.0, inverse * qi[part])
                strength = weighted * (inverse * inverse)
                for n, term in enumerate((strength * dx, strength * dy, strength * dz, weighted)):
                    sums[n] = sums[n] + ((term[0:8] + term[8:16]) + (term[16:24] + term[24:32]))
            for n in range(4):
                line = jnp.sum(sums[n], axis=0, keepdims=True)
                if n < 3:
                    line = line * qj
                out_ref[n, pl.ds(g * 8 + b, 1), :] = line
        return carry

    lax.fori_loop(low, high, group, 0)


class Place:
    def __init__(self):
        dom = lax.axis_index("dom")
        self.here = (dom // 8, (dom // 2) % 4, lax.axis_index("lvl"))
        self.core = dom % 2
        self.twin = self.device(self.here, 1 - self.core)

    def device(self, place, core):
        return ((place[0] * 4 + place[1]) * 2 + core, place[2])

    def moved(self, axis, by):
        place = tuple((v + by) % 4 if n == axis else v for n, v in enumerate(self.here))
        return self.device(place, self.core)

    def greet(self):
        barrier = pltpu.get_barrier_semaphore()
        for axis in range(3):
            for by in (1, 2, 3):
                pl.semaphore_signal(barrier, inc=1, device_id=self.moved(axis, by), device_id_type=MESH)
        pl.semaphore_signal(barrier, inc=1, device_id=self.twin, device_id_type=MESH)
        return barrier


def sender(send_sem, recv_sem):
    started = []

    def send(source, target, where):
        n = len(started)
        copy = pltpu.make_async_remote_copy(
            src_ref=source,
            dst_ref=target,
            send_sem=send_sem.at[n],
            recv_sem=recv_sem.at[n],
            device_id=where,
            device_id_type=MESH,
        )
        copy.start()
        started.append(copy)
        return copy

    return started, send


def exchange(place, send, source, one, two, target, between):
    (y, x, z), core = place.here, place.core
    copy = send(source.at[:, :, 1 - core], one.at[core], place.twin)
    one[core] = source[:, :, core]
    between(0)
    copy.wait_recv()
    copies = [send(one.at[:, :, (x + by) % 4], two.at[x], place.moved(1, by)) for by in (1, 2, 3)]
    two[x] = one[:, :, x]
    between(1)
    for copy in copies:
        copy.wait_recv()
    copies = [send(two.at[:, :, (y + by) % 4], target.at[y], place.moved(0, by)) for by in (1, 2, 3)]
    target[y] = two[:, :, y]
    between(2)
    for copy in copies:
        copy.wait_recv()


PARTS = ((0, 16, 24, (2, 0, 1)), (24, 32, 48, (0, 1, 2)), (48, 56, 64, (1, 2, 0)))
COPIES = 66
NEAR_FIRST = 4
SLABS = 9


def gather_kernel(
    atoms_ref, whole_ref, m2m_ref, m2l_hbm,
    all_ref, parent_ref, near_ref, lkeys_ref, lcount_ref, ckeys_ref, ccount_ref, m2l_ref, arrived_ref, place_ref, ids_ref,
    packed, one, two, turned, acc, rows, part_ref, got_c, got_x, got_y, sum_c, sum_x, slabs, send_sem, recv_sem, slab_sem
):
    me = Place()
    here, core, twin = me.here, me.core, me.twin
    table_ref = whole_ref.at[0:64]
    leaf_items = [whole_ref.at[64 + 32 * n : 96 + 32 * n] for n in range(3)]
    coarse_items = [whole_ref.at[160 + 16 * n : 176 + 16 * n] for n in range(3)]

    def slab(g, slot):
        return pltpu.make_async_copy(m2l_hbm.at[pl.ds(g * SLABS, SLABS)], slabs.at[slot], slab_sem.at[slot])

    m2l_ref[OFFSETS * ROWS :, :] = jnp.zeros((ROWS, LANES), jnp.float32)
    slab(0, 0).start()
    barrier = me.greet()
    block_moments(atoms_ref, table_ref[...], whole_ref[208:209, :], place_ref, packed, turned, acc, rows)
    pl.semaphore_wait(barrier, 10)

    started, send = sender(send_sem, recv_sem)

    def block(done, axis, by, low, high):
        y, x, z = (
            slice(None) if n in done else ((here[n] + by) % 4 if n == axis else here[n]) for n in range(3)
        )
        return all_ref.at[y, x, core, z, slice(low, high)]

    def put(ref, where):
        return send(ref, ref, where)

    def parents(done):
        y, x, z = (slice(None) if n in done else here[n] for n in range(3))
        return parent_ref.at[z, y, x, core]

    waiting = {}

    def stage(n):
        if n == 0:
            waiting["p"] = [send(part_ref.at[:, :, 1 - core], got_c, twin)]
            return
        for copy in waiting["p"]:
            copy.wait_recv()
        if n == 1:
            sum_c[...] = part_ref[:, :, core] + got_c[...]
            waiting["p"] = [
                send(sum_c.at[:, (here[1] + by) % 4], got_x.at[by - 1], me.moved(1, by)) for by in (1, 2, 3)
            ]
        elif n == 2:
            sum_x[...] = (sum_c[:, here[1]] + got_x[0]) + (got_x[1] + got_x[2])
            waiting["p"] = [
                send(sum_x.at[(here[0] + by) % 4], got_y.at[by - 1], me.moved(0, by)) for by in (1, 2, 3)
            ]
        elif n == 3:
            parent_ref[here[2], here[0], here[1], core] = (sum_x[here[0]] + got_y[0]) + (got_y[1] + got_y[2])
            waiting["p"] = [put(parents(()), me.moved(2, by)) for by in (1, 2, 3)]
        elif n == 4:
            waiting["p"] = [put(parents((2,)), me.moved(0, by)) for by in (1, 2, 3)]
        elif n == 5:
            waiting["p"] = [put(parents((2, 0)), me.moved(1, by)) for by in (1, 2, 3)]
        elif n == 6:
            waiting["p"] = [put(parents((2, 0, 1)), twin)]

    sorts = [
        (keys, stage)
        for pair in itertools.zip_longest(
            *([(keys, stage) for stage in bitonic_stages(keys.shape[0] * LANES)] for keys in (lkeys_ref, ckeys_ref))
        )
        for keys, stage in filter(None, pair)
    ]

    def sort(low, high):
        now = {}
        for keys, stage in sorts[low:high]:
            name = id(keys)
            if name not in now:
                now[name] = (keys, keys[...])
            now[name] = (keys, bitonic_stage(now[name][1], *stage))
        for keys, value in now.values():
            keys[...] = value

    def turn(low, high):
        def group(g, carry):
            slot = g % 2

            @pl.when(g < COEF // SLABS - 1)
            def _():
                slab(g + 1, 1 - slot).start()

            slab(g, slot).wait()
            for u in range(SLABS):
                for p in range(3):
                    wide = min(LANES, OFFSETS - p * LANES)
                    lines = slabs[slot, u, :, p * LANES : p * LANES + wide].T
                    start = p * LANES * ROWS + g * SLABS + u
                    even = wide // 8 * 8
                    m2l_ref[pl.ds(start, even, stride=ROWS), 0:COEF] = lines[:even]
                    if even < wide:
                        m2l_ref[pl.ds(start + even * ROWS, wide - even, stride=ROWS), 0:COEF] = lines[even:]
            return carry

        lax.fori_loop(low, high, group, 0)

    def fill(n):
        if n == 0:
            write_keys(leaf_items, 4 * LEAF_DEV, 8192, lkeys_ref, lcount_ref)
            write_keys(coarse_items, LEAF_DEV, 1024, ckeys_ref, ccount_ref)
        elif n < 5:
            sort(44 * n - 44, 44 * n)
        turn(*((0, 0), (0, 0), (0, 0), (0, 0), (0, 1), (1, 5), (5, 8), (8, 9))[n])
        if n == 7:
            near_groups(atoms_ref, atoms_ref.at[3], near_ref, 0, NEAR_FIRST)

    exchange(me, send, packed, one, two, arrived_ref, fill)
    first_slot = ((here[0] * 4 + here[1]) * 2 + core) * GROUP * LEAF_DEV + here[2] * LEAF_DEV
    all_ref[here[0], here[1], core, here[2]] = leaf_moments(
        arrived_ref[...].reshape(32 * CAP, LANES), table_ref, m2m_ref, here[2], first_slot, part_ref, ids_ref
    )

    last = []
    for phase in range(2):
        direct = []
        for low, middle, high, order in PARTS:
            axis, done = order[phase], order[:phase]
            direct.append([put(block(done, axis, 0, low, high), me.moved(axis, by)) for by in (1, 3, 2)])
        stage(2 * phase)
        fill(phase + 3)
        stage(2 * phase + 1)
        for (low, middle, high, order), copies in zip(PARTS, direct):
            for copy in copies:
                copy.wait_recv()
    first, second = [], []
    for low, middle, high, order in PARTS:
        axis, done = order[2], order[:2]
        first.append([put(block(done, axis, 0, low, high), me.moved(axis, by)) for by in (1, 3)])
    for low, middle, high, order in PARTS:
        last.append(put(block(order[:2], order[2], 0, low, high), twin))
    stage(4)
    fill(5)
    for (low, middle, high, order), (right, left) in zip(PARTS, first):
        axis, done = order[2], order[:2]
        right.wait_recv()
        a = put(block(done, axis, 3, low, middle), me.moved(axis, 1))
        left.wait_recv()
        b = put(block(done, axis, 1, middle, high), me.moved(axis, 3))
        second.append((a, b))
    for low, middle, high, order in PARTS:
        last.append(put(block(order[:2], order[2], 3, low, high), twin))
        last.append(put(block(order[:2], order[2], 1, low, high), twin))
    stage(5)
    fill(6)
    for (low, middle, high, order), pair in zip(PARTS, second):
        axis, done = order[2], order[:2]
        for copy in pair:
            copy.wait_recv()
        last.append(put(block(done, axis, 2, low, high), twin))
    stage(6)
    fill(7)
    for copy in last:
        copy.wait_recv()
    for copy in waiting["p"]:
        copy.wait_recv()
    for copy in started:
        copy.wait_send()
    assert len(started) == COPIES


def gather(atoms, integers, m2m_ops, m2l_ops):
    whole = pl.BlockSpec(memory_space=VMEM)
    f32, i32 = jnp.float32, jnp.int32
    blocks = atoms.shape[1]
    return pl.pallas_call(
        gather_kernel,
        out_shape=(
            jax.ShapeDtypeStruct((4, 4, 2, 4, LEAF_DEV, LANES), f32),
            jax.ShapeDtypeStruct((4, 4, 4, 2, 8, LANES), f32),
            jax.ShapeDtypeStruct(atoms.shape, f32),
            jax.ShapeDtypeStruct((64, LANES), i32),
            jax.ShapeDtypeStruct((1, LANES), i32),
            jax.ShapeDtypeStruct((32, LANES), i32),
            jax.ShapeDtypeStruct((1, LANES), i32),
            jax.ShapeDtypeStruct(((OFFSETS + 1) * ROWS, LANES), f32),
            jax.ShapeDtypeStruct((4, 4, 2, CAP, LANES), f32),
            jax.ShapeDtypeStruct((1, blocks), i32),
            jax.ShapeDtypeStruct((LEAF_DEV, LANES), i32),
        ),
        in_specs=[whole] * 3 + [pl.BlockSpec(memory_space=pl.ANY)],
        out_specs=(whole,) * 11,
        scratch_shapes=[
            VMEM((4, 4, 2, CAP, LANES), f32),
            VMEM((2, 4, 4, CAP, LANES), f32),
            VMEM((4, 2, 4, CAP, LANES), f32),
            VMEM((4, LANES, blocks), f32),
            VMEM((COEF, 8, blocks), f32),
            VMEM((LANES, blocks), f32),
            VMEM((4, 4, 2, 8, LANES), f32),
            VMEM((4, 4, 8, LANES), f32),
            VMEM((3, 4, 8, LANES), f32),
            VMEM((3, 8, LANES), f32),
            VMEM((4, 4, 8, LANES), f32),
            VMEM((4, 8, LANES), f32),
            VMEM((2, SLABS, COEF, OFFSETS), f32),
            pltpu.SemaphoreType.DMA((COPIES,)),
            pltpu.SemaphoreType.DMA((COPIES,)),
            pltpu.SemaphoreType.DMA((2,)),
        ],
        compiler_params=pltpu.CompilerParams(collective_id=0, has_side_effects=True, vmem_limit_bytes=42 * MIB),
        name="gather",
    )(atoms, integers, m2m_ops.transpose(1, 0, 2), m2l_ops.transpose(1, 2, 0))


def far_kernel(
    terms_ref, parent_ref, ids_ref, arrived_ref, ops_ref, atoms_ref, place_ref, near_ref, matrix_ref,
    force_ref, phi_ref, basis, near, got, sent, one, two, returned, turned, lines, send_sem, recv_sem
):
    me = Place()
    lvl = me.here[2]
    blocks = atoms_ref.shape[1]
    barrier = me.greet()
    for d in range(3):
        turned[d] = atoms_ref[d].T
    shifted = by_octant(parent_ref[...], ops_ref, ids_ref[...][:, 0:1] & 7)
    pl.semaphore_wait(barrier, 10)

    started, send = sender(send_sem, recv_sem)
    shared = [send(terms_ref.at[(lvl + by) % 4], got.at[by - 1], me.moved(2, by)) for by in (1, 2, 3)]
    total = shifted + terms_ref[lvl]

    def prepare(i, carry):
        at = pl.ds(pl.multiple_of(i * 32, 32), 32)

        def emit(row, degree, value):
            basis[row, at, :] = value

        harmonics(turned[0, at, :], turned[1, at, :], turned[2, at, :], emit)
        return carry

    lax.fori_loop(0, 3, prepare, 0)
    done = NEAR_FIRST * 8
    near[:, 0:done] = near_ref[:, 0:done]

    def fill(low, high):
        near_groups(atoms_ref, atoms_ref.at[3], near, low, high)

    fill(4, 8)
    tags = arrived_ref[...].reshape(32 * CAP, LANES)[:, 127:128].astype(jnp.int32)
    member = (iota((32 * CAP, LEAF_DEV), 1) + 1 == tags).astype(jnp.float32)
    for copy in shared:
        copy.wait_recv()
    total = (total + got[0]) + (got[1] + got[2])
    sent[...] = dot(member, total).reshape(sent.shape)

    def between(n):
        if n == 0:
            lax.fori_loop(3, 4, prepare, 0)
        fill(*((8, 10), (10, 13), (13, 16))[n])

    exchange(me, send, sent, one, two, returned, between)
    spread = (iota((32 * CAP, blocks), 0) == place_ref[...]).astype(jnp.float32)

    columns = dot(returned[...].reshape(32 * CAP, LANES), spread, ((0,), (0,)))
    lines[...] = dot(matrix_ref[...], columns)

    def chunk(i, carry):
        at = pl.ds(pl.multiple_of(i * 32, 32), 32)
        sums = [None] * 4
        for row in range(COEF):
            value = basis[row, at, :]
            starts = [(3, 0)] + ([(d, 96 + 64 * d) for d in range(3)] if row < TOP * TOP else [])
            for n, start in starts:
                term = lines[start + row : start + row + 1, :] * value
                sums[n] = term if sums[n] is None else sums[n] + term
        for n in range(4):
            turned[n, at, :] = sums[n]
        return carry

    lax.fori_loop(0, 4, chunk, 0)
    charge = atoms_ref[3]
    for d in range(3):
        force_ref[d] = near[d] - charge * turned[d].T
    phi_ref[...] = near[3] + turned[3].T

    for copy in started:
        copy.wait_send()


def far_field(terms, parent_locals, ids, arrived, l2l_ops, atoms, place, near):
    whole = pl.BlockSpec(memory_space=VMEM)
    f32 = jnp.float32
    return pl.pallas_call(
        far_kernel,
        out_shape=(
            jax.ShapeDtypeStruct((3,) + atoms.shape[1:], f32),
            jax.ShapeDtypeStruct(atoms.shape[1:], f32),
        ),
        in_specs=[whole] * 9,
        out_specs=(whole, whole),
        scratch_shapes=[
            VMEM((COEF,) + atoms.shape[1:], f32),
            VMEM(atoms.shape, f32),
            VMEM((3, LEAF_DEV, LANES), f32),
            VMEM((4, 4, 2, CAP, LANES), f32),
            VMEM((2, 4, 4, CAP, LANES), f32),
            VMEM((4, 2, 4, CAP, LANES), f32),
            VMEM((4, 4, 2, CAP, LANES), f32),
            VMEM(atoms.shape, f32),
            VMEM((G_ROWS, LANES), f32),
            pltpu.SemaphoreType.DMA((10,)),
            pltpu.SemaphoreType.DMA((10,)),
        ],
        compiler_params=pltpu.CompilerParams(collective_id=1, has_side_effects=True, vmem_limit_bytes=20 * MIB),
        name="far_field",
    )(
        terms.reshape(GROUP, LEAF_DEV, LANES), parent_locals, ids, arrived, l2l_ops.transpose(1, 0, 2), atoms, place, near,
        jnp.asarray(gradient_matrix()),
    )


def shards(
    positions,
    charges,
    block_leaf,
    leaf_slot,
    m2m_ops,
    l2l_ops,
    m2l_ops,
    item_target,
    item_source,
    item_offset,
    coarse_target,
    coarse_source,
    coarse_offset,
):
    blocks = block_leaf.shape[0]
    leaves_all = leaf_slot.shape[0]
    parents_all = leaves_all // 8
    atoms = jnp.concatenate([positions.reshape(3, blocks, LANES), charges.reshape(1, blocks, LANES)])
    integers = [leaf_slot, item_target, item_source, item_offset, coarse_target, coarse_source, coarse_offset, block_leaf]
    integers = jnp.concatenate([a.reshape(-1, LANES) for a in integers])
    (
        source_table, parent_table, near, leaf_keys, leaf_count, coarse_keys, coarse_count, turned_ops, arrived, place, ids
    ) = gather(atoms, integers, m2m_ops, m2l_ops)
    source_table = source_table.reshape(leaves_all, LANES)
    parent_table = parent_table.reshape(parents_all, LANES)
    terms, parent_locals = translate(
        leaf_keys,
        leaf_count,
        coarse_keys,
        coarse_count,
        source_table,
        parent_table,
        turned_ops.reshape(OFFSETS + 1, ROWS, LANES),
    )
    forces, potential = far_field(terms, parent_locals, ids, arrived, l2l_ops, atoms, place, near)
    return forces.reshape(3, blocks * LANES), potential.reshape(blocks * LANES)


def solution(mesh):
    in_specs = (
        P(None, ("dom", "lvl")),
        P(("dom", "lvl")),
        P(("dom", "lvl")),
        P(),
        P(),
        P(),
        P(),
        P("dom", "lvl", None),
        P("dom", "lvl", None),
        P("dom", "lvl", None),
        P("dom", "lvl", None),
        P("dom", "lvl", None),
        P("dom", "lvl", None),
    )
    out_specs = (P(None, ("dom", "lvl")), P(("dom", "lvl")))
    return jax.shard_map(shards, mesh=mesh, in_specs=in_specs, out_specs=out_specs, check_vma=False)
```

```python
import functools
import itertools
import math

import jax
import jax.numpy as jnp
import numpy as np
from jax import lax
from jax.experimental import pallas as pl
from jax.experimental.pallas import tpu as pltpu
from jax.sharding import PartitionSpec as P

COEF = 81
OFFSETS = 316
ROWS = 88
TOP = 8
LANES = 128
LEAF_DEV = 64
CAP = 8
GROUP = 4
SOFTENING = 0.04
HIGH = lax.Precision.HIGHEST
VMEM = pltpu.VMEM
MIB = 1 << 20
MESH = pl.DeviceIdType.MESH


def dot(a, b, contract=((1,), (0,))):
    return lax.dot_general(
        a, b, (contract, ((), ())), precision=HIGH, preferred_element_type=jnp.float32
    )


def row_index(degree, azimuth, imaginary):
    start = degree * degree
    return start if azimuth == 0 else start + 2 * azimuth - 1 + int(imaginary)


def row_weight(degree, azimuth):
    return math.sqrt(math.factorial(degree + azimuth) * math.factorial(degree - azimuth))


def harmonics(x, y, z, emit):
    squared = x * x + y * y + z * z
    diag_re, diag_im = None, None
    for azimuth in range(TOP + 1):
        if azimuth == 1:
            diag_re, diag_im = -0.5 * x, -0.5 * y
        elif azimuth > 1:
            factor = -1.0 / (2.0 * azimuth)
            fx, fy = factor * x, factor * y
            diag_re, diag_im = fx * diag_re - fy * diag_im, fx * diag_im + fy * diag_re
        if azimuth == 0:
            parts = [jnp.ones_like(x)]
        else:
            parts = [diag_re, diag_im]
        for which, value in enumerate(parts):
            lower, upper = None, value
            for degree in range(azimuth, TOP + 1):
                if degree > azimuth:
                    factor = 1.0 / ((degree + azimuth) * (degree - azimuth))
                    if degree == 1 and azimuth == 0:
                        fresh = z
                    elif lower is None:
                        fresh = (factor * (2 * degree - 1)) * z * upper
                    else:
                        fresh = (factor * (2 * degree - 1)) * z * upper - (factor * squared) * lower
                    lower, upper = upper, fresh
                emit(row_index(degree, azimuth, which == 1), degree, upper)


G_ROWS = 96 + 3 * 64


def gradient_matrix():
    out = np.zeros((G_ROWS, LANES), np.float64)

    def add(axis, row, degree, azimuth, value_re, value_im):
        if degree < 0 or azimuth > degree:
            return
        out[96 + 64 * axis + row_index(degree, azimuth, 0), row] += value_re
        if azimuth:
            out[96 + 64 * axis + row_index(degree, azimuth, 1), row] += value_im

    for degree in range(TOP + 1):
        for azimuth in range(degree + 1):
            for imaginary in range(2 if azimuth else 1):
                row = row_index(degree, azimuth, imaginary)
                w = row_weight(degree, azimuth)
                out[row, row] = w
                below = degree - 1
                if imaginary:
                    add(2, row, below, azimuth, 0.0, w)
                    add(0, row, below, azimuth + 1, 0.0, 0.5 * w)
                    add(0, row, below, azimuth - 1, 0.0, -0.5 * w)
                    add(1, row, below, azimuth + 1, -0.5 * w, 0.0)
                    add(1, row, below, azimuth - 1, -0.5 * w, 0.0)
                elif azimuth:
                    add(2, row, below, azimuth, w, 0.0)
                    add(0, row, below, azimuth + 1, 0.5 * w, 0.0)
                    add(0, row, below, azimuth - 1, -0.5 * w, 0.0)
                    add(1, row, below, azimuth + 1, 0.0, 0.5 * w)
                    add(1, row, below, azimuth - 1, 0.0, 0.5 * w)
                else:
                    add(2, row, below, 0, w, 0.0)
                    add(0, row, below, 1, w, 0.0)
                    add(1, row, below, 1, 0.0, w)
    return out.astype(np.float32)


def iota(shape, dim):
    return lax.broadcasted_iota(jnp.int32, shape, dim)


WEIGHTS = [row_weight(l, (row - l * l + 1) // 2) for l in range(TOP + 1) for row in range(l * l, (l + 1) * (l + 1))]


def block_moments(atoms_ref, table, leaf, place_ref, packed_ref, turned, acc, rows):
    blocks = leaf.shape[1]
    high = (iota((64, blocks), 0) == (leaf >> 7)).astype(jnp.float32)
    lines = dot(table.astype(jnp.float32), high, ((0,), (0,)))
    slot = jnp.sum(
        jnp.where(iota((LANES, blocks), 0) == (leaf & 127), lines, 0.0), axis=0, keepdims=True
    ).astype(jnp.int32)
    owner = slot >> 8
    hits = iota((32, blocks), 0) == owner
    earlier = (iota((blocks, blocks), 0) < iota((blocks, blocks), 1)).astype(jnp.float32)
    before = dot(hits.astype(jnp.float32), earlier)
    rank = jnp.sum(jnp.where(hits, before, 0.0), axis=0, keepdims=True).astype(jnp.int32)
    place = owner * CAP + rank
    place_ref[...] = place

    for d in range(4):
        turned[d] = atoms_ref[d].T
    acc[...] = jnp.zeros_like(acc)

    def chunk(i, carry):
        at = pl.ds(pl.multiple_of(i * 32, 32), 32)
        x, y, z, q = (turned[d, at, :] for d in range(4))

        def emit(row, degree, value):
            part = q * value
            acc[row] += (part[0:8] + part[8:16]) + (part[16:24] + part[24:32])

        harmonics(x, y, z, emit)
        return carry

    lax.fori_loop(0, 4, chunk, 0)
    rows[...] = jnp.zeros_like(rows)
    for k in range(COEF):
        rows[k : k + 1, :] = WEIGHTS[k] * jnp.sum(acc[k], axis=0, keepdims=True)
    rows[127:128, :] = ((slot & 63) + 1).astype(jnp.float32)
    spread = (iota((32 * CAP, blocks), 0) == place).astype(jnp.float32)
    packed_ref[...] = dot(spread, rows[...].T).reshape(packed_ref.shape)


def by_octant(values, ops_ref, octant):
    lines = ops_ref.shape[0] * 8
    moved = dot(values[:, :COEF], ops_ref[...].reshape(lines, COEF), ((1,), (1,)))
    moved = jnp.where(iota(moved.shape, 1) & 7 == octant, moved, 0.0)
    fold = (iota((lines, LANES), 0) >> 3 == iota((lines, LANES), 1)).astype(jnp.float32)
    return dot(moved, fold)


def leaf_moments(arrived, table_ref, ops_ref, group, first, part_ref, ids_ref):
    tags = arrived[:, 127:128].astype(jnp.int32)
    member = (iota((arrived.shape[0], LEAF_DEV), 1) + 1 == tags).astype(jnp.float32)
    leaf = dot(member, arrived, ((0,), (0,)))
    leaf = jnp.where(iota(leaf.shape, 1) < COEF, leaf, 0.0)
    slots = first + iota((LEAF_DEV, LANES), 0)
    found = jnp.zeros((LEAF_DEV, LANES), jnp.int32)
    lane = iota((LEAF_DEV, LANES), 1)
    table = table_ref[pl.ds(pl.multiple_of(group * 16, 16), 16), :]
    for h in range(16):
        number = (group * 16 + h) * 128 + lane
        found = found + jnp.where(table[h : h + 1, :] == slots, number, 0)
    ids = jnp.sum(found.astype(jnp.float32), axis=1, keepdims=True).astype(jnp.int32)
    ids_ref[...] = jnp.broadcast_to(ids, (LEAF_DEV, LANES))
    children = by_octant(leaf, ops_ref, ids & 7)
    within = (ids >> 3) - group * 256
    picks = (iota((LEAF_DEV, 256), 1) == within).astype(jnp.float32)
    part_ref[...] = dot(picks, children, ((0,), (0,))).reshape(part_ref.shape)
    return leaf


def bitonic_stages(size):
    out, span = [], 2
    while span <= size:
        step = span // 2
        while step >= 1:
            out.append((span, step))
            step //= 2
        span *= 2
    return out


def bitonic_stage(x, span, step):
    rows = x.shape[0]
    index = iota(x.shape, 0) * LANES + iota(x.shape, 1)
    axis, shift, extent = (1, step, LANES) if step < LANES else (0, step // LANES, rows)
    second = (index & step) != 0
    other = jnp.where(second, pltpu.roll(x, shift, axis), pltpu.roll(x, extent - shift, axis))
    take_small = ((index & span) == 0) != second
    return jnp.where(take_small, jnp.minimum(x, other), jnp.maximum(x, other))


def write_keys(items, targets, sources, keys_ref, count_ref):
    target_ref, source_ref, offset_ref = items
    rows = target_ref.shape[0]
    none = ((sources - 1) << 9) | OFFSETS
    keys_ref[...] = jnp.full(keys_ref.shape, ((targets - 1) << 23) | none, jnp.int32)
    keys_ref[0:rows, :] = (target_ref[...] << 23) | (source_ref[...] << 9) | offset_ref[...]
    numbers = iota((targets, LANES), 0)
    count = jnp.zeros((targets, LANES), jnp.float32)
    for r in range(rows):
        count = count + (numbers == target_ref[r : r + 1, :]).astype(jnp.float32)
    count = jnp.sum(count, axis=1, keepdims=True)
    fours = jnp.zeros((1, 1), jnp.int32)
    for p in range((targets + LANES - 1) // LANES):
        size = min(LANES, targets - p * LANES)
        part = count[p * LANES : p * LANES + size]
        diagonal = iota((size, LANES), 0) == iota((size, LANES), 1)
        line = jnp.sum(jnp.where(diagonal, part, 0.0), axis=0, keepdims=True).astype(jnp.int32)
        filled = (line + 3) >> 2
        fours = fours + jnp.sum(filled.astype(jnp.float32), axis=1, keepdims=True).astype(jnp.int32)
        own = iota((1, LANES), 1) + p * LANES
        for turn in range(3):
            goal = jnp.where(turn < filled * 4 - line, own, targets - 1)
            at = rows + 3 * p + turn
            keys_ref[at : at + 1, :] = (goal << 23) | none
    count_ref[...] = jnp.broadcast_to(fours, count_ref.shape)


def translate_kernel(
    leaf_list, leaf_count, coarse_list, coarse_count, leaf_src, coarse_src, ops, leaf_out, coarse_out, acc, leaf_keys, coarse_keys, sems
):
    loads = [
        pltpu.make_async_copy(listing.at[pl.ds(0, keys.shape[0])], keys, sems.at[n])
        for n, (listing, keys) in enumerate(((coarse_list, coarse_keys), (leaf_list, leaf_keys)))
    ]
    for load in loads:
        load.start()

    def work(load, keys, count, src, out):
        targets = out.shape[0]

        def clear(t, carry):
            for u in range(4):
                acc[t * 4 + u] = jnp.zeros(acc.shape[1:], jnp.float32)
            return carry

        lax.fori_loop(0, targets // 4, clear, 0)
        load.wait()

        def term(key):
            row = src[pl.ds((key >> 9) & (src.shape[0] - 1), 1), :][:, :COEF]
            return ops[key & 511, :COEF, :COEF] * row

        def step(i, carry):
            for u in range(8):
                four = [keys[i * 32 + u * 4 + n] for n in range(4)]
                total = (term(four[0]) + term(four[1])) + (term(four[2]) + term(four[3]))
                acc[four[0] >> 23, :COEF, :COEF] += total
            return carry

        lax.fori_loop(0, (count[0, 0] + 7) // 8, step, 0)
        lane = iota((ROWS, LANES), 1)
        for low in range(0, targets, LANES):
            size = min(LANES, targets - low)

            def finish(i, columns):
                for u in range(8):
                    t = i * 8 + u
                    columns = jnp.where(lane == t, jnp.sum(acc[low + t], axis=1, keepdims=True), columns)
                return columns

            columns = lax.fori_loop(0, size // 8, finish, jnp.zeros((ROWS, LANES), jnp.float32))
            padded = jnp.concatenate([columns, jnp.zeros((LANES - ROWS, LANES), jnp.float32)], axis=0)
            out[low : low + size, :] = padded.T[:size]

    work(loads[0], coarse_keys, coarse_count, coarse_src, coarse_out)
    work(loads[1], leaf_keys, leaf_count, leaf_src, leaf_out)


def translate(leaf_keys, leaf_count, coarse_keys, coarse_count, leaf_table, coarse_table, ops):
    smem = pl.BlockSpec(memory_space=pltpu.SMEM)
    whole = pl.BlockSpec(memory_space=VMEM)
    return pl.pallas_call(
        translate_kernel,
        out_shape=(
            jax.ShapeDtypeStruct((4 * LEAF_DEV, LANES), jnp.float32),
            jax.ShapeDtypeStruct((LEAF_DEV, LANES), jnp.float32),
        ),
        in_specs=[pl.BlockSpec(memory_space=pl.ANY), smem] * 2 + [whole] * 3,
        out_specs=(whole, whole),
        scratch_shapes=[
            VMEM((4 * LEAF_DEV, ROWS, LANES), jnp.float32),
            pltpu.SMEM((5120,), jnp.int32),
            pltpu.SMEM((3072,), jnp.int32),
            pltpu.SemaphoreType.DMA((2,)),
        ],
        compiler_params=pltpu.CompilerParams(vmem_limit_bytes=16 * MIB),
        name="translate",
    )(leaf_keys.reshape(-1), leaf_count, coarse_keys.reshape(-1), coarse_count, leaf_table, coarse_table, ops)


def near_tiles(atoms, out, low, high):
    def tile(t, carry):
        at = pl.ds(pl.multiple_of(t * 32, 32), 32)
        x, y, z = (atoms[d, at, :] for d in range(3))
        own = iota((32, LANES), 0) + t * 32

        def fours(masked):
            def four(i, sums):
                for u in range(4):
                    j = i * 4 + u
                    xj, yj, zj, qj = (atoms[d, pl.ds(j, 1), :] for d in range(4))
                    dx, dy, dz = x - xj, y - yj, z - zj
                    inverse = lax.rsqrt(dx * dx + dy * dy + dz * dz + SOFTENING)
                    weighted = inverse * qj
                    if masked:
                        weighted = jnp.where(own == j, 0.0, weighted)
                    strength = weighted * (inverse * inverse)
                    terms = (strength * dx, strength * dy, strength * dz, weighted)
                    sums = tuple(a + b for a, b in zip(sums, terms))
                return sums

            return four

        sums = (jnp.zeros((32, LANES), jnp.float32),) * 4
        sums = lax.fori_loop(0, t * 8, fours(False), sums)
        sums = lax.fori_loop(t * 8, t * 8 + 8, fours(True), sums)
        sums = lax.fori_loop(t * 8 + 8, 32, fours(False), sums)
        for d in range(3):
            out[d, at, :] = sums[d] * atoms[3, at, :]
        out[3, at, :] = sums[3]
        return carry

    lax.fori_loop(low, high, tile, 0)


class Place:
    def __init__(self):
        dom = lax.axis_index("dom")
        self.here = (dom // 8, (dom // 2) % 4, lax.axis_index("lvl"))
        self.core = dom % 2
        self.twin = self.device(self.here, 1 - self.core)

    def device(self, place, core):
        return ((place[0] * 4 + place[1]) * 2 + core, place[2])

    def moved(self, axis, by):
        place = tuple((v + by) % 4 if n == axis else v for n, v in enumerate(self.here))
        return self.device(place, self.core)

    def greet(self):
        barrier = pltpu.get_barrier_semaphore()
        for axis in range(3):
            for by in (1, 2, 3):
                pl.semaphore_signal(barrier, inc=1, device_id=self.moved(axis, by), device_id_type=MESH)
        pl.semaphore_signal(barrier, inc=1, device_id=self.twin, device_id_type=MESH)
        return barrier


def sender(send_sem, recv_sem):
    started = []

    def send(source, target, where):
        n = len(started)
        copy = pltpu.make_async_remote_copy(
            src_ref=source,
            dst_ref=target,
            send_sem=send_sem.at[n],
            recv_sem=recv_sem.at[n],
            device_id=where,
            device_id_type=MESH,
        )
        copy.start()
        started.append(copy)
        return copy

    return started, send


def exchange(place, send, source, one, two, target, between):
    (y, x, z), core = place.here, place.core
    copy = send(source.at[:, :, 1 - core], one.at[core], place.twin)
    one[core] = source[:, :, core]
    between(0)
    copy.wait_recv()
    copies = [send(one.at[:, :, (x + by) % 4], two.at[x], place.moved(1, by)) for by in (1, 2, 3)]
    two[x] = one[:, :, x]
    between(1)
    for copy in copies:
        copy.wait_recv()
    copies = [send(two.at[:, :, (y + by) % 4], target.at[y], place.moved(0, by)) for by in (1, 2, 3)]
    target[y] = two[:, :, y]
    between(2)
    for copy in copies:
        copy.wait_recv()


PARTS = ((0, 16, 24, (2, 0, 1)), (24, 32, 48, (0, 1, 2)), (48, 56, 64, (1, 2, 0)))
COPIES = 66
SLABS = 9


def gather_kernel(
    atoms_ref, whole_ref, m2m_ref, m2l_hbm,
    all_ref, parent_ref, lkeys_ref, lcount_ref, ckeys_ref, ccount_ref, m2l_ref, arrived_ref, place_ref, ids_ref,
    packed, one, two, turned, acc, rows, part_ref, got_c, got_x, got_y, sum_c, sum_x, slabs, send_sem, recv_sem, slab_sem
):
    me = Place()
    here, core, twin = me.here, me.core, me.twin
    table_ref = whole_ref.at[0:64]
    leaf_items = [whole_ref.at[64 + 32 * n : 96 + 32 * n] for n in range(3)]
    coarse_items = [whole_ref.at[160 + 16 * n : 176 + 16 * n] for n in range(3)]

    def slab(g, slot):
        return pltpu.make_async_copy(m2l_hbm.at[pl.ds(g * SLABS, SLABS)], slabs.at[slot], slab_sem.at[slot])

    m2l_ref[OFFSETS * ROWS :, :] = jnp.zeros((ROWS, LANES), jnp.float32)
    slab(0, 0).start()
    barrier = me.greet()
    block_moments(atoms_ref, table_ref[...], whole_ref[208:209, :], place_ref, packed, turned, acc, rows)
    pl.semaphore_wait(barrier, 10)

    started, send = sender(send_sem, recv_sem)

    def block(done, axis, by, low, high):
        y, x, z = (
            slice(None) if n in done else ((here[n] + by) % 4 if n == axis else here[n]) for n in range(3)
        )
        return all_ref.at[y, x, core, z, slice(low, high)]

    def put(ref, where):
        return send(ref, ref, where)

    def parents(done):
        y, x, z = (slice(None) if n in done else here[n] for n in range(3))
        return parent_ref.at[z, y, x, core]

    waiting = {}

    def stage(n):
        if n == 0:
            waiting["p"] = [send(part_ref.at[:, :, 1 - core], got_c, twin)]
            return
        for copy in waiting["p"]:
            copy.wait_recv()
        if n == 1:
            sum_c[...] = part_ref[:, :, core] + got_c[...]
            waiting["p"] = [
                send(sum_c.at[:, (here[1] + by) % 4], got_x.at[by - 1], me.moved(1, by)) for by in (1, 2, 3)
            ]
        elif n == 2:
            sum_x[...] = (sum_c[:, here[1]] + got_x[0]) + (got_x[1] + got_x[2])
            waiting["p"] = [
                send(sum_x.at[(here[0] + by) % 4], got_y.at[by - 1], me.moved(0, by)) for by in (1, 2, 3)
            ]
        elif n == 3:
            parent_ref[here[2], here[0], here[1], core] = (sum_x[here[0]] + got_y[0]) + (got_y[1] + got_y[2])
            waiting["p"] = [put(parents(()), me.moved(2, by)) for by in (1, 2, 3)]
        elif n == 4:
            waiting["p"] = [put(parents((2,)), me.moved(0, by)) for by in (1, 2, 3)]
        elif n == 5:
            waiting["p"] = [put(parents((2, 0)), me.moved(1, by)) for by in (1, 2, 3)]
        elif n == 6:
            waiting["p"] = [put(parents((2, 0, 1)), twin)]

    sorts = [
        (keys, stage)
        for pair in itertools.zip_longest(
            *([(keys, stage) for stage in bitonic_stages(keys.shape[0] * LANES)] for keys in (lkeys_ref, ckeys_ref))
        )
        for keys, stage in filter(None, pair)
    ]

    def sort(low, high):
        now = {}
        for keys, stage in sorts[low:high]:
            name = id(keys)
            if name not in now:
                now[name] = (keys, keys[...])
            now[name] = (keys, bitonic_stage(now[name][1], *stage))
        for keys, value in now.values():
            keys[...] = value

    def turn(low, high):
        def group(g, carry):
            slot = g % 2

            @pl.when(g < COEF // SLABS - 1)
            def _():
                slab(g + 1, 1 - slot).start()

            slab(g, slot).wait()
            for u in range(SLABS):
                for p in range(3):
                    wide = min(LANES, OFFSETS - p * LANES)
                    lines = slabs[slot, u, :, p * LANES : p * LANES + wide].T
                    start = p * LANES * ROWS + g * SLABS + u
                    even = wide // 8 * 8
                    m2l_ref[pl.ds(start, even, stride=ROWS), 0:COEF] = lines[:even]
                    if even < wide:
                        m2l_ref[pl.ds(start + even * ROWS, wide - even, stride=ROWS), 0:COEF] = lines[even:]
            return carry

        lax.fori_loop(low, high, group, 0)

    def fill(n):
        if n == 0:
            write_keys(leaf_items, 4 * LEAF_DEV, 8192, lkeys_ref, lcount_ref)
            write_keys(coarse_items, LEAF_DEV, 1024, ckeys_ref, ccount_ref)
        elif n < 5:
            sort(44 * n - 44, 44 * n)
        turn(*((0, 0), (0, 0), (0, 0), (0, 0), (0, 1), (1, 5), (5, 8), (8, 9))[n])

    exchange(me, send, packed, one, two, arrived_ref, fill)
    first_slot = ((here[0] * 4 + here[1]) * 2 + core) * GROUP * LEAF_DEV + here[2] * LEAF_DEV
    all_ref[here[0], here[1], core, here[2]] = leaf_moments(
        arrived_ref[...].reshape(32 * CAP, LANES), table_ref, m2m_ref, here[2], first_slot, part_ref, ids_ref
    )

    last = []
    for phase in range(2):
        direct = []
        for low, middle, high, order in PARTS:
            axis, done = order[phase], order[:phase]
            direct.append([put(block(done, axis, 0, low, high), me.moved(axis, by)) for by in (1, 3, 2)])
        stage(2 * phase)
        fill(phase + 3)
        stage(2 * phase + 1)
        for (low, middle, high, order), copies in zip(PARTS, direct):
            for copy in copies:
                copy.wait_recv()
    first, second = [], []
    for low, middle, high, order in PARTS:
        axis, done = order[2], order[:2]
        first.append([put(block(done, axis, 0, low, high), me.moved(axis, by)) for by in (1, 3)])
    for low, middle, high, order in PARTS:
        last.append(put(block(order[:2], order[2], 0, low, high), twin))
    stage(4)
    fill(5)
    for (low, middle, high, order), (right, left) in zip(PARTS, first):
        axis, done = order[2], order[:2]
        right.wait_recv()
        a = put(block(done, axis, 3, low, middle), me.moved(axis, 1))
        left.wait_recv()
        b = put(block(done, axis, 1, middle, high), me.moved(axis, 3))
        second.append((a, b))
    for low, middle, high, order in PARTS:
        last.append(put(block(order[:2], order[2], 3, low, high), twin))
        last.append(put(block(order[:2], order[2], 1, low, high), twin))
    stage(5)
    fill(6)
    for (low, middle, high, order), pair in zip(PARTS, second):
        axis, done = order[2], order[:2]
        for copy in pair:
            copy.wait_recv()
        last.append(put(block(done, axis, 2, low, high), twin))
    stage(6)
    fill(7)
    for copy in last:
        copy.wait_recv()
    for copy in waiting["p"]:
        copy.wait_recv()
    for copy in started:
        copy.wait_send()
    assert len(started) == COPIES


def gather(atoms, integers, m2m_ops, m2l_ops):
    whole = pl.BlockSpec(memory_space=VMEM)
    f32, i32 = jnp.float32, jnp.int32
    blocks = atoms.shape[1]
    return pl.pallas_call(
        gather_kernel,
        out_shape=(
            jax.ShapeDtypeStruct((4, 4, 2, 4, LEAF_DEV, LANES), f32),
            jax.ShapeDtypeStruct((4, 4, 4, 2, 8, LANES), f32),
            jax.ShapeDtypeStruct((64, LANES), i32),
            jax.ShapeDtypeStruct((1, LANES), i32),
            jax.ShapeDtypeStruct((32, LANES), i32),
            jax.ShapeDtypeStruct((1, LANES), i32),
            jax.ShapeDtypeStruct(((OFFSETS + 1) * ROWS, LANES), f32),
            jax.ShapeDtypeStruct((4, 4, 2, CAP, LANES), f32),
            jax.ShapeDtypeStruct((1, blocks), i32),
            jax.ShapeDtypeStruct((LEAF_DEV, LANES), i32),
        ),
        in_specs=[whole] * 3 + [pl.BlockSpec(memory_space=pl.ANY)],
        out_specs=(whole,) * 10,
        scratch_shapes=[
            VMEM((4, 4, 2, CAP, LANES), f32),
            VMEM((2, 4, 4, CAP, LANES), f32),
            VMEM((4, 2, 4, CAP, LANES), f32),
            VMEM((4, LANES, blocks), f32),
            VMEM((COEF, 8, blocks), f32),
            VMEM((LANES, blocks), f32),
            VMEM((4, 4, 2, 8, LANES), f32),
            VMEM((4, 4, 8, LANES), f32),
            VMEM((3, 4, 8, LANES), f32),
            VMEM((3, 8, LANES), f32),
            VMEM((4, 4, 8, LANES), f32),
            VMEM((4, 8, LANES), f32),
            VMEM((2, SLABS, COEF, OFFSETS), f32),
            pltpu.SemaphoreType.DMA((COPIES,)),
            pltpu.SemaphoreType.DMA((COPIES,)),
            pltpu.SemaphoreType.DMA((2,)),
        ],
        compiler_params=pltpu.CompilerParams(collective_id=0, has_side_effects=True, vmem_limit_bytes=24 * MIB),
        name="gather",
    )(atoms, integers, m2m_ops.transpose(1, 0, 2), m2l_ops.transpose(1, 2, 0))


def far_kernel(
    terms_ref, parent_ref, ids_ref, arrived_ref, ops_ref, atoms_ref, place_ref, matrix_ref,
    force_ref, phi_ref, basis, near, got, sent, one, two, returned, turned, lines, send_sem, recv_sem
):
    me = Place()
    lvl = me.here[2]
    blocks = atoms_ref.shape[1]
    barrier = me.greet()
    for d in range(4):
        turned[d] = atoms_ref[d].T
    shifted = by_octant(parent_ref[...], ops_ref, ids_ref[...][:, 0:1] & 7)
    pl.semaphore_wait(barrier, 10)

    started, send = sender(send_sem, recv_sem)
    shared = [send(terms_ref.at[(lvl + by) % 4], got.at[by - 1], me.moved(2, by)) for by in (1, 2, 3)]
    total = shifted + terms_ref[lvl]

    def prepare(i, carry):
        at = pl.ds(pl.multiple_of(i * 32, 32), 32)

        def emit(row, degree, value):
            basis[row, at, :] = value

        harmonics(turned[0, at, :], turned[1, at, :], turned[2, at, :], emit)
        return carry

    lax.fori_loop(0, 3, prepare, 0)
    near_tiles(turned, near, 0, 1)
    tags = arrived_ref[...].reshape(32 * CAP, LANES)[:, 127:128].astype(jnp.int32)
    member = (iota((32 * CAP, LEAF_DEV), 1) + 1 == tags).astype(jnp.float32)
    for copy in shared:
        copy.wait_recv()
    total = (total + got[0]) + (got[1] + got[2])
    sent[...] = dot(member, total).reshape(sent.shape)

    def between(n):
        if n == 0:
            lax.fori_loop(3, 4, prepare, 0)
        near_tiles(turned, near, n + 1, n + 2)

    exchange(me, send, sent, one, two, returned, between)
    spread = (iota((32 * CAP, blocks), 0) == place_ref[...]).astype(jnp.float32)

    columns = dot(returned[...].reshape(32 * CAP, LANES), spread, ((0,), (0,)))
    lines[...] = dot(matrix_ref[...], columns)

    def chunk(i, carry):
        at = pl.ds(pl.multiple_of(i * 32, 32), 32)
        sums = [None] * 4
        for row in range(COEF):
            value = basis[row, at, :]
            starts = [(3, 0)] + ([(d, 96 + 64 * d) for d in range(3)] if row < TOP * TOP else [])
            for n, start in starts:
                term = lines[start + row : start + row + 1, :] * value
                sums[n] = term if sums[n] is None else sums[n] + term
        for n in range(3):
            near[n, at, :] = near[n, at, :] - turned[3, at, :] * sums[n]
        near[3, at, :] = near[3, at, :] + sums[3]
        return carry

    lax.fori_loop(0, 4, chunk, 0)
    for d in range(3):
        force_ref[d] = near[d].T
    phi_ref[...] = near[3].T
    for copy in started:
        copy.wait_send()


def far_field(terms, parent_locals, ids, arrived, l2l_ops, atoms, place):
    whole = pl.BlockSpec(memory_space=VMEM)
    f32 = jnp.float32
    return pl.pallas_call(
        far_kernel,
        out_shape=(
            jax.ShapeDtypeStruct((3,) + atoms.shape[1:], f32),
            jax.ShapeDtypeStruct(atoms.shape[1:], f32),
        ),
        in_specs=[whole] * 8,
        out_specs=(whole, whole),
        scratch_shapes=[
            VMEM((COEF,) + atoms.shape[1:], f32),
            VMEM(atoms.shape, f32),
            VMEM((3, LEAF_DEV, LANES), f32),
            VMEM((4, 4, 2, CAP, LANES), f32),
            VMEM((2, 4, 4, CAP, LANES), f32),
            VMEM((4, 2, 4, CAP, LANES), f32),
            VMEM((4, 4, 2, CAP, LANES), f32),
            VMEM(atoms.shape, f32),
            VMEM((G_ROWS, LANES), f32),
            pltpu.SemaphoreType.DMA((10,)),
            pltpu.SemaphoreType.DMA((10,)),
        ],
        compiler_params=pltpu.CompilerParams(collective_id=1, has_side_effects=True, vmem_limit_bytes=20 * MIB),
        name="far_field",
    )(
        terms.reshape(GROUP, LEAF_DEV, LANES), parent_locals, ids, arrived, l2l_ops.transpose(1, 0, 2), atoms, place,
        jnp.asarray(gradient_matrix()),
    )


def stacked(arrays):
    rows = sum(a.shape[0] for a in arrays)
    total, start = None, 0
    for a in arrays:
        part = jnp.pad(a, ((start, rows - start - a.shape[0]), (0, 0)))
        total = part if total is None else total + part
        start += a.shape[0]
    return total


def shards(
    positions,
    charges,
    block_leaf,
    leaf_slot,
    m2m_ops,
    l2l_ops,
    m2l_ops,
    item_target,
    item_source,
    item_offset,
    coarse_target,
    coarse_source,
    coarse_offset,
):
    blocks = block_leaf.shape[0]
    leaves_all = leaf_slot.shape[0]
    parents_all = leaves_all // 8
    atoms = jnp.concatenate([positions.reshape(3, blocks, LANES), charges.reshape(1, blocks, LANES)])
    integers = [leaf_slot, item_target, item_source, item_offset, coarse_target, coarse_source, coarse_offset, block_leaf]
    integers = stacked([a.reshape(-1, LANES) for a in integers])
    (
        source_table, parent_table, leaf_keys, leaf_count, coarse_keys, coarse_count, turned_ops, arrived, place, ids
    ) = gather(atoms, integers, m2m_ops, m2l_ops)
    source_table = source_table.reshape(leaves_all, LANES)
    parent_table = parent_table.reshape(parents_all, LANES)
    terms, parent_locals = translate(
        leaf_keys,
        leaf_count,
        coarse_keys,
        coarse_count,
        source_table,
        parent_table,
        turned_ops.reshape(OFFSETS + 1, ROWS, LANES),
    )
    forces, potential = far_field(terms, parent_locals, ids, arrived, l2l_ops, atoms, place)
    return forces.reshape(3, blocks * LANES), potential.reshape(blocks * LANES)


def solution(mesh):
    in_specs = (
        P(None, ("dom", "lvl")),
        P(("dom", "lvl")),
        P(("dom", "lvl")),
        P(),
        P(),
        P(),
        P(),
        P("dom", "lvl", None),
        P("dom", "lvl", None),
        P("dom", "lvl", None),
        P("dom", "lvl", None),
        P("dom", "lvl", None),
        P("dom", "lvl", None),
    )
    out_specs = (P(None, ("dom", "lvl")), P(("dom", "lvl")))
    return jax.shard_map(shards, mesh=mesh, in_specs=in_specs, out_specs=out_specs, check_vma=False)
```

```python
import functools
import itertools
import math

import jax
import jax.numpy as jnp
import numpy as np
from jax import lax
from jax.experimental import pallas as pl
from jax.experimental.pallas import tpu as pltpu
from jax.sharding import PartitionSpec as P

COEF = 81
OFFSETS = 316
ROWS = 88
TOP = 8
LANES = 128
LEAF_DEV = 64
CAP = 8
GROUP = 4
SOFTENING = 0.04
HIGH = lax.Precision.HIGHEST
VMEM = pltpu.VMEM
MIB = 1 << 20
MESH = pl.DeviceIdType.MESH


def dot(a, b, contract=((1,), (0,))):
    return lax.dot_general(
        a, b, (contract, ((), ())), precision=HIGH, preferred_element_type=jnp.float32
    )


def row_index(degree, azimuth, imaginary):
    start = degree * degree
    return start if azimuth == 0 else start + 2 * azimuth - 1 + int(imaginary)


def row_weight(degree, azimuth):
    return math.sqrt(math.factorial(degree + azimuth) * math.factorial(degree - azimuth))


def harmonics(x, y, z, emit):
    squared = x * x + y * y + z * z
    diag_re, diag_im = None, None
    for azimuth in range(TOP + 1):
        if azimuth == 1:
            diag_re, diag_im = -0.5 * x, -0.5 * y
        elif azimuth > 1:
            factor = -1.0 / (2.0 * azimuth)
            fx, fy = factor * x, factor * y
            diag_re, diag_im = fx * diag_re - fy * diag_im, fx * diag_im + fy * diag_re
        if azimuth == 0:
            parts = [jnp.ones_like(x)]
        else:
            parts = [diag_re, diag_im]
        for which, value in enumerate(parts):
            lower, upper = None, value
            for degree in range(azimuth, TOP + 1):
                if degree > azimuth:
                    factor = 1.0 / ((degree + azimuth) * (degree - azimuth))
                    if degree == 1 and azimuth == 0:
                        fresh = z
                    elif lower is None:
                        fresh = (factor * (2 * degree - 1)) * z * upper
                    else:
                        fresh = (factor * (2 * degree - 1)) * z * upper - (factor * squared) * lower
                    lower, upper = upper, fresh
                emit(row_index(degree, azimuth, which == 1), degree, upper)


G_ROWS = 96 + 3 * 64


def gradient_matrix():
    out = np.zeros((G_ROWS, LANES), np.float64)

    def add(axis, row, degree, azimuth, value_re, value_im):
        if degree < 0 or azimuth > degree:
            return
        out[96 + 64 * axis + row_index(degree, azimuth, 0), row] += value_re
        if azimuth:
            out[96 + 64 * axis + row_index(degree, azimuth, 1), row] += value_im

    for degree in range(TOP + 1):
        for azimuth in range(degree + 1):
            for imaginary in range(2 if azimuth else 1):
                row = row_index(degree, azimuth, imaginary)
                w = row_weight(degree, azimuth)
                out[row, row] = w
                below = degree - 1
                if imaginary:
                    add(2, row, below, azimuth, 0.0, w)
                    add(0, row, below, azimuth + 1, 0.0, 0.5 * w)
                    add(0, row, below, azimuth - 1, 0.0, -0.5 * w)
                    add(1, row, below, azimuth + 1, -0.5 * w, 0.0)
                    add(1, row, below, azimuth - 1, -0.5 * w, 0.0)
                elif azimuth:
                    add(2, row, below, azimuth, w, 0.0)
                    add(0, row, below, azimuth + 1, 0.5 * w, 0.0)
                    add(0, row, below, azimuth - 1, -0.5 * w, 0.0)
                    add(1, row, below, azimuth + 1, 0.0, 0.5 * w)
                    add(1, row, below, azimuth - 1, 0.0, 0.5 * w)
                else:
                    add(2, row, below, 0, w, 0.0)
                    add(0, row, below, 1, w, 0.0)
                    add(1, row, below, 1, 0.0, w)
    return out.astype(np.float32)


def iota(shape, dim):
    return lax.broadcasted_iota(jnp.int32, shape, dim)


WEIGHTS = [row_weight(l, (row - l * l + 1) // 2) for l in range(TOP + 1) for row in range(l * l, (l + 1) * (l + 1))]


def block_moments(atoms_ref, table, leaf, place_ref, packed_ref, turned, acc, rows):
    blocks = leaf.shape[1]
    high = (iota((64, blocks), 0) == (leaf >> 7)).astype(jnp.float32)
    lines = dot(table.astype(jnp.float32), high, ((0,), (0,)))
    slot = jnp.sum(
        jnp.where(iota((LANES, blocks), 0) == (leaf & 127), lines, 0.0), axis=0, keepdims=True
    ).astype(jnp.int32)
    owner = slot >> 8
    hits = iota((32, blocks), 0) == owner
    earlier = (iota((blocks, blocks), 0) < iota((blocks, blocks), 1)).astype(jnp.float32)
    before = dot(hits.astype(jnp.float32), earlier)
    rank = jnp.sum(jnp.where(hits, before, 0.0), axis=0, keepdims=True).astype(jnp.int32)
    place = owner * CAP + rank
    place_ref[...] = place

    for d in range(4):
        turned[d] = atoms_ref[d].T
    acc[...] = jnp.zeros_like(acc)

    def chunk(i, carry):
        at = pl.ds(pl.multiple_of(i * 32, 32), 32)
        x, y, z, q = (turned[d, at, :] for d in range(4))

        def emit(row, degree, value):
            part = q * value
            acc[row] += (part[0:8] + part[8:16]) + (part[16:24] + part[24:32])

        harmonics(x, y, z, emit)
        return carry

    lax.fori_loop(0, 4, chunk, 0)
    rows[...] = jnp.zeros_like(rows)
    for k in range(COEF):
        rows[k : k + 1, :] = WEIGHTS[k] * jnp.sum(acc[k], axis=0, keepdims=True)
    rows[127:128, :] = ((slot & 63) + 1).astype(jnp.float32)
    spread = (iota((32 * CAP, blocks), 0) == place).astype(jnp.float32)
    packed_ref[...] = dot(spread, rows[...].T).reshape(packed_ref.shape)


def by_octant(values, ops_ref, octant):
    lines = ops_ref.shape[0] * 8
    moved = dot(values[:, :COEF], ops_ref[...].reshape(lines, COEF), ((1,), (1,)))
    moved = jnp.where(iota(moved.shape, 1) & 7 == octant, moved, 0.0)
    fold = (iota((lines, LANES), 0) >> 3 == iota((lines, LANES), 1)).astype(jnp.float32)
    return dot(moved, fold)


def leaf_moments(arrived, table_ref, ops_ref, group, first, part_ref, ids_ref):
    tags = arrived[:, 127:128].astype(jnp.int32)
    member = (iota((arrived.shape[0], LEAF_DEV), 1) + 1 == tags).astype(jnp.float32)
    leaf = dot(member, arrived, ((0,), (0,)))
    leaf = jnp.where(iota(leaf.shape, 1) < COEF, leaf, 0.0)
    slots = first + iota((LEAF_DEV, LANES), 0)
    found = jnp.zeros((LEAF_DEV, LANES), jnp.int32)
    lane = iota((LEAF_DEV, LANES), 1)
    table = table_ref[pl.ds(pl.multiple_of(group * 16, 16), 16), :]
    for h in range(16):
        number = (group * 16 + h) * 128 + lane
        found = found + jnp.where(table[h : h + 1, :] == slots, number, 0)
    ids = jnp.sum(found.astype(jnp.float32), axis=1, keepdims=True).astype(jnp.int32)
    ids_ref[...] = jnp.broadcast_to(ids, (LEAF_DEV, LANES))
    children = by_octant(leaf, ops_ref, ids & 7)
    within = (ids >> 3) - group * 256
    picks = (iota((LEAF_DEV, 256), 1) == within).astype(jnp.float32)
    part_ref[...] = dot(picks, children, ((0,), (0,))).reshape(part_ref.shape)
    return leaf


def bitonic_stages(size):
    out, span = [], 2
    while span <= size:
        step = span // 2
        while step >= 1:
            out.append((span, step))
            step //= 2
        span *= 2
    return out


def bitonic_stage(x, span, step):
    rows = x.shape[0]
    index = iota(x.shape, 0) * LANES + iota(x.shape, 1)
    axis, shift, extent = (1, step, LANES) if step < LANES else (0, step // LANES, rows)
    second = (index & step) != 0
    other = jnp.where(second, pltpu.roll(x, shift, axis), pltpu.roll(x, extent - shift, axis))
    take_small = ((index & span) == 0) != second
    return jnp.where(take_small, jnp.minimum(x, other), jnp.maximum(x, other))


def write_keys(items, targets, sources, keys_ref, count_ref):
    target_ref, source_ref, offset_ref = items
    rows = target_ref.shape[0]
    none = ((sources - 1) << 9) | OFFSETS
    keys_ref[...] = jnp.full(keys_ref.shape, ((targets - 1) << 23) | none, jnp.int32)
    keys_ref[0:rows, :] = (target_ref[...] << 23) | (source_ref[...] << 9) | offset_ref[...]
    numbers = iota((targets, LANES), 0)
    count = jnp.zeros((targets, LANES), jnp.float32)
    for r in range(rows):
        count = count + (numbers == target_ref[r : r + 1, :]).astype(jnp.float32)
    count = jnp.sum(count, axis=1, keepdims=True)
    fours = jnp.zeros((1, 1), jnp.int32)
    for p in range((targets + LANES - 1) // LANES):
        size = min(LANES, targets - p * LANES)
        part = count[p * LANES : p * LANES + size]
        diagonal = iota((size, LANES), 0) == iota((size, LANES), 1)
        line = jnp.sum(jnp.where(diagonal, part, 0.0), axis=0, keepdims=True).astype(jnp.int32)
        filled = (line + 3) >> 2
        fours = fours + jnp.sum(filled.astype(jnp.float32), axis=1, keepdims=True).astype(jnp.int32)
        own = iota((1, LANES), 1) + p * LANES
        for turn in range(3):
            goal = jnp.where(turn < filled * 4 - line, own, targets - 1)
            at = rows + 3 * p + turn
            keys_ref[at : at + 1, :] = (goal << 23) | none
    count_ref[...] = jnp.broadcast_to(fours, count_ref.shape)


def translate_kernel(
    leaf_list, leaf_count, coarse_list, coarse_count, leaf_src, coarse_src, ops, leaf_out, coarse_out, acc, leaf_keys, coarse_keys, sems
):
    loads = [
        pltpu.make_async_copy(listing.at[pl.ds(0, keys.shape[0])], keys, sems.at[n])
        for n, (listing, keys) in enumerate(((coarse_list, coarse_keys), (leaf_list, leaf_keys)))
    ]
    for load in loads:
        load.start()

    def work(load, keys, count, src, out):
        targets = out.shape[0]

        def clear(t, carry):
            for u in range(4):
                acc[t * 4 + u] = jnp.zeros(acc.shape[1:], jnp.float32)
            return carry

        lax.fori_loop(0, targets // 4, clear, 0)
        load.wait()

        def term(key):
            row = src[pl.ds((key >> 9) & (src.shape[0] - 1), 1), :][:, :COEF]
            return ops[key & 511, :COEF, :COEF] * row

        def step(i, carry):
            for u in range(8):
                four = [keys[i * 32 + u * 4 + n] for n in range(4)]
                total = (term(four[0]) + term(four[1])) + (term(four[2]) + term(four[3]))
                acc[four[0] >> 23, :COEF, :COEF] += total
            return carry

        lax.fori_loop(0, (count[0, 0] + 7) // 8, step, 0)
        lane = iota((ROWS, LANES), 1)
        for low in range(0, targets, LANES):
            size = min(LANES, targets - low)

            def finish(i, columns):
                for u in range(8):
                    t = i * 8 + u
                    columns = jnp.where(lane == t, jnp.sum(acc[low + t], axis=1, keepdims=True), columns)
                return columns

            columns = lax.fori_loop(0, size // 8, finish, jnp.zeros((ROWS, LANES), jnp.float32))
            padded = jnp.concatenate([columns, jnp.zeros((LANES - ROWS, LANES), jnp.float32)], axis=0)
            out[low : low + size, :] = padded.T[:size]

    work(loads[0], coarse_keys, coarse_count, coarse_src, coarse_out)
    work(loads[1], leaf_keys, leaf_count, leaf_src, leaf_out)


def translate(leaf_keys, leaf_count, coarse_keys, coarse_count, leaf_table, coarse_table, ops):
    smem = pl.BlockSpec(memory_space=pltpu.SMEM)
    whole = pl.BlockSpec(memory_space=VMEM)
    return pl.pallas_call(
        translate_kernel,
        out_shape=(
            jax.ShapeDtypeStruct((4 * LEAF_DEV, LANES), jnp.float32),
            jax.ShapeDtypeStruct((LEAF_DEV, LANES), jnp.float32),
        ),
        in_specs=[pl.BlockSpec(memory_space=pl.ANY), smem] * 2 + [whole] * 3,
        out_specs=(whole, whole),
        scratch_shapes=[
            VMEM((4 * LEAF_DEV, ROWS, LANES), jnp.float32),
            pltpu.SMEM((5120,), jnp.int32),
            pltpu.SMEM((3072,), jnp.int32),
            pltpu.SemaphoreType.DMA((2,)),
        ],
        compiler_params=pltpu.CompilerParams(vmem_limit_bytes=16 * MIB),
        name="translate",
    )(leaf_keys.reshape(-1), leaf_count, coarse_keys.reshape(-1), coarse_count, leaf_table, coarse_table, ops)


def near_tiles(atoms, out, low, high):
    def tile(t, carry):
        at = pl.ds(pl.multiple_of(t * 32, 32), 32)
        x, y, z = (atoms[d, at, :] for d in range(3))
        own = iota((32, LANES), 0) + t * 32

        def fours(masked):
            def four(i, sums):
                for u in range(4):
                    j = i * 4 + u
                    xj, yj, zj, qj = (atoms[d, pl.ds(j, 1), :] for d in range(4))
                    dx, dy, dz = x - xj, y - yj, z - zj
                    inverse = lax.rsqrt(dx * dx + dy * dy + dz * dz + SOFTENING)
                    weighted = inverse * qj
                    if masked:
                        weighted = jnp.where(own == j, 0.0, weighted)
                    strength = weighted * (inverse * inverse)
                    terms = (strength * dx, strength * dy, strength * dz, weighted)
                    sums = tuple(a + b for a, b in zip(sums, terms))
                return sums

            return four

        sums = (jnp.zeros((32, LANES), jnp.float32),) * 4
        sums = lax.fori_loop(0, t * 8, fours(False), sums)
        sums = lax.fori_loop(t * 8, t * 8 + 8, fours(True), sums)
        sums = lax.fori_loop(t * 8 + 8, 32, fours(False), sums)
        for d in range(3):
            out[d, at, :] = sums[d] * atoms[3, at, :]
        out[3, at, :] = sums[3]
        return carry

    lax.fori_loop(low, high, tile, 0)


class Place:
    def __init__(self):
        dom = lax.axis_index("dom")
        self.here = (dom // 8, (dom // 2) % 4, lax.axis_index("lvl"))
        self.core = dom % 2
        self.twin = self.device(self.here, 1 - self.core)

    def device(self, place, core):
        return ((place[0] * 4 + place[1]) * 2 + core, place[2])

    def moved(self, axis, by):
        place = tuple((v + by) % 4 if n == axis else v for n, v in enumerate(self.here))
        return self.device(place, self.core)

    def greet(self):
        barrier = pltpu.get_barrier_semaphore()
        for axis in range(3):
            for by in (1, 2, 3):
                pl.semaphore_signal(barrier, inc=1, device_id=self.moved(axis, by), device_id_type=MESH)
        pl.semaphore_signal(barrier, inc=1, device_id=self.twin, device_id_type=MESH)
        return barrier


def sender(send_sem, recv_sem):
    started = []

    def send(source, target, where):
        n = len(started)
        copy = pltpu.make_async_remote_copy(
            src_ref=source,
            dst_ref=target,
            send_sem=send_sem.at[n],
            recv_sem=recv_sem.at[n],
            device_id=where,
            device_id_type=MESH,
        )
        copy.start()
        started.append(copy)
        return copy

    return started, send


def exchange(place, send, source, one, two, target, between):
    (y, x, z), core = place.here, place.core
    copy = send(source.at[:, :, 1 - core], one.at[core], place.twin)
    one[core] = source[:, :, core]
    between(0)
    copy.wait_recv()
    copies = [send(one.at[:, :, (x + by) % 4], two.at[x], place.moved(1, by)) for by in (1, 2, 3)]
    two[x] = one[:, :, x]
    between(1)
    for copy in copies:
        copy.wait_recv()
    copies = [send(two.at[:, :, (y + by) % 4], target.at[y], place.moved(0, by)) for by in (1, 2, 3)]
    target[y] = two[:, :, y]
    between(2)
    for copy in copies:
        copy.wait_recv()


PARTS = ((0, 16, 24, (2, 0, 1)), (24, 32, 48, (0, 1, 2)), (48, 56, 64, (1, 2, 0)))
COPIES = 66
NEAR_FIRST = 2
SLABS = 9


def gather_kernel(
    atoms_ref, whole_ref, m2m_ref, m2l_hbm,
    all_ref, parent_ref, near_ref, lkeys_ref, lcount_ref, ckeys_ref, ccount_ref, m2l_ref, arrived_ref, place_ref, ids_ref,
    packed, one, two, turned, acc, rows, part_ref, got_c, got_x, got_y, sum_c, sum_x, slabs, send_sem, recv_sem, slab_sem
):
    me = Place()
    here, core, twin = me.here, me.core, me.twin
    table_ref = whole_ref.at[0:64]
    leaf_items = [whole_ref.at[64 + 32 * n : 96 + 32 * n] for n in range(3)]
    coarse_items = [whole_ref.at[160 + 16 * n : 176 + 16 * n] for n in range(3)]

    def slab(g, slot):
        return pltpu.make_async_copy(m2l_hbm.at[pl.ds(g * SLABS, SLABS)], slabs.at[slot], slab_sem.at[slot])

    m2l_ref[OFFSETS * ROWS :, :] = jnp.zeros((ROWS, LANES), jnp.float32)
    slab(0, 0).start()
    barrier = me.greet()
    block_moments(atoms_ref, table_ref[...], whole_ref[208:209, :], place_ref, packed, turned, acc, rows)
    pl.semaphore_wait(barrier, 10)

    started, send = sender(send_sem, recv_sem)

    def block(done, axis, by, low, high):
        y, x, z = (
            slice(None) if n in done else ((here[n] + by) % 4 if n == axis else here[n]) for n in range(3)
        )
        return all_ref.at[y, x, core, z, slice(low, high)]

    def put(ref, where):
        return send(ref, ref, where)

    def parents(done):
        y, x, z = (slice(None) if n in done else here[n] for n in range(3))
        return parent_ref.at[z, y, x, core]

    waiting = {}

    def stage(n):
        if n == 0:
            waiting["p"] = [send(part_ref.at[:, :, 1 - core], got_c, twin)]
            return
        for copy in waiting["p"]:
            copy.wait_recv()
        if n == 1:
            sum_c[...] = part_ref[:, :, core] + got_c[...]
            waiting["p"] = [
                send(sum_c.at[:, (here[1] + by) % 4], got_x.at[by - 1], me.moved(1, by)) for by in (1, 2, 3)
            ]
        elif n == 2:
            sum_x[...] = (sum_c[:, here[1]] + got_x[0]) + (got_x[1] + got_x[2])
            waiting["p"] = [
                send(sum_x.at[(here[0] + by) % 4], got_y.at[by - 1], me.moved(0, by)) for by in (1, 2, 3)
            ]
        elif n == 3:
            parent_ref[here[2], here[0], here[1], core] = (sum_x[here[0]] + got_y[0]) + (got_y[1] + got_y[2])
            waiting["p"] = [put(parents(()), me.moved(2, by)) for by in (1, 2, 3)]
        elif n == 4:
            waiting["p"] = [put(parents((2,)), me.moved(0, by)) for by in (1, 2, 3)]
        elif n == 5:
            waiting["p"] = [put(parents((2, 0)), me.moved(1, by)) for by in (1, 2, 3)]
        elif n == 6:
            waiting["p"] = [put(parents((2, 0, 1)), twin)]

    sorts = [
        (keys, stage)
        for pair in itertools.zip_longest(
            *([(keys, stage) for stage in bitonic_stages(keys.shape[0] * LANES)] for keys in (lkeys_ref, ckeys_ref))
        )
        for keys, stage in filter(None, pair)
    ]

    def sort(low, high):
        now = {}
        for keys, stage in sorts[low:high]:
            name = id(keys)
            if name not in now:
                now[name] = (keys, keys[...])
            now[name] = (keys, bitonic_stage(now[name][1], *stage))
        for keys, value in now.values():
            keys[...] = value

    def turn(low, high):
        def group(g, carry):
            slot = g % 2

            @pl.when(g < COEF // SLABS - 1)
            def _():
                slab(g + 1, 1 - slot).start()

            slab(g, slot).wait()
            for u in range(SLABS):
                for p in range(3):
                    wide = min(LANES, OFFSETS - p * LANES)
                    lines = slabs[slot, u, :, p * LANES : p * LANES + wide].T
                    start = p * LANES * ROWS + g * SLABS + u
                    even = wide // 8 * 8
                    m2l_ref[pl.ds(start, even, stride=ROWS), 0:COEF] = lines[:even]
                    if even < wide:
                        m2l_ref[pl.ds(start + even * ROWS, wide - even, stride=ROWS), 0:COEF] = lines[even:]
            return carry

        lax.fori_loop(low, high, group, 0)

    def fill(n):
        if n == 0:
            write_keys(leaf_items, 4 * LEAF_DEV, 8192, lkeys_ref, lcount_ref)
            write_keys(coarse_items, LEAF_DEV, 1024, ckeys_ref, ccount_ref)
        elif n < 5:
            sort(44 * n - 44, 44 * n)
        turn(*((0, 0), (0, 0), (0, 0), (0, 0), (0, 0), (0, 4), (4, 7), (7, 9))[n])
        if n in (3, 4):
            near_tiles(turned, near_ref, n - 3, n - 2)

    exchange(me, send, packed, one, two, arrived_ref, fill)
    first_slot = ((here[0] * 4 + here[1]) * 2 + core) * GROUP * LEAF_DEV + here[2] * LEAF_DEV
    all_ref[here[0], here[1], core, here[2]] = leaf_moments(
        arrived_ref[...].reshape(32 * CAP, LANES), table_ref, m2m_ref, here[2], first_slot, part_ref, ids_ref
    )

    last = []
    for phase in range(2):
        direct = []
        for low, middle, high, order in PARTS:
            axis, done = order[phase], order[:phase]
            direct.append([put(block(done, axis, 0, low, high), me.moved(axis, by)) for by in (1, 3, 2)])
        stage(2 * phase)
        fill(phase + 3)
        stage(2 * phase + 1)
        for (low, middle, high, order), copies in zip(PARTS, direct):
            for copy in copies:
                copy.wait_recv()
    first, second = [], []
    for low, middle, high, order in PARTS:
        axis, done = order[2], order[:2]
        first.append([put(block(done, axis, 0, low, high), me.moved(axis, by)) for by in (1, 3)])
    for low, middle, high, order in PARTS:
        last.append(put(block(order[:2], order[2], 0, low, high), twin))
    stage(4)
    fill(5)
    for (low, middle, high, order), (right, left) in zip(PARTS, first):
        axis, done = order[2], order[:2]
        right.wait_recv()
        a = put(block(done, axis, 3, low, middle), me.moved(axis, 1))
        left.wait_recv()
        b = put(block(done, axis, 1, middle, high), me.moved(axis, 3))
        second.append((a, b))
    for low, middle, high, order in PARTS:
        last.append(put(block(order[:2], order[2], 3, low, high), twin))
        last.append(put(block(order[:2], order[2], 1, low, high), twin))
    stage(5)
    fill(6)
    for (low, middle, high, order), pair in zip(PARTS, second):
        axis, done = order[2], order[:2]
        for copy in pair:
            copy.wait_recv()
        last.append(put(block(done, axis, 2, low, high), twin))
    stage(6)
    fill(7)
    for copy in last:
        copy.wait_recv()
    for copy in waiting["p"]:
        copy.wait_recv()
    for copy in started:
        copy.wait_send()
    assert len(started) == COPIES


def gather(atoms, integers, m2m_ops, m2l_ops):
    whole = pl.BlockSpec(memory_space=VMEM)
    f32, i32 = jnp.float32, jnp.int32
    blocks = atoms.shape[1]
    return pl.pallas_call(
        gather_kernel,
        out_shape=(
            jax.ShapeDtypeStruct((4, 4, 2, 4, LEAF_DEV, LANES), f32),
            jax.ShapeDtypeStruct((4, 4, 4, 2, 8, LANES), f32),
            jax.ShapeDtypeStruct((4, 32 * NEAR_FIRST, blocks), f32),
            jax.ShapeDtypeStruct((64, LANES), i32),
            jax.ShapeDtypeStruct((1, LANES), i32),
            jax.ShapeDtypeStruct((32, LANES), i32),
            jax.ShapeDtypeStruct((1, LANES), i32),
            jax.ShapeDtypeStruct(((OFFSETS + 1) * ROWS, LANES), f32),
            jax.ShapeDtypeStruct((4, 4, 2, CAP, LANES), f32),
            jax.ShapeDtypeStruct((1, blocks), i32),
            jax.ShapeDtypeStruct((LEAF_DEV, LANES), i32),
        ),
        in_specs=[whole] * 3 + [pl.BlockSpec(memory_space=pl.ANY)],
        out_specs=(whole,) * 11,
        scratch_shapes=[
            VMEM((4, 4, 2, CAP, LANES), f32),
            VMEM((2, 4, 4, CAP, LANES), f32),
            VMEM((4, 2, 4, CAP, LANES), f32),
            VMEM((4, LANES, blocks), f32),
            VMEM((COEF, 8, blocks), f32),
            VMEM((LANES, blocks), f32),
            VMEM((4, 4, 2, 8, LANES), f32),
            VMEM((4, 4, 8, LANES), f32),
            VMEM((3, 4, 8, LANES), f32),
            VMEM((3, 8, LANES), f32),
            VMEM((4, 4, 8, LANES), f32),
            VMEM((4, 8, LANES), f32),
            VMEM((2, SLABS, COEF, OFFSETS), f32),
            pltpu.SemaphoreType.DMA((COPIES,)),
            pltpu.SemaphoreType.DMA((COPIES,)),
            pltpu.SemaphoreType.DMA((2,)),
        ],
        compiler_params=pltpu.CompilerParams(collective_id=0, has_side_effects=True, vmem_limit_bytes=24 * MIB),
        name="gather",
    )(atoms, integers, m2m_ops.transpose(1, 0, 2), m2l_ops.transpose(1, 2, 0))


def far_kernel(
    terms_ref, parent_ref, ids_ref, arrived_ref, ops_ref, atoms_ref, place_ref, near_ref, matrix_ref,
    force_ref, phi_ref, basis, near, got, sent, one, two, returned, turned, lines, send_sem, recv_sem
):
    me = Place()
    lvl = me.here[2]
    blocks = atoms_ref.shape[1]
    barrier = me.greet()
    for d in range(4):
        turned[d] = atoms_ref[d].T
    shifted = by_octant(parent_ref[...], ops_ref, ids_ref[...][:, 0:1] & 7)
    pl.semaphore_wait(barrier, 10)

    started, send = sender(send_sem, recv_sem)
    shared = [send(terms_ref.at[(lvl + by) % 4], got.at[by - 1], me.moved(2, by)) for by in (1, 2, 3)]
    total = shifted + terms_ref[lvl]

    def prepare(i, carry):
        at = pl.ds(pl.multiple_of(i * 32, 32), 32)

        def emit(row, degree, value):
            basis[row, at, :] = value

        harmonics(turned[0, at, :], turned[1, at, :], turned[2, at, :], emit)
        return carry

    lax.fori_loop(0, 3, prepare, 0)
    near[:, 0 : 32 * NEAR_FIRST] = near_ref[...]
    near_tiles(turned, near, 2, 3)
    tags = arrived_ref[...].reshape(32 * CAP, LANES)[:, 127:128].astype(jnp.int32)
    member = (iota((32 * CAP, LEAF_DEV), 1) + 1 == tags).astype(jnp.float32)
    for copy in shared:
        copy.wait_recv()
    total = (total + got[0]) + (got[1] + got[2])
    sent[...] = dot(member, total).reshape(sent.shape)

    def between(n):
        if n == 0:
            lax.fori_loop(3, 4, prepare, 0)
        if n == 1:
            near_tiles(turned, near, 3, 4)

    exchange(me, send, sent, one, two, returned, between)
    spread = (iota((32 * CAP, blocks), 0) == place_ref[...]).astype(jnp.float32)

    columns = dot(returned[...].reshape(32 * CAP, LANES), spread, ((0,), (0,)))
    lines[...] = dot(matrix_ref[...], columns)

    def chunk(i, carry):
        at = pl.ds(pl.multiple_of(i * 32, 32), 32)
        sums = [None] * 4
        for row in range(COEF):
            value = basis[row, at, :]
            starts = [(3, 0)] + ([(d, 96 + 64 * d) for d in range(3)] if row < TOP * TOP else [])
            for n, start in starts:
                term = lines[start + row : start + row + 1, :] * value
                sums[n] = term if sums[n] is None else sums[n] + term
        for n in range(3):
            near[n, at, :] = near[n, at, :] - turned[3, at, :] * sums[n]
        near[3, at, :] = near[3, at, :] + sums[3]
        return carry

    lax.fori_loop(0, 4, chunk, 0)
    for d in range(3):
        force_ref[d] = near[d].T
    phi_ref[...] = near[3].T
    for copy in started:
        copy.wait_send()


def far_field(terms, parent_locals, ids, arrived, l2l_ops, atoms, place, near):
    whole = pl.BlockSpec(memory_space=VMEM)
    f32 = jnp.float32
    return pl.pallas_call(
        far_kernel,
        out_shape=(
            jax.ShapeDtypeStruct((3,) + atoms.shape[1:], f32),
            jax.ShapeDtypeStruct(atoms.shape[1:], f32),
        ),
        in_specs=[whole] * 9,
        out_specs=(whole, whole),
        scratch_shapes=[
            VMEM((COEF,) + atoms.shape[1:], f32),
            VMEM(atoms.shape, f32),
            VMEM((3, LEAF_DEV, LANES), f32),
            VMEM((4, 4, 2, CAP, LANES), f32),
            VMEM((2, 4, 4, CAP, LANES), f32),
            VMEM((4, 2, 4, CAP, LANES), f32),
            VMEM((4, 4, 2, CAP, LANES), f32),
            VMEM(atoms.shape, f32),
            VMEM((G_ROWS, LANES), f32),
            pltpu.SemaphoreType.DMA((10,)),
            pltpu.SemaphoreType.DMA((10,)),
        ],
        compiler_params=pltpu.CompilerParams(collective_id=1, has_side_effects=True, vmem_limit_bytes=20 * MIB),
        name="far_field",
    )(
        terms.reshape(GROUP, LEAF_DEV, LANES), parent_locals, ids, arrived, l2l_ops.transpose(1, 0, 2), atoms, place, near,
        jnp.asarray(gradient_matrix()),
    )


def stacked(arrays):
    rows = sum(a.shape[0] for a in arrays)
    total, start = None, 0
    for a in arrays:
        part = jnp.pad(a, ((start, rows - start - a.shape[0]), (0, 0)))
        total = part if total is None else total + part
        start += a.shape[0]
    return total


def shards(
    positions,
    charges,
    block_leaf,
    leaf_slot,
    m2m_ops,
    l2l_ops,
    m2l_ops,
    item_target,
    item_source,
    item_offset,
    coarse_target,
    coarse_source,
    coarse_offset,
):
    blocks = block_leaf.shape[0]
    leaves_all = leaf_slot.shape[0]
    parents_all = leaves_all // 8
    atoms = jnp.concatenate([positions.reshape(3, blocks, LANES), charges.reshape(1, blocks, LANES)])
    integers = [leaf_slot, item_target, item_source, item_offset, coarse_target, coarse_source, coarse_offset, block_leaf]
    integers = stacked([a.reshape(-1, LANES) for a in integers])
    (
        source_table, parent_table, near, leaf_keys, leaf_count, coarse_keys, coarse_count, turned_ops, arrived, place, ids
    ) = gather(atoms, integers, m2m_ops, m2l_ops)
    source_table = source_table.reshape(leaves_all, LANES)
    parent_table = parent_table.reshape(parents_all, LANES)
    terms, parent_locals = translate(
        leaf_keys,
        leaf_count,
        coarse_keys,
        coarse_count,
        source_table,
        parent_table,
        turned_ops.reshape(OFFSETS + 1, ROWS, LANES),
    )
    forces, potential = far_field(terms, parent_locals, ids, arrived, l2l_ops, atoms, place, near)
    return forces.reshape(3, blocks * LANES), potential.reshape(blocks * LANES)


def solution(mesh):
    in_specs = (
        P(None, ("dom", "lvl")),
        P(("dom", "lvl")),
        P(("dom", "lvl")),
        P(),
        P(),
        P(),
        P(),
        P("dom", "lvl", None),
        P("dom", "lvl", None),
        P("dom", "lvl", None),
        P("dom", "lvl", None),
        P("dom", "lvl", None),
        P("dom", "lvl", None),
    )
    out_specs = (P(None, ("dom", "lvl")), P(("dom", "lvl")))
    return jax.shard_map(shards, mesh=mesh, in_specs=in_specs, out_specs=out_specs, check_vma=False)
```

```python
import functools
import itertools
import math

import jax
import jax.numpy as jnp
import numpy as np
from jax import lax
from jax.experimental import pallas as pl
from jax.experimental.pallas import tpu as pltpu
from jax.sharding import PartitionSpec as P

COEF = 81
OFFSETS = 316
ROWS = 88
TOP = 8
LANES = 128
LEAF_DEV = 64
CAP = 8
GROUP = 4
SOFTENING = 0.04
HIGH = lax.Precision.HIGHEST
VMEM = pltpu.VMEM
MIB = 1 << 20
MESH = pl.DeviceIdType.MESH


def dot(a, b, contract=((1,), (0,))):
    return lax.dot_general(
        a, b, (contract, ((), ())), precision=HIGH, preferred_element_type=jnp.float32
    )


def row_index(degree, azimuth, imaginary):
    start = degree * degree
    return start if azimuth == 0 else start + 2 * azimuth - 1 + int(imaginary)


def row_weight(degree, azimuth):
    return math.sqrt(math.factorial(degree + azimuth) * math.factorial(degree - azimuth))


def harmonics(x, y, z, emit):
    squared = x * x + y * y + z * z
    diag_re, diag_im = None, None
    for azimuth in range(TOP + 1):
        if azimuth == 1:
            diag_re, diag_im = -0.5 * x, -0.5 * y
        elif azimuth > 1:
            factor = -1.0 / (2.0 * azimuth)
            fx, fy = factor * x, factor * y
            diag_re, diag_im = fx * diag_re - fy * diag_im, fx * diag_im + fy * diag_re
        if azimuth == 0:
            parts = [jnp.ones_like(x)]
        else:
            parts = [diag_re, diag_im]
        for which, value in enumerate(parts):
            lower, upper = None, value
            for degree in range(azimuth, TOP + 1):
                if degree > azimuth:
                    factor = 1.0 / ((degree + azimuth) * (degree - azimuth))
                    if degree == 1 and azimuth == 0:
                        fresh = z
                    elif lower is None:
                        fresh = (factor * (2 * degree - 1)) * z * upper
                    else:
                        fresh = (factor * (2 * degree - 1)) * z * upper - (factor * squared) * lower
                    lower, upper = upper, fresh
                emit(row_index(degree, azimuth, which == 1), degree, upper)


G_ROWS = 96 + 3 * 64


def gradient_matrix():
    out = np.zeros((G_ROWS, LANES), np.float64)

    def add(axis, row, degree, azimuth, value_re, value_im):
        if degree < 0 or azimuth > degree:
            return
        out[96 + 64 * axis + row_index(degree, azimuth, 0), row] += value_re
        if azimuth:
            out[96 + 64 * axis + row_index(degree, azimuth, 1), row] += value_im

    for degree in range(TOP + 1):
        for azimuth in range(degree + 1):
            for imaginary in range(2 if azimuth else 1):
                row = row_index(degree, azimuth, imaginary)
                w = row_weight(degree, azimuth)
                out[row, row] = w
                below = degree - 1
                if imaginary:
                    add(2, row, below, azimuth, 0.0, w)
                    add(0, row, below, azimuth + 1, 0.0, 0.5 * w)
                    add(0, row, below, azimuth - 1, 0.0, -0.5 * w)
                    add(1, row, below, azimuth + 1, -0.5 * w, 0.0)
                    add(1, row, below, azimuth - 1, -0.5 * w, 0.0)
                elif azimuth:
                    add(2, row, below, azimuth, w, 0.0)
                    add(0, row, below, azimuth + 1, 0.5 * w, 0.0)
                    add(0, row, below, azimuth - 1, -0.5 * w, 0.0)
                    add(1, row, below, azimuth + 1, 0.0, 0.5 * w)
                    add(1, row, below, azimuth - 1, 0.0, 0.5 * w)
                else:
                    add(2, row, below, 0, w, 0.0)
                    add(0, row, below, 1, w, 0.0)
                    add(1, row, below, 1, 0.0, w)
    return out.astype(np.float32)


def iota(shape, dim):
    return lax.broadcasted_iota(jnp.int32, shape, dim)


WEIGHTS = [row_weight(l, (row - l * l + 1) // 2) for l in range(TOP + 1) for row in range(l * l, (l + 1) * (l + 1))]


def block_moments(atoms_ref, table, leaf, place_ref, packed_ref, turned, acc, rows):
    blocks = leaf.shape[1]
    high = (iota((64, blocks), 0) == (leaf >> 7)).astype(jnp.float32)
    lines = dot(table.astype(jnp.float32), high, ((0,), (0,)))
    slot = jnp.sum(
        jnp.where(iota((LANES, blocks), 0) == (leaf & 127), lines, 0.0), axis=0, keepdims=True
    ).astype(jnp.int32)
    owner = slot >> 8
    hits = iota((32, blocks), 0) == owner
    earlier = (iota((blocks, blocks), 0) < iota((blocks, blocks), 1)).astype(jnp.float32)
    before = dot(hits.astype(jnp.float32), earlier)
    rank = jnp.sum(jnp.where(hits, before, 0.0), axis=0, keepdims=True).astype(jnp.int32)
    place = owner * CAP + rank
    place_ref[...] = place

    for d in range(4):
        turned[d] = atoms_ref[d].T
    acc[...] = jnp.zeros_like(acc)

    def chunk(i, carry):
        at = pl.ds(pl.multiple_of(i * 32, 32), 32)
        x, y, z, q = (turned[d, at, :] for d in range(4))

        def emit(row, degree, value):
            part = q * value
            acc[row] += (part[0:8] + part[8:16]) + (part[16:24] + part[24:32])

        harmonics(x, y, z, emit)
        return carry

    lax.fori_loop(0, 4, chunk, 0)
    rows[...] = jnp.zeros_like(rows)
    for k in range(COEF):
        rows[k : k + 1, :] = WEIGHTS[k] * jnp.sum(acc[k], axis=0, keepdims=True)
    rows[127:128, :] = ((slot & 63) + 1).astype(jnp.float32)
    spread = (iota((32 * CAP, blocks), 0) == place).astype(jnp.float32)
    packed_ref[...] = dot(spread, rows[...].T).reshape(packed_ref.shape)


def by_octant(values, ops_ref, octant):
    lines = ops_ref.shape[0] * 8
    moved = dot(values[:, :COEF], ops_ref[...].reshape(lines, COEF), ((1,), (1,)))
    moved = jnp.where(iota(moved.shape, 1) & 7 == octant, moved, 0.0)
    fold = (iota((lines, LANES), 0) >> 3 == iota((lines, LANES), 1)).astype(jnp.float32)
    return dot(moved, fold)


def leaf_moments(arrived, table_ref, ops_ref, group, first, part_ref, ids_ref):
    tags = arrived[:, 127:128].astype(jnp.int32)
    member = (iota((arrived.shape[0], LEAF_DEV), 1) + 1 == tags).astype(jnp.float32)
    leaf = dot(member, arrived, ((0,), (0,)))
    leaf = jnp.where(iota(leaf.shape, 1) < COEF, leaf, 0.0)
    slots = first + iota((LEAF_DEV, LANES), 0)
    found = jnp.zeros((LEAF_DEV, LANES), jnp.int32)
    lane = iota((LEAF_DEV, LANES), 1)
    table = table_ref[pl.ds(pl.multiple_of(group * 16, 16), 16), :]
    for h in range(16):
        number = (group * 16 + h) * 128 + lane
        found = found + jnp.where(table[h : h + 1, :] == slots, number, 0)
    ids = jnp.sum(found.astype(jnp.float32), axis=1, keepdims=True).astype(jnp.int32)
    ids_ref[...] = jnp.broadcast_to(ids, (LEAF_DEV, LANES))
    children = by_octant(leaf, ops_ref, ids & 7)
    within = (ids >> 3) - group * 256
    picks = (iota((LEAF_DEV, 256), 1) == within).astype(jnp.float32)
    part_ref[...] = dot(picks, children, ((0,), (0,))).reshape(part_ref.shape)
    return leaf


def bitonic_stages(size):
    out, span = [], 2
    while span <= size:
        step = span // 2
        while step >= 1:
            out.append((span, step))
            step //= 2
        span *= 2
    return out


def bitonic_stage(x, span, step):
    rows = x.shape[0]
    index = iota(x.shape, 0) * LANES + iota(x.shape, 1)
    axis, shift, extent = (1, step, LANES) if step < LANES else (0, step // LANES, rows)
    second = (index & step) != 0
    other = jnp.where(second, pltpu.roll(x, shift, axis), pltpu.roll(x, extent - shift, axis))
    take_small = ((index & span) == 0) != second
    return jnp.where(take_small, jnp.minimum(x, other), jnp.maximum(x, other))


def write_keys(items, targets, sources, keys_ref, count_ref):
    target_ref, source_ref, offset_ref = items
    rows = target_ref.shape[0]
    none = ((sources - 1) << 9) | OFFSETS
    keys_ref[...] = jnp.full(keys_ref.shape, ((targets - 1) << 23) | none, jnp.int32)
    keys_ref[0:rows, :] = (target_ref[...] << 23) | (source_ref[...] << 9) | offset_ref[...]
    numbers = iota((targets, LANES), 0)
    count = jnp.zeros((targets, LANES), jnp.float32)
    for r in range(rows):
        count = count + (numbers == target_ref[r : r + 1, :]).astype(jnp.float32)
    count = jnp.sum(count, axis=1, keepdims=True)
    fours = jnp.zeros((1, 1), jnp.int32)
    for p in range((targets + LANES - 1) // LANES):
        size = min(LANES, targets - p * LANES)
        part = count[p * LANES : p * LANES + size]
        diagonal = iota((size, LANES), 0) == iota((size, LANES), 1)
        line = jnp.sum(jnp.where(diagonal, part, 0.0), axis=0, keepdims=True).astype(jnp.int32)
        filled = (line + 3) >> 2
        fours = fours + jnp.sum(filled.astype(jnp.float32), axis=1, keepdims=True).astype(jnp.int32)
        own = iota((1, LANES), 1) + p * LANES
        for turn in range(3):
            goal = jnp.where(turn < filled * 4 - line, own, targets - 1)
            at = rows + 3 * p + turn
            keys_ref[at : at + 1, :] = (goal << 23) | none
    count_ref[...] = jnp.broadcast_to(fours, count_ref.shape)


def translate_kernel(
    leaf_list, leaf_count, coarse_list, coarse_count, leaf_src, coarse_src, ops, leaf_out, coarse_out, acc, leaf_keys, coarse_keys, sems
):
    loads = [
        pltpu.make_async_copy(listing.at[pl.ds(0, keys.shape[0])], keys, sems.at[n])
        for n, (listing, keys) in enumerate(((coarse_list, coarse_keys), (leaf_list, leaf_keys)))
    ]
    for load in loads:
        load.start()

    def work(load, keys, count, src, out):
        targets = out.shape[0]

        def clear(t, carry):
            for u in range(4):
                acc[t * 4 + u] = jnp.zeros(acc.shape[1:], jnp.float32)
            return carry

        lax.fori_loop(0, targets // 4, clear, 0)
        load.wait()

        def term(key):
            row = src[pl.ds((key >> 9) & (src.shape[0] - 1), 1), :][:, :COEF]
            return ops[key & 511, :COEF, :COEF] * row

        def step(i, carry):
            for u in range(8):
                four = [keys[i * 32 + u * 4 + n] for n in range(4)]
                total = (term(four[0]) + term(four[1])) + (term(four[2]) + term(four[3]))
                acc[four[0] >> 23, :COEF, :COEF] += total
            return carry

        lax.fori_loop(0, (count[0, 0] + 7) // 8, step, 0)
        lane = iota((ROWS, LANES), 1)
        for low in range(0, targets, LANES):
            size = min(LANES, targets - low)

            def finish(i, columns):
                for u in range(8):
                    t = i * 8 + u
                    columns = jnp.where(lane == t, jnp.sum(acc[low + t], axis=1, keepdims=True), columns)
                return columns

            columns = lax.fori_loop(0, size // 8, finish, jnp.zeros((ROWS, LANES), jnp.float32))
            padded = jnp.concatenate([columns, jnp.zeros((LANES - ROWS, LANES), jnp.float32)], axis=0)
            out[low : low + size, :] = padded.T[:size]

    work(loads[0], coarse_keys, coarse_count, coarse_src, coarse_out)
    work(loads[1], leaf_keys, leaf_count, leaf_src, leaf_out)


def translate(leaf_keys, leaf_count, coarse_keys, coarse_count, leaf_table, coarse_table, ops):
    smem = pl.BlockSpec(memory_space=pltpu.SMEM)
    whole = pl.BlockSpec(memory_space=VMEM)
    return pl.pallas_call(
        translate_kernel,
        out_shape=(
            jax.ShapeDtypeStruct((4 * LEAF_DEV, LANES), jnp.float32),
            jax.ShapeDtypeStruct((LEAF_DEV, LANES), jnp.float32),
        ),
        in_specs=[pl.BlockSpec(memory_space=pl.ANY), smem] * 2 + [whole] * 3,
        out_specs=(whole, whole),
        scratch_shapes=[
            VMEM((4 * LEAF_DEV, ROWS, LANES), jnp.float32),
            pltpu.SMEM((5120,), jnp.int32),
            pltpu.SMEM((3072,), jnp.int32),
            pltpu.SemaphoreType.DMA((2,)),
        ],
        compiler_params=pltpu.CompilerParams(vmem_limit_bytes=16 * MIB),
        name="translate",
    )(leaf_keys.reshape(-1), leaf_count, coarse_keys.reshape(-1), coarse_count, leaf_table, coarse_table, ops)


def near_tiles(atoms, out, low, high):
    def tile(t, carry):
        at = pl.ds(pl.multiple_of(t * 32, 32), 32)
        x, y, z = (atoms[d, at, :] for d in range(3))
        own = iota((32, LANES), 0) + t * 32

        def fours(masked):
            def four(i, sums):
                for u in range(4):
                    j = i * 4 + u
                    xj, yj, zj, qj = (atoms[d, pl.ds(j, 1), :] for d in range(4))
                    dx, dy, dz = x - xj, y - yj, z - zj
                    inverse = lax.rsqrt(dx * dx + dy * dy + dz * dz + SOFTENING)
                    weighted = inverse * qj
                    if masked:
                        weighted = jnp.where(own == j, 0.0, weighted)
                    strength = weighted * (inverse * inverse)
                    terms = (strength * dx, strength * dy, strength * dz, weighted)
                    sums = tuple(a + b for a, b in zip(sums, terms))
                return sums

            return four

        sums = (jnp.zeros((32, LANES), jnp.float32),) * 4
        sums = lax.fori_loop(0, t * 8, fours(False), sums)
        sums = lax.fori_loop(t * 8, t * 8 + 8, fours(True), sums)
        sums = lax.fori_loop(t * 8 + 8, 32, fours(False), sums)
        for d in range(3):
            out[d, at, :] = sums[d] * atoms[3, at, :]
        out[3, at, :] = sums[3]
        return carry

    lax.fori_loop(low, high, tile, 0)


class Place:
    def __init__(self):
        dom = lax.axis_index("dom")
        self.here = (dom // 8, (dom // 2) % 4, lax.axis_index("lvl"))
        self.core = dom % 2
        self.twin = self.device(self.here, 1 - self.core)

    def device(self, place, core):
        return ((place[0] * 4 + place[1]) * 2 + core, place[2])

    def moved(self, axis, by):
        place = tuple((v + by) % 4 if n == axis else v for n, v in enumerate(self.here))
        return self.device(place, self.core)

    def greet(self):
        barrier = pltpu.get_barrier_semaphore()
        for axis in range(3):
            for by in (1, 2, 3):
                pl.semaphore_signal(barrier, inc=1, device_id=self.moved(axis, by), device_id_type=MESH)
        pl.semaphore_signal(barrier, inc=1, device_id=self.twin, device_id_type=MESH)
        return barrier


def sender(send_sem, recv_sem):
    started = []

    def send(source, target, where):
        n = len(started)
        copy = pltpu.make_async_remote_copy(
            src_ref=source,
            dst_ref=target,
            send_sem=send_sem.at[n],
            recv_sem=recv_sem.at[n],
            device_id=where,
            device_id_type=MESH,
        )
        copy.start()
        started.append(copy)
        return copy

    return started, send


def exchange(place, send, source, one, two, target, between):
    (y, x, z), core = place.here, place.core
    copy = send(source.at[:, :, 1 - core], one.at[core], place.twin)
    one[core] = source[:, :, core]
    between(0)
    copy.wait_recv()
    copies = [send(one.at[:, :, (x + by) % 4], two.at[x], place.moved(1, by)) for by in (1, 2, 3)]
    two[x] = one[:, :, x]
    between(1)
    for copy in copies:
        copy.wait_recv()
    copies = [send(two.at[:, :, (y + by) % 4], target.at[y], place.moved(0, by)) for by in (1, 2, 3)]
    target[y] = two[:, :, y]
    between(2)
    for copy in copies:
        copy.wait_recv()


PARTS = ((0, 16, 24, (2, 0, 1)), (24, 32, 48, (0, 1, 2)), (48, 56, 64, (1, 2, 0)))
COPIES = 66
NEAR_FIRST = 2
SLABS = 9


def gather_kernel(
    atoms_ref, whole_ref, m2m_ref, m2l_hbm,
    all_ref, parent_ref, near_ref, lkeys_ref, lcount_ref, ckeys_ref, ccount_ref, m2l_ref, arrived_ref, place_ref, ids_ref,
    packed, one, two, turned, acc, rows, part_ref, got_c, got_x, got_y, sum_c, sum_x, slabs, send_sem, recv_sem, slab_sem
):
    me = Place()
    here, core, twin = me.here, me.core, me.twin
    table_ref = whole_ref.at[0:64]
    leaf_items = [whole_ref.at[64 + 32 * n : 96 + 32 * n] for n in range(3)]
    coarse_items = [whole_ref.at[160 + 16 * n : 176 + 16 * n] for n in range(3)]

    def slab(g, slot):
        return pltpu.make_async_copy(m2l_hbm.at[pl.ds(g * SLABS, SLABS)], slabs.at[slot], slab_sem.at[slot])

    m2l_ref[OFFSETS * ROWS :, :] = jnp.zeros((ROWS, LANES), jnp.float32)
    slab(0, 0).start()
    barrier = me.greet()
    block_moments(atoms_ref, table_ref[...], whole_ref[208:209, :], place_ref, packed, turned, acc, rows)
    pl.semaphore_wait(barrier, 10)

    started, send = sender(send_sem, recv_sem)

    def block(done, axis, by, low, high):
        y, x, z = (
            slice(None) if n in done else ((here[n] + by) % 4 if n == axis else here[n]) for n in range(3)
        )
        return all_ref.at[y, x, core, z, slice(low, high)]

    def put(ref, where):
        return send(ref, ref, where)

    def parents(done):
        y, x, z = (slice(None) if n in done else here[n] for n in range(3))
        return parent_ref.at[z, y, x, core]

    waiting = {}

    def stage(n):
        if n == 0:
            waiting["p"] = [send(part_ref.at[:, :, 1 - core], got_c, twin)]
            return
        for copy in waiting["p"]:
            copy.wait_recv()
        if n == 1:
            sum_c[...] = part_ref[:, :, core] + got_c[...]
            waiting["p"] = [
                send(sum_c.at[:, (here[1] + by) % 4], got_x.at[by - 1], me.moved(1, by)) for by in (1, 2, 3)
            ]
        elif n == 2:
            sum_x[...] = (sum_c[:, here[1]] + got_x[0]) + (got_x[1] + got_x[2])
            waiting["p"] = [
                send(sum_x.at[(here[0] + by) % 4], got_y.at[by - 1], me.moved(0, by)) for by in (1, 2, 3)
            ]
        elif n == 3:
            parent_ref[here[2], here[0], here[1], core] = (sum_x[here[0]] + got_y[0]) + (got_y[1] + got_y[2])
            waiting["p"] = [put(parents(()), me.moved(2, by)) for by in (1, 2, 3)]
        elif n == 4:
            waiting["p"] = [put(parents((2,)), me.moved(0, by)) for by in (1, 2, 3)]
        elif n == 5:
            waiting["p"] = [put(parents((2, 0)), me.moved(1, by)) for by in (1, 2, 3)]
        elif n == 6:
            waiting["p"] = [put(parents((2, 0, 1)), twin)]

    sorts = [
        (keys, stage)
        for pair in itertools.zip_longest(
            *([(keys, stage) for stage in bitonic_stages(keys.shape[0] * LANES)] for keys in (lkeys_ref, ckeys_ref))
        )
        for keys, stage in filter(None, pair)
    ]

    def sort(low, high):
        now = {}
        for keys, stage in sorts[low:high]:
            name = id(keys)
            if name not in now:
                now[name] = (keys, keys[...])
            now[name] = (keys, bitonic_stage(now[name][1], *stage))
        for keys, value in now.values():
            keys[...] = value

    def turn(low, high):
        def group(g, carry):
            slot = g % 2

            @pl.when(g < COEF // SLABS - 1)
            def _():
                slab(g + 1, 1 - slot).start()

            slab(g, slot).wait()
            for u in range(SLABS):
                for p in range(3):
                    wide = min(LANES, OFFSETS - p * LANES)
                    lines = slabs[slot, u, :, p * LANES : p * LANES + wide].T
                    start = p * LANES * ROWS + g * SLABS + u
                    even = wide // 8 * 8
                    m2l_ref[pl.ds(start, even, stride=ROWS), 0:COEF] = lines[:even]
                    if even < wide:
                        m2l_ref[pl.ds(start + even * ROWS, wide - even, stride=ROWS), 0:COEF] = lines[even:]
            return carry

        lax.fori_loop(low, high, group, 0)

    def fill(n):
        if n == 0:
            write_keys(leaf_items, 4 * LEAF_DEV, 8192, lkeys_ref, lcount_ref)
            write_keys(coarse_items, LEAF_DEV, 1024, ckeys_ref, ccount_ref)
        elif n < 5:
            sort(44 * n - 44, 44 * n)
        turn(*((0, 0), (0, 0), (0, 0), (0, 0), (0, 0), (0, 4), (4, 7), (7, 9))[n])
        if n in (3, 4):
            near_tiles(turned, near_ref, n - 3, n - 2)

    exchange(me, send, packed, one, two, arrived_ref, fill)
    first_slot = ((here[0] * 4 + here[1]) * 2 + core) * GROUP * LEAF_DEV + here[2] * LEAF_DEV
    all_ref[here[0], here[1], core, here[2]] = leaf_moments(
        arrived_ref[...].reshape(32 * CAP, LANES), table_ref, m2m_ref, here[2], first_slot, part_ref, ids_ref
    )

    last = []
    for phase in range(2):
        direct = []
        for low, middle, high, order in PARTS:
            axis, done = order[phase], order[:phase]
            direct.append([put(block(done, axis, 0, low, high), me.moved(axis, by)) for by in (1, 3, 2)])
        stage(2 * phase)
        fill(phase + 3)
        stage(2 * phase + 1)
        for (low, middle, high, order), copies in zip(PARTS, direct):
            for copy in copies:
                copy.wait_recv()
    first, second = [], []
    for low, middle, high, order in PARTS:
        axis, done = order[2], order[:2]
        first.append([put(block(done, axis, 0, low, high), me.moved(axis, by)) for by in (1, 3)])
    for low, middle, high, order in PARTS:
        last.append(put(block(order[:2], order[2], 0, low, high), twin))
    stage(4)
    fill(5)
    for (low, middle, high, order), (right, left) in zip(PARTS, first):
        axis, done = order[2], order[:2]
        right.wait_recv()
        a = put(block(done, axis, 3, low, middle), me.moved(axis, 1))
        left.wait_recv()
        b = put(block(done, axis, 1, middle, high), me.moved(axis, 3))
        second.append((a, b))
    for low, middle, high, order in PARTS:
        last.append(put(block(order[:2], order[2], 3, low, high), twin))
        last.append(put(block(order[:2], order[2], 1, low, high), twin))
    stage(5)
    fill(6)
    for (low, middle, high, order), pair in zip(PARTS, second):
        axis, done = order[2], order[:2]
        for copy in pair:
            copy.wait_recv()
        last.append(put(block(done, axis, 2, low, high), twin))
    stage(6)
    fill(7)
    for copy in last:
        copy.wait_recv()
    for copy in waiting["p"]:
        copy.wait_recv()
    for copy in started:
        copy.wait_send()
    assert len(started) == COPIES


def gather(atoms, integers, m2m_ops, m2l_ops):
    whole = pl.BlockSpec(memory_space=VMEM)
    f32, i32 = jnp.float32, jnp.int32
    blocks = atoms.shape[1]
    return pl.pallas_call(
        gather_kernel,
        out_shape=(
            jax.ShapeDtypeStruct((4, 4, 2, 4, LEAF_DEV, LANES), f32),
            jax.ShapeDtypeStruct((4, 4, 4, 2, 8, LANES), f32),
            jax.ShapeDtypeStruct((4, 32 * NEAR_FIRST, blocks), f32),
            jax.ShapeDtypeStruct((64, LANES), i32),
            jax.ShapeDtypeStruct((1, LANES), i32),
            jax.ShapeDtypeStruct((32, LANES), i32),
            jax.ShapeDtypeStruct((1, LANES), i32),
            jax.ShapeDtypeStruct(((OFFSETS + 1) * ROWS, LANES), f32),
            jax.ShapeDtypeStruct((4, 4, 2, CAP, LANES), f32),
            jax.ShapeDtypeStruct((1, blocks), i32),
            jax.ShapeDtypeStruct((LEAF_DEV, LANES), i32),
        ),
        in_specs=[whole] * 3 + [pl.BlockSpec(memory_space=pl.ANY)],
        out_specs=(whole,) * 11,
        scratch_shapes=[
            VMEM((4, 4, 2, CAP, LANES), f32),
            VMEM((2, 4, 4, CAP, LANES), f32),
            VMEM((4, 2, 4, CAP, LANES), f32),
            VMEM((4, LANES, blocks), f32),
            VMEM((COEF, 8, blocks), f32),
            VMEM((LANES, blocks), f32),
            VMEM((4, 4, 2, 8, LANES), f32),
            VMEM((4, 4, 8, LANES), f32),
            VMEM((3, 4, 8, LANES), f32),
            VMEM((3, 8, LANES), f32),
            VMEM((4, 4, 8, LANES), f32),
            VMEM((4, 8, LANES), f32),
            VMEM((2, SLABS, COEF, OFFSETS), f32),
            pltpu.SemaphoreType.DMA((COPIES,)),
            pltpu.SemaphoreType.DMA((COPIES,)),
            pltpu.SemaphoreType.DMA((2,)),
        ],
        compiler_params=pltpu.CompilerParams(collective_id=0, has_side_effects=True, vmem_limit_bytes=24 * MIB),
        name="gather",
    )(atoms, integers, m2m_ops.transpose(1, 0, 2), m2l_ops.transpose(1, 2, 0))


def far_kernel(
    terms_ref, parent_ref, ids_ref, arrived_ref, ops_ref, atoms_ref, place_ref, near_ref, matrix_ref,
    force_ref, phi_ref, basis, near, got, sent, one, two, returned, turned, lines, send_sem, recv_sem
):
    me = Place()
    lvl = me.here[2]
    blocks = atoms_ref.shape[1]
    barrier = me.greet()
    pl.semaphore_wait(barrier, 10)

    started, send = sender(send_sem, recv_sem)
    shared = [send(terms_ref.at[(lvl + by) % 4], got.at[by - 1], me.moved(2, by)) for by in (1, 2, 3)]
    for d in range(4):
        turned[d] = atoms_ref[d].T
    shifted = by_octant(parent_ref[...], ops_ref, ids_ref[...][:, 0:1] & 7)
    total = shifted + terms_ref[lvl]

    def prepare(i, carry):
        at = pl.ds(pl.multiple_of(i * 32, 32), 32)

        def emit(row, degree, value):
            basis[row, at, :] = value

        harmonics(turned[0, at, :], turned[1, at, :], turned[2, at, :], emit)
        return carry

    lax.fori_loop(0, 3, prepare, 0)
    near[:, 0 : 32 * NEAR_FIRST] = near_ref[...]
    near_tiles(turned, near, 2, 3)
    tags = arrived_ref[...].reshape(32 * CAP, LANES)[:, 127:128].astype(jnp.int32)
    member = (iota((32 * CAP, LEAF_DEV), 1) + 1 == tags).astype(jnp.float32)
    for copy in shared:
        copy.wait_recv()
    total = (total + got[0]) + (got[1] + got[2])
    sent[...] = dot(member, total).reshape(sent.shape)

    def between(n):
        if n == 0:
            lax.fori_loop(3, 4, prepare, 0)
        if n == 1:
            near_tiles(turned, near, 3, 4)

    exchange(me, send, sent, one, two, returned, between)
    spread = (iota((32 * CAP, blocks), 0) == place_ref[...]).astype(jnp.float32)

    columns = dot(returned[...].reshape(32 * CAP, LANES), spread, ((0,), (0,)))
    lines[...] = dot(matrix_ref[...], columns)

    def chunk(i, carry):
        at = pl.ds(pl.multiple_of(i * 32, 32), 32)
        sums = [None] * 4
        for row in range(COEF):
            value = basis[row, at, :]
            starts = [(3, 0)] + ([(d, 96 + 64 * d) for d in range(3)] if row < TOP * TOP else [])
            for n, start in starts:
                term = lines[start + row : start + row + 1, :] * value
                sums[n] = term if sums[n] is None else sums[n] + term
        for n in range(3):
            near[n, at, :] = near[n, at, :] - turned[3, at, :] * sums[n]
        near[3, at, :] = near[3, at, :] + sums[3]
        return carry

    lax.fori_loop(0, 4, chunk, 0)
    for d in range(3):
        force_ref[d] = near[d].T
    phi_ref[...] = near[3].T
    for copy in started:
        copy.wait_send()


def far_field(terms, parent_locals, ids, arrived, l2l_ops, atoms, place, near):
    whole = pl.BlockSpec(memory_space=VMEM)
    f32 = jnp.float32
    return pl.pallas_call(
        far_kernel,
        out_shape=(
            jax.ShapeDtypeStruct((3,) + atoms.shape[1:], f32),
            jax.ShapeDtypeStruct(atoms.shape[1:], f32),
        ),
        in_specs=[whole] * 9,
        out_specs=(whole, whole),
        scratch_shapes=[
            VMEM((COEF,) + atoms.shape[1:], f32),
            VMEM(atoms.shape, f32),
            VMEM((3, LEAF_DEV, LANES), f32),
            VMEM((4, 4, 2, CAP, LANES), f32),
            VMEM((2, 4, 4, CAP, LANES), f32),
            VMEM((4, 2, 4, CAP, LANES), f32),
            VMEM((4, 4, 2, CAP, LANES), f32),
            VMEM(atoms.shape, f32),
            VMEM((G_ROWS, LANES), f32),
            pltpu.SemaphoreType.DMA((10,)),
            pltpu.SemaphoreType.DMA((10,)),
        ],
        compiler_params=pltpu.CompilerParams(collective_id=1, has_side_effects=True, vmem_limit_bytes=20 * MIB),
        name="far_field",
    )(
        terms.reshape(GROUP, LEAF_DEV, LANES), parent_locals, ids, arrived, l2l_ops.transpose(1, 0, 2), atoms, place, near,
        jnp.asarray(gradient_matrix()),
    )


def stacked(arrays):
    rows = sum(a.shape[0] for a in arrays)
    total, start = None, 0
    for a in arrays:
        part = jnp.pad(a, ((start, rows - start - a.shape[0]), (0, 0)))
        total = part if total is None else total + part
        start += a.shape[0]
    return total


def shards(
    positions,
    charges,
    block_leaf,
    leaf_slot,
    m2m_ops,
    l2l_ops,
    m2l_ops,
    item_target,
    item_source,
    item_offset,
    coarse_target,
    coarse_source,
    coarse_offset,
):
    blocks = block_leaf.shape[0]
    leaves_all = leaf_slot.shape[0]
    parents_all = leaves_all // 8
    atoms = jnp.concatenate([positions.reshape(3, blocks, LANES), charges.reshape(1, blocks, LANES)])
    integers = [leaf_slot, item_target, item_source, item_offset, coarse_target, coarse_source, coarse_offset, block_leaf]
    integers = stacked([a.reshape(-1, LANES) for a in integers])
    (
        source_table, parent_table, near, leaf_keys, leaf_count, coarse_keys, coarse_count, turned_ops, arrived, place, ids
    ) = gather(atoms, integers, m2m_ops, m2l_ops)
    source_table = source_table.reshape(leaves_all, LANES)
    parent_table = parent_table.reshape(parents_all, LANES)
    terms, parent_locals = translate(
        leaf_keys,
        leaf_count,
        coarse_keys,
        coarse_count,
        source_table,
        parent_table,
        turned_ops.reshape(OFFSETS + 1, ROWS, LANES),
    )
    forces, potential = far_field(terms, parent_locals, ids, arrived, l2l_ops, atoms, place, near)
    return forces.reshape(3, blocks * LANES), potential.reshape(blocks * LANES)


def solution(mesh):
    in_specs = (
        P(None, ("dom", "lvl")),
        P(("dom", "lvl")),
        P(("dom", "lvl")),
        P(),
        P(),
        P(),
        P(),
        P("dom", "lvl", None),
        P("dom", "lvl", None),
        P("dom", "lvl", None),
        P("dom", "lvl", None),
        P("dom", "lvl", None),
        P("dom", "lvl", None),
    )
    out_specs = (P(None, ("dom", "lvl")), P(("dom", "lvl")))
    return jax.shard_map(shards, mesh=mesh, in_specs=in_specs, out_specs=out_specs, check_vma=False)
```
